32 devices in a mesh: seq: 8 (over z, y), rep: 4 (over x, core).
Axes of the slice: x: 2, y: 2, z: 4, core: 2. Of those that a mesh axis runs over, the one named last changes fastest.
Arguments:
- inputs: bfloat16 [64, 512, 512], P('rep', 'seq'), may hold values from -6 to 6
- cotangent: bfloat16 [64, 512, 512], P('rep', 'seq'), may hold values from -6 to 6
- segments: int32 [64, 512], P('rep', 'seq'), may hold values from 0 to 511, as said below
- owners: int32 [24], replicated, may hold values from 0 to 23, each once
- weights: float32 [512, 24, 256], P('seq', 'rep'), may hold values from -0.25 to 0.25
- left_bases: float32 [24, 512, 512], P('rep'), as said below
- right_bases: float32 [24, 256, 256], P('rep'), as said below
- moment_one: float32 [512, 24, 256], P('seq', 'rep')
- moment_two: float32 [512, 24, 256], P('seq', 'rep'), as said below
- norm_params: float32 [4, 512], replicated
- norm_one: float32 [4, 512], replicated
- norm_two: float32 [4, 512], replicated, as said below
- positions: float32 [512, 512], replicated, may hold values from -3 to 3
- pos_one: float32 [512, 512], replicated
- pos_two: float32 [512, 512], replicated, as said below
Outputs:
- result: bfloat16 [64, 512, 512], P('rep', 'seq')
- input_grad: float32 [64, 512, 512], P('rep', 'seq')
- new_moment_one: float32 [512, 24, 256], P('seq', 'rep')
- new_moment_two: float32 [512, 24, 256], P('seq', 'rep')
- new_weights: float32 [512, 24, 256], P('seq', 'rep')
- new_norm_one: float32 [4, 512], replicated
- new_norm_two: float32 [4, 512], replicated
- new_norms: float32 [4, 512], replicated
- new_pos_one: float32 [512, 512], replicated
- new_pos_two: float32 [512, 512], replicated
- new_positions: float32 [512, 512], replicated
The draws below stay inside these ranges and needn't reach their ends.
Inputs may be any that keep to these rules, and one draw needn't show every extreme that they name: `segments`: each row starts at document 0 and its numbers never fall, by at most one from a character to the next; in each aligned block of 16 rows one row is a single document and another has a new document at every character. `owners`: each slot holds exactly one tile. `left_bases`: each slot's basis is orthogonal. `right_bases`: each slot's basis is orthogonal. `moment_two`: all entries are positive. `norm_two`: all entries are positive. `pos_two`: all entries are positive.
All inputs are finite; a program needn't handle non-finite values.
Results may differ from the reference program's by a relative error of at most 0.015.
Values may be sent and summed in bfloat16 or wider, within the bound.
No kernel may reach another device: no remote copies, remote signals or barrier semaphores. Data moves between devices by JAX's collectives and lax.ppermute only.
A program may use at most 192 MiB of HBM per device.

```python
import math
import jax
import jax.numpy as jnp
from jax import lax

D = 512
H = 8
WIN = 512
NSEQ = 16
STEP = 10
L = 512
NSEQS = 64
TC = 256
TILES = 24


def orthogonal_stack(subkey, stacked, matrix_order):
    frequency = jnp.arange(matrix_order)[:, None]
    sample = jnp.arange(matrix_order)[None, :]
    phases = (2 * sample + 1) * frequency % (4 * matrix_order)
    cosine = jnp.cos(jnp.pi * phases.astype(jnp.float32) / (2.0 * matrix_order)) * math.sqrt(2.0 / matrix_order)
    cosine = cosine * jnp.where(frequency == 0, math.sqrt(0.5), 1.0)
    sign_key, order_key = jax.random.split(subkey)
    sign_flip = (2 * jax.random.randint(sign_key, (stacked, matrix_order, 1), 0, 2) - 1).astype(jnp.float32)
    orders = jax.vmap(lambda single: jax.random.permutation(single, matrix_order))(jax.random.split(order_key, stacked))
    return jnp.take_along_axis(sign_flip * cosine[None], orders[:, None, :], axis=2)


def draw_left_bases(key, part):
    key = jax.random.fold_in(key, 21)
    return orthogonal_stack(key, TILES, D)


def draw_right_bases(key, part):
    key = jax.random.fold_in(key, 22)
    return orthogonal_stack(key, TILES, TC)


def draw_segments(key, part):
    key = jax.random.fold_in(key, 5)
    rate_key, bit_key, pick_key = jax.random.split(key, 3)
    rates = jax.random.randint(rate_key, (NSEQS,), 0, 4)
    limits = (1 << 20) // (8 * jnp.left_shift(1, 2 * rates))
    values = jax.random.randint(bit_key, (NSEQS, L), 0, 1 << 20)
    starts = (values < limits[:, None]) & (jnp.arange(L)[None, :] > 0)
    chosen = jax.random.randint(pick_key, (NSEQS // NSEQ,), 0, NSEQ)
    place = jnp.arange(NSEQS) % NSEQ
    whole = place == jnp.repeat(chosen, NSEQ)
    every = place == jnp.repeat((chosen + 1) % NSEQ, NSEQ)
    starts = starts | every[:, None] & (jnp.arange(L)[None, :] > 0)
    starts = starts & jnp.logical_not(whole)[:, None]
    return jnp.cumsum(starts.astype(jnp.int32), axis=1).astype(jnp.int32)


def draw_moment_one(key, part):
    key = jax.random.fold_in(key, 31)
    spread = 0.25 * math.sqrt(NSEQS * L)
    return spread * jax.random.normal(key, (D, TILES, TC), jnp.float32)


def draw_moment_two(key, part):
    key = jax.random.fold_in(key, 32)
    spread = 0.25 * math.sqrt(NSEQS * L)
    return spread * spread * jnp.exp(jax.random.uniform(key, (D, TILES, TC), jnp.float32, math.log(0.5), math.log(8.0)))


def draw_norm_params(key, part):
    key = jax.random.fold_in(key, 41)
    source = jax.random.normal(key, (4, D), jnp.float32)
    return jnp.where(jnp.arange(4)[:, None] % 2 == 0, 1.0 + 0.25 * source, 0.3 * source)


def draw_norm_one(key, part):
    key = jax.random.fold_in(key, 42)
    spread = 0.5 * math.sqrt(NSEQS * L)
    return spread * jax.random.normal(key, (4, D), jnp.float32)


def draw_norm_two(key, part):
    key = jax.random.fold_in(key, 43)
    spread = 0.5 * math.sqrt(NSEQS * L)
    return spread * spread * jnp.exp(jax.random.uniform(key, (4, D), jnp.float32, math.log(0.5), math.log(8.0)))


def draw_pos_one(key, part):
    key = jax.random.fold_in(key, 44)
    spread = 0.5 * math.sqrt(NSEQS * L / WIN)
    return spread * jax.random.normal(key, (WIN, D), jnp.float32)


def draw_pos_two(key, part):
    key = jax.random.fold_in(key, 45)
    spread = 0.5 * math.sqrt(NSEQS * L / WIN)
    return spread * spread * jnp.exp(jax.random.uniform(key, (WIN, D), jnp.float32, math.log(0.5), math.log(8.0)))


def block_levels(stream_key, shape, pieces, smallest, top_value):
    def one(position, blocks):
        draws = jax.random.uniform(jax.random.fold_in(jax.random.fold_in(stream_key, 6), position), (blocks,), jnp.float32, smallest / len(pieces), top_value / len(pieces))
        return jnp.repeat(jnp.exp(draws), shape[position] // blocks).reshape((-1,) + (1,) * (len(shape) - position - 1))

    level = one(*pieces[0])
    for cut in pieces[1:]:
        level = level * one(*cut)
    return level


def centred(key, shape, scale, limit, cuts=(), held_as=jnp.bfloat16):
    factor_of = block_levels(key, shape, cuts, -0.22, 0.18) if cuts else 1.0
    drawn = jax.random.normal(key, shape, jnp.float32) * scale * factor_of
    return jnp.minimum(jnp.maximum(drawn, -limit), limit).astype(held_as)


def setup_inputs(seed: int = 0) -> dict:
    streams_of = jax.random.split(jax.random.key(seed), 16)
    return {
        "inputs": centred(streams_of[0], (NSEQS, L, D), 1.0, 6.0, ((0, 4), (1, 8))),
        "cotangent": centred(streams_of[1], (NSEQS, L, D), 1.0, 6.0, ((0, 4), (1, 8))),
        "segments": draw_segments(jax.random.fold_in(streams_of[15], 71), 0),
        "owners": jax.random.permutation(streams_of[3], TILES).astype(jnp.int32),
        "weights": centred(streams_of[4], (D, TILES, TC), D ** -0.5, 0.25, ((0, 8), (1, 4)), jnp.float32),
        "left_bases": draw_left_bases(jax.random.fold_in(streams_of[15], 71), 0),
        "right_bases": draw_right_bases(jax.random.fold_in(streams_of[15], 71), 0),
        "moment_one": draw_moment_one(jax.random.fold_in(streams_of[15], 71), 0),
        "moment_two": draw_moment_two(jax.random.fold_in(streams_of[15], 71), 0),
        "norm_params": draw_norm_params(jax.random.fold_in(streams_of[15], 71), 0),
        "norm_one": draw_norm_one(jax.random.fold_in(streams_of[15], 71), 0),
        "norm_two": draw_norm_two(jax.random.fold_in(streams_of[15], 71), 0),
        "positions": centred(streams_of[12], (WIN, D), 0.5, 3.0, (), jnp.float32),
        "pos_one": draw_pos_one(jax.random.fold_in(streams_of[15], 71), 0),
        "pos_two": draw_pos_two(jax.random.fold_in(streams_of[15], 71), 0),
    }


EPS_NORM = 1e-05
EPS_ADAM = 1e-08
BETA = 0.5
LEARN = 0.02
LEARN_SMALL = 0.2
DECAY = 0.01
MASKED = -1e+30
HIGH_PRECISION = lax.Precision.HIGHEST

@jax.custom_vjp
def low_precision_cast(v):
    return lax.optimization_barrier(v.astype(jnp.bfloat16)).astype(jnp.float32)

@jax.custom_vjp
def low_precision_backward(v):
    return v

def low_keep(v):
    return (low_precision_cast(v), None)

def low_pass(kept, grad):
    return (grad,)

def back_keep(v):
    return (v, None)

def back_low(kept, grad):
    return (low_precision_cast(grad),)
low_precision_cast.defvjp(low_keep, low_pass)
low_precision_backward.defvjp(back_keep, back_low)

def split_tiles(query_key_value_weight, output_weight, up_weight, down_weight):
    model_width = query_key_value_weight.shape[0]
    half_width = model_width // 2
    blocks = down_weight.shape[0] // model_width
    down_tiles = down_weight.reshape(blocks, model_width, 2, half_width).transpose(1, 0, 2, 3).reshape(model_width, 2 * blocks, half_width)
    return jnp.concatenate([query_key_value_weight.reshape(model_width, -1, half_width), output_weight.reshape(model_width, -1, half_width), up_weight.reshape(model_width, -1, half_width), down_tiles], axis=1)

def join_tiles(tile_stack):
    model_width, count_all, half_width = tile_stack.shape
    hidden = (count_all - 8) * model_width // 4
    up_count = 2 * hidden // model_width
    blocks = hidden // model_width
    query_key_value_weight = tile_stack[:, 0:6].reshape(model_width, 3 * model_width)
    output_weight = tile_stack[:, 6:8].reshape(model_width, model_width)
    up_weight = tile_stack[:, 8:8 + up_count].reshape(model_width, hidden)
    down_weight = tile_stack[:, 8 + up_count:].reshape(model_width, blocks, 2, half_width).transpose(1, 0, 2, 3).reshape(hidden, model_width)
    return (query_key_value_weight, output_weight, up_weight, down_weight)

def layer_norm(values, gain, shift):
    center = values - lax.optimization_barrier(jnp.mean(values, axis=-1, keepdims=True))
    scaled = center * lax.rsqrt(lax.optimization_barrier(jnp.mean(center * center, axis=-1, keepdims=True)) + EPS_NORM)
    return scaled * gain + shift

def adam_step(gradient, first, second):
    first_new = BETA * first + (1.0 - BETA) * gradient
    second_new = BETA * second + (1.0 - BETA) * gradient * gradient
    fix = 1.0 - BETA ** STEP
    direction = first_new / fix / (jnp.sqrt(second_new / fix) + EPS_ADAM)
    return (first_new, second_new, direction)

def forward(inputs_f, pos_f, norm_f, query_key_value_weight, output_weight, up_weight, down_weight, segments):
    seq_total, length, model_width = inputs_f.shape
    head_dim = model_width // H
    hidden_residual_sum = inputs_f + jnp.tile(pos_f, (length // WIN, 1))[None]
    projected_output = low_precision_cast(low_precision_backward(jnp.einsum('ynp,pz->ynz', low_precision_cast(hidden_residual_sum), low_precision_cast(query_key_value_weight), precision=HIGH_PRECISION)))

    def attend(paired):
        rows_all, doc_ids = paired
        parts = rows_all.reshape(length // WIN, WIN, H, 3, head_dim)
        query = parts[:, :, :, 0]
        keys_all = parts[:, :, :, 1]
        values = parts[:, :, :, 2]
        scores = low_precision_backward(jnp.einsum('wqhe,wkhe->whqk', query, keys_all, precision=HIGH_PRECISION) * head_dim ** (-0.5))
        window_ids = doc_ids.reshape(length // WIN, WIN)
        causal = jnp.arange(WIN)[:, None] >= jnp.arange(WIN)[None, :]
        allowed = (window_ids[:, :, None] == window_ids[:, None, :]) & causal[None]
        masked = jnp.where(allowed[:, None], scores, MASKED)
        probs = low_precision_cast(jax.nn.softmax(masked, axis=-1))
        mixed_heads = jnp.einsum('whqk,wkhe->wqhe', probs, values, precision=HIGH_PRECISION)
        return mixed_heads.reshape(length, model_width)
    mixed_heads = lax.map(jax.checkpoint(attend), (projected_output, segments))
    mixed_heads = low_precision_cast(low_precision_backward(mixed_heads))
    attention_output = low_precision_backward(jnp.einsum('cgw,wu->cgu', mixed_heads, low_precision_cast(output_weight), precision=HIGH_PRECISION))
    first_normed_input = layer_norm(hidden_residual_sum + attention_output, norm_f[0], norm_f[1])
    preactivation_hidden = low_precision_backward(jnp.einsum('vzx,xm->vzm', low_precision_cast(first_normed_input), low_precision_cast(up_weight), precision=HIGH_PRECISION))
    activated_hidden = low_precision_cast(jax.nn.gelu(preactivation_hidden))
    branch_output = low_precision_backward(jnp.einsum('ebm,mo->ebo', activated_hidden, low_precision_cast(down_weight), precision=HIGH_PRECISION))
    return layer_norm(first_normed_input + branch_output, norm_f[2], norm_f[3])

def reference(inputs, cotangent, segments, owners, weights, left_bases, right_bases, moment_one, moment_two, norm_params, norm_one, norm_two, positions, pos_one, pos_two):
    query_key_value_weight, output_weight, up_weight, down_weight = join_tiles(weights[:, owners, :])

    def wrapped(inputs_f, pos_f, norm_f, qkv_f, out_f, up_f, down_f):
        return forward(inputs_f, pos_f, norm_f, qkv_f, out_f, up_f, down_f, segments)
    result, pullback = jax.vjp(wrapped, inputs.astype(jnp.float32), positions, norm_params, query_key_value_weight, output_weight, up_weight, down_weight)
    grad_in, grad_pos, grad_norm, grad_qkv, grad_out, grad_up, grad_down = pullback(cotangent.astype(jnp.float32))
    grad_tiles = split_tiles(grad_qkv, grad_out, grad_up, grad_down)
    grad_slots = jnp.zeros_like(grad_tiles).at[:, owners, :].set(grad_tiles)
    turned = jnp.einsum('sir,isc->rsc', left_bases, grad_slots, precision=HIGH_PRECISION)
    turned = jnp.einsum('rsc,scd->rsd', turned, right_bases, precision=HIGH_PRECISION)
    first_new, second_new, direction = adam_step(turned, moment_one, moment_two)
    change = jnp.einsum('rsc,sdc->rsd', direction, right_bases, precision=HIGH_PRECISION)
    change = jnp.einsum('sir,rsd->isd', left_bases, change, precision=HIGH_PRECISION)
    new_weights = weights - LEARN * (change + DECAY * weights)
    norm_first, norm_second, norm_dir = adam_step(grad_norm, norm_one, norm_two)
    pos_first, pos_second, pos_dir = adam_step(grad_pos, pos_one, pos_two)
    return (result.astype(jnp.bfloat16), grad_in, first_new, second_new, new_weights, norm_first, norm_second, norm_params - LEARN_SMALL * norm_dir, pos_first, pos_second, positions - LEARN_SMALL * pos_dir)
```

```python
import functools

import jax
import jax.numpy as jnp
from jax import lax
from jax.experimental import pallas as pl
from jax.experimental.pallas import tpu as pltpu
from jax.sharding import PartitionSpec as P

H = 8
WIN = 512
STEP = 10

EPS_NORM = 1e-05
EPS_ADAM = 1e-08
BETA = 0.5
LEARN = 0.02
LEARN_SMALL = 0.2
DECAY = 0.01
MASKED = -1e30

BF = jnp.bfloat16
F32 = jnp.float32
VMEM_LIMIT = 58 * 1024 * 1024
GELU_A = 0.7978845608028654
GELU_B = 0.044715


def nn(a, b):
    return lax.dot_general(a, b, (((1,), (0,)), ((), ())), preferred_element_type=F32)


def nt(a, b):
    return lax.dot_general(a, b, (((1,), (1,)), ((), ())), preferred_element_type=F32)


def tn(a, b):
    return lax.dot_general(a, b, (((0,), (0,)), ((), ())), preferred_element_type=F32)


def adam_step(gradient, first, second):
    first_new = BETA * first + (1.0 - BETA) * gradient
    second_new = BETA * second + (1.0 - BETA) * gradient * gradient
    fix = 1.0 - BETA**STEP
    direction = first_new / fix / (jnp.sqrt(second_new / fix) + EPS_ADAM)
    return (first_new, second_new, direction)


def row_norm(values):
    center = values - jnp.mean(values, axis=-1, keepdims=True)
    inverse = lax.rsqrt(jnp.mean(center * center, axis=-1, keepdims=True) + EPS_NORM)
    return center * inverse, inverse


def norm_pull(grad_rows, scaled, inverse, gain):
    scaled_grad = grad_rows * gain
    grad_input = inverse * (
        scaled_grad
        - jnp.mean(scaled_grad, axis=-1, keepdims=True)
        - scaled * jnp.mean(scaled_grad * scaled, axis=-1, keepdims=True)
    )
    grad_gain = jnp.sum(grad_rows * scaled, axis=0, keepdims=True)
    grad_shift = jnp.sum(grad_rows, axis=0, keepdims=True)
    return grad_input, grad_gain, grad_shift


def attend_kernel(x_ref, pos_ref, w_ref, ids_row, ids_col, qkv_ref, mixed_ref, lse_ref, bias):
    win, width = pos_ref.shape
    dim = width // H
    tile = w_ref.shape[2]
    hidden = x_ref[...].reshape(win, width).astype(F32) + pos_ref[...]
    low = hidden.astype(BF)
    for t in range(w_ref.shape[0]):
        qkv_ref[0, :, t * tile : (t + 1) * tile] = nn(low, w_ref[t]).astype(BF)
    row = lax.broadcasted_iota(jnp.int32, (win, win), 0)
    col = lax.broadcasted_iota(jnp.int32, (win, win), 1)
    allowed = (ids_col[0] == ids_row[0]) & (row >= col)
    bias[...] = jnp.where(allowed, 0.0, MASKED)
    half = win // 2
    sums = []
    for pair in range(H // 2):
        outs = []
        for h in (2 * pair, 2 * pair + 1):
            base = 3 * dim * h
            query = qkv_ref[0, :, base : base + dim] * (dim**-0.5)
            keys = qkv_ref[0, :, base + dim : base + 2 * dim]
            values = qkv_ref[0, :, base + 2 * dim : base + 3 * dim]
            parts, logs = [], []
            for lo, count in ((0, half), (half, win)):
                scores = nt(query[lo : lo + half], keys[:count]) + bias[lo : lo + half, :count]
                highest = jnp.max(scores, axis=-1, keepdims=True)
                powers = jnp.exp(scores - highest)
                total = jnp.sum(powers, axis=-1, keepdims=True)
                parts.append(nn(powers.astype(BF), values[:count]) / total)
                logs.append(highest + jnp.log(total))
            outs.append(jnp.concatenate(parts, axis=0))
            sums.append(jnp.concatenate(logs, axis=0))
        mixed_ref[0, :, pair * 2 * dim : (pair + 1) * 2 * dim] = jnp.concatenate(outs, axis=1).astype(BF)
    lanes = jnp.concatenate(sums + [jnp.zeros((win, 128 - H), F32)], axis=1)
    lse_ref[0] = lanes.T[:H]


def attend_forward(x, positions, w_qkv, ids):
    group, wins, span, width = x.shape
    win = group * span
    return pl.pallas_call(
        attend_kernel,
        grid=(wins,),
        in_specs=[
            pl.BlockSpec((group, 1, span, width), lambda i: (0, i, 0, 0)),
            pl.BlockSpec((win, width), lambda i: (0, 0)),
            pl.BlockSpec(w_qkv.shape, lambda i: (0, 0, 0)),
            pl.BlockSpec((1, 1, win), lambda i: (i, 0, 0)),
            pl.BlockSpec((1, win, 1), lambda i: (i, 0, 0)),
        ],
        out_specs=[
            pl.BlockSpec((1, win, 3 * width), lambda i: (i, 0, 0)),
            pl.BlockSpec((1, win, width), lambda i: (i, 0, 0)),
            pl.BlockSpec((1, H, win), lambda i: (i, 0, 0)),
        ],
        out_shape=[
            jax.ShapeDtypeStruct((wins, win, 3 * width), BF),
            jax.ShapeDtypeStruct((wins, win, width), BF),
            jax.ShapeDtypeStruct((wins, H, win), F32),
        ],
        scratch_shapes=[pltpu.VMEM((win, win), F32)],
        compiler_params=pltpu.CompilerParams(vmem_limit_bytes=VMEM_LIMIT),
        name="attend_forward",
    )(x, positions, w_qkv, ids[:, None, :], ids[:, :, None])


def middle_kernel(
    x_ref,
    pos_ref,
    mixed_ref,
    cot_ref,
    w_out,
    w_up,
    w_down,
    norm_ref,
    result_ref,
    mid_ref,
    gmixed_ref,
    dout_ref,
    dup_ref,
    ddown_ref,
    dnorm_ref,
    act,
    slope,
    gpre,
    acc_out,
    acc_up,
    acc_down,
):
    step = pl.program_id(0)
    last = pl.num_programs(0) - 1
    win, width = pos_ref.shape
    tile = w_up.shape[2]
    ups = w_up.shape[0]
    blocks = w_down.shape[0] // 2

    @pl.when(step == 0)
    def _():
        acc_out[...] = jnp.zeros_like(acc_out)
        acc_up[...] = jnp.zeros_like(acc_up)
        acc_down[...] = jnp.zeros_like(acc_down)
        dnorm_ref[...] = jnp.zeros_like(dnorm_ref)

    mixed = mixed_ref[0]
    hidden = x_ref[...].reshape(win, width).astype(F32) + pos_ref[...]
    attn = jnp.concatenate([nn(mixed, w_out[t]) for t in range(w_out.shape[0])], axis=1)
    scaled_one, inverse_one = row_norm(hidden + attn)
    normed = scaled_one * norm_ref[0:1] + norm_ref[1:2]
    low = normed.astype(BF)
    for t in range(ups):
        pre = nn(low, w_up[t])
        square = pre * pre
        bent = jnp.tanh(GELU_A * pre * (1.0 + GELU_B * square))
        act[:, t * tile : (t + 1) * tile] = (0.5 * pre * (1.0 + bent)).astype(BF)
        slope[:, t * tile : (t + 1) * tile] = (
            0.5 * (1.0 + bent)
            + 0.5 * pre * (1.0 - bent * bent) * (GELU_A + 3.0 * GELU_A * GELU_B * square)
        ).astype(BF)
    branch = jnp.concatenate(
        [
            sum(nn(act[:, b * width : (b + 1) * width], w_down[2 * b + j]) for b in range(blocks))
            for j in range(2)
        ],
        axis=1,
    )
    scaled_two, inverse_two = row_norm(normed + branch)
    result = scaled_two * norm_ref[2:3] + norm_ref[3:4]
    result_ref[...] = result.astype(BF).reshape(result_ref.shape)
    grad_resid, gain_two, shift_two = norm_pull(
        cot_ref[...].reshape(win, width).astype(F32), scaled_two, inverse_two, norm_ref[2:3]
    )
    gb = grad_resid.astype(BF)
    for b in range(blocks):
        cols = slice(b * width, (b + 1) * width)
        gact = nt(gb[:, :tile], w_down[2 * b]) + nt(gb[:, tile:], w_down[2 * b + 1])
        gpre[:, cols] = (gact * slope[:, cols].astype(F32)).astype(BF)
    grad_normed = grad_resid + sum(
        nt(gpre[:, t * tile : (t + 1) * tile], w_up[t]) for t in range(ups)
    )
    grad_mid, gain_one, shift_one = norm_pull(grad_normed, scaled_one, inverse_one, norm_ref[0:1])
    mid_ref[0] = grad_mid
    ga = grad_mid.astype(BF)
    gmixed_ref[0] = sum(
        nt(ga[:, t * tile : (t + 1) * tile], w_out[t]) for t in range(w_out.shape[0])
    ).astype(BF)
    dnorm_ref[...] += jnp.concatenate([gain_one, shift_one, gain_two, shift_two], axis=0)
    for b in range(blocks):
        act_t = act[:, b * width : (b + 1) * width].T
        for j in range(2):
            acc_down[2 * b + j] += nn(act_t, gb[:, j * tile : (j + 1) * tile])
    low_t = low.T
    for t in range(ups):
        acc_up[t] += nn(low_t, gpre[:, t * tile : (t + 1) * tile])
    mixed_t = mixed.T
    for t in range(w_out.shape[0]):
        acc_out[t] += nn(mixed_t, ga[:, t * tile : (t + 1) * tile])

    @pl.when(step == last)
    def _():
        dout_ref[...] = acc_out[...].astype(BF)
        dup_ref[...] = acc_up[...].astype(BF)
        ddown_ref[...] = acc_down[...].astype(BF)


def middle(x, positions, mixed, cot, w_out, w_up, w_down, norms):
    group, wins, span, width = x.shape
    win = group * span
    hidden = w_up.shape[0] * w_up.shape[2]

    def whole(shape):
        return pl.BlockSpec(shape, lambda i: (0,) * len(shape))

    seq_spec = pl.BlockSpec((group, 1, span, width), lambda i: (0, i, 0, 0))
    row_spec = pl.BlockSpec((1, win, width), lambda i: (i, 0, 0))
    return pl.pallas_call(
        middle_kernel,
        grid=(wins,),
        in_specs=[
            seq_spec,
            whole((win, width)),
            row_spec,
            seq_spec,
            whole(w_out.shape),
            whole(w_up.shape),
            whole(w_down.shape),
            whole(norms.shape),
        ],
        out_specs=[
            seq_spec,
            row_spec,
            row_spec,
            whole(w_out.shape),
            whole(w_up.shape),
            whole(w_down.shape),
            whole(norms.shape),
        ],
        out_shape=[
            jax.ShapeDtypeStruct(x.shape, BF),
            jax.ShapeDtypeStruct((wins, win, width), F32),
            jax.ShapeDtypeStruct((wins, win, width), BF),
            jax.ShapeDtypeStruct(w_out.shape, BF),
            jax.ShapeDtypeStruct(w_up.shape, BF),
            jax.ShapeDtypeStruct(w_down.shape, BF),
            jax.ShapeDtypeStruct(norms.shape, F32),
        ],
        scratch_shapes=[
            pltpu.VMEM((win, hidden), BF),
            pltpu.VMEM((win, hidden), BF),
            pltpu.VMEM((win, hidden), BF),
            pltpu.VMEM(w_out.shape, F32),
            pltpu.VMEM(w_up.shape, F32),
            pltpu.VMEM(w_down.shape, F32),
        ],
        compiler_params=pltpu.CompilerParams(vmem_limit_bytes=VMEM_LIMIT),
        name="middle",
    )(x, positions, mixed, cot, w_out, w_up, w_down, norms)


def attend_back_kernel(
    x_ref,
    pos_ref,
    qkv_ref,
    lse_ref,
    gmixed_ref,
    mid_ref,
    w_ref,
    ids_row,
    ids_col,
    dqkv_ref,
    ginput_ref,
    bias,
    gproj,
    acc,
):
    step = pl.program_id(0)
    last = pl.num_programs(0) - 1
    win, width = pos_ref.shape
    dim = width // H
    tile = w_ref.shape[2]
    factor = dim**-0.5
    half = win // 2

    @pl.when(step == 0)
    def _():
        acc[...] = jnp.zeros_like(acc)

    key = lax.broadcasted_iota(jnp.int32, (win, win), 0)
    query_at = lax.broadcasted_iota(jnp.int32, (win, win), 1)
    allowed = (ids_col[0] == ids_row[0]) & (query_at >= key)
    bias[...] = jnp.where(allowed, 0.0, MASKED)
    for pair in range(H // 2):
        packed = []
        for h in (2 * pair, 2 * pair + 1):
            base = 3 * dim * h
            query = qkv_ref[0, :, base : base + dim] * factor
            keys = qkv_ref[0, :, base + dim : base + 2 * dim]
            values = qkv_ref[0, :, base + 2 * dim : base + 3 * dim]
            gout = gmixed_ref[0, :, h * dim : (h + 1) * dim]
            lse = lse_ref[0, h : h + 1, :]
            blocks = []
            inner_late = None
            for lo, first in ((half, half), (0, 0)):
                scores = nt(keys[lo : lo + half], query[first:]) + bias[lo : lo + half, first:]
                probs = jnp.exp(scores - lse[:, first:])
                gprobs = nt(values[lo : lo + half], gout[first:])
                inner = jnp.sum(probs * gprobs, axis=0, keepdims=True)
                blocks.append((probs, gprobs, inner))
            (probs_b, gprobs_b, inner_b), (probs_a, gprobs_a, inner_a) = blocks
            inner_late = inner_a[:, half:] + inner_b
            inner_full = jnp.concatenate([inner_a[:, :half], inner_late], axis=1)
            gs_a = (probs_a * (gprobs_a - inner_full)).astype(BF)
            gs_b = (probs_b * (gprobs_b - inner_late)).astype(BF)
            gvalues = jnp.concatenate(
                [nn(probs_a.astype(BF), gout), nn(probs_b.astype(BF), gout[half:])], axis=0
            )
            gkeys = jnp.concatenate([nn(gs_a, query), nn(gs_b, query[half:])], axis=0)
            gq_a = tn(gs_a, keys[:half])
            gq_b = tn(gs_b, keys[half:])
            gquery = jnp.concatenate([gq_a[:half], gq_a[half:] + gq_b], axis=0) * factor
            packed += [gquery.astype(BF), gkeys.astype(BF), gvalues.astype(BF)]
        gproj[:, pair * 6 * dim : (pair + 1) * 6 * dim] = jnp.concatenate(packed, axis=1)
    hidden = x_ref[...].reshape(win, width).astype(F32) + pos_ref[...]
    low_t = hidden.astype(BF).T
    total = mid_ref[0]
    for t in range(w_ref.shape[0]):
        part = gproj[:, t * tile : (t + 1) * tile]
        acc[t] += nn(low_t, part)
        total += nt(part, w_ref[t])
    ginput_ref[...] = total.astype(BF).reshape(ginput_ref.shape)

    @pl.when(step == last)
    def _():
        dqkv_ref[...] = acc[...].astype(BF)


def attend_backward(x, positions, qkv, lse, gmixed, mid, w_qkv, ids):
    group, wins, span, width = x.shape
    win = group * span
    seq_spec = pl.BlockSpec((group, 1, span, width), lambda i: (0, i, 0, 0))
    return pl.pallas_call(
        attend_back_kernel,
        grid=(wins,),
        in_specs=[
            seq_spec,
            pl.BlockSpec((win, width), lambda i: (0, 0)),
            pl.BlockSpec((1, win, 3 * width), lambda i: (i, 0, 0)),
            pl.BlockSpec((1, H, win), lambda i: (i, 0, 0)),
            pl.BlockSpec((1, win, width), lambda i: (i, 0, 0)),
            pl.BlockSpec((1, win, width), lambda i: (i, 0, 0)),
            pl.BlockSpec(w_qkv.shape, lambda i: (0, 0, 0)),
            pl.BlockSpec((1, 1, win), lambda i: (i, 0, 0)),
            pl.BlockSpec((1, win, 1), lambda i: (i, 0, 0)),
        ],
        out_specs=[pl.BlockSpec(w_qkv.shape, lambda i: (0, 0, 0)), seq_spec],
        out_shape=[
            jax.ShapeDtypeStruct(w_qkv.shape, BF),
            jax.ShapeDtypeStruct(x.shape, BF),
        ],
        scratch_shapes=[
            pltpu.VMEM((win, win), F32),
            pltpu.VMEM((win, 3 * width), BF),
            pltpu.VMEM(w_qkv.shape, F32),
        ],
        compiler_params=pltpu.CompilerParams(vmem_limit_bytes=VMEM_LIMIT),
        name="attend_backward",
    )(x, positions, qkv, lse, gmixed, mid, w_qkv, ids[:, None, :], ids[:, :, None])


def swap(x, axis, bit):
    size = lax.axis_size(axis)
    return lax.ppermute(x, axis, [(i, i ^ bit) for i in range(size)])


def groups_of(axis, group):
    size = lax.axis_size(axis)
    if group == size:
        return None
    return [[base + i for i in range(group)] for base in range(0, size, group)]


def exchange(x, axis, group):
    return lax.all_to_all(
        x, axis, 0, 0, axis_index_groups=groups_of(axis, group), tiled=True
    )


def spread(x, axis):
    size = lax.axis_size(axis)
    return lax.all_to_all(jnp.broadcast_to(x[None], (size,) + x.shape), axis, 0, 0, tiled=True)


def pick(x, index, axis):
    return lax.dynamic_index_in_dim(x, index, axis, keepdims=False)


def in_order(second, own, other, axis):
    low = jnp.where(second == 0, own, other)
    high = jnp.where(second == 0, other, own)
    return jnp.stack([low, high], axis=axis)


def body(
    inputs,
    cotangent,
    segments,
    owners,
    weights,
    left_bases,
    right_bases,
    moment_one,
    moment_two,
    norm_params,
    norm_one,
    norm_two,
    positions,
    pos_one,
    pos_two,
):
    seqs = lax.axis_size("seq")
    reps = lax.axis_size("rep")
    me_s = lax.axis_index("seq")
    me_r = lax.axis_index("rep")
    core = me_r & 1
    seq_local, span, width = inputs.shape
    rows_dev, slots, tile = weights.shape
    tiles = owners.shape[0]
    half = rows_dev // 2
    group = WIN // span
    place = me_s % group
    wins = seq_local // group

    x = exchange(inputs, "seq", group).reshape(group, wins, span, width)
    cot = exchange(cotangent, "seq", group).reshape(group, wins, span, width)
    ids = segments[None]
    bit = 1
    while bit < group:
        ids = jnp.concatenate([ids, swap(ids, "seq", bit)], axis=0)
        bit *= 2
    ids = jnp.take(ids, jnp.arange(group) ^ place, axis=0)
    ids = lax.dynamic_slice_in_dim(ids, place * wins, wins, 1)
    ids = ids.transpose(1, 0, 2).reshape(wins, WIN)

    low_w = weights.astype(BF).transpose(1, 0, 2)
    kept = lax.dynamic_slice_in_dim(low_w, core * half, half, 1)
    sent = lax.dynamic_slice_in_dim(low_w, (1 - core) * half, half, 1)
    buf = jnp.concatenate([kept, swap(sent, "rep", 1)], axis=0)
    bit = 2
    while bit < reps:
        buf = jnp.concatenate([buf, swap(buf, "rep", bit)], axis=0)
        bit *= 2
    by_tile = jnp.take(buf, ((owners // slots) ^ me_r) * slots + owners % slots, axis=0)

    def gather_tiles(some):
        count = some.shape[0]
        rows = spread(some, "seq")
        both = in_order(core, rows, swap(rows, "rep", 1), 1)
        return both.transpose(2, 0, 1, 3, 4).reshape(count, rows_dev * seqs, tile)

    qkv_tiles = 3 * width // tile
    out_tiles = width // tile
    up_tiles = (tiles - qkv_tiles - out_tiles) // 2
    w_qkv = gather_tiles(by_tile[:qkv_tiles])
    w_rest = gather_tiles(by_tile[qkv_tiles:])
    w_out = w_rest[:out_tiles]
    w_up = w_rest[out_tiles : out_tiles + up_tiles]
    w_down = w_rest[out_tiles + up_tiles :]

    qkv, mixed, lse = attend_forward(x, positions, w_qkv, ids)
    result, mid, gmixed, d_out, d_up, d_down, d_norm = middle(
        x, positions, mixed, cot, w_out, w_up, w_down, norm_params
    )
    result = exchange(result.reshape(seq_local, span, width), "seq", group)

    def reduce_tiles(grads):
        count = grads.shape[0]
        parts = grads.reshape(count, seqs, 2, half, tile)
        own = pick(parts, core, 2).astype(F32)
        got = swap(pick(parts, 1 - core, 2), "rep", 1).astype(F32)
        mine = (own + got).astype(BF).transpose(1, 0, 2, 3)
        came = lax.all_to_all(mine, "seq", 0, 0, tiled=True)
        return jnp.sum(came.astype(F32), axis=0).astype(BF)

    g_rest = reduce_tiles(jnp.concatenate([d_out, d_up, d_down], axis=0))
    d_qkv, g_input = attend_backward(x, positions, qkv, lse, gmixed, mid, w_qkv, ids)
    g_qkv = reduce_tiles(d_qkv)
    g_input = exchange(g_input.reshape(seq_local, span, width), "seq", group).astype(F32)

    g_tiles = jnp.concatenate([g_qkv, g_rest], axis=0)
    tile_of = jnp.argsort(owners)
    order = ((jnp.arange(reps) ^ me_r)[:, None] * slots + jnp.arange(slots)[None, :]).reshape(-1)
    buf = jnp.take(g_tiles, jnp.take(tile_of, order), axis=0)
    bit = reps // 2
    while bit > 1:
        cut = bit * slots
        got = swap(buf[cut:], "rep", bit)
        buf = (buf[:cut].astype(F32) + got.astype(F32)).astype(BF)
        bit //= 2
    rows = in_order(core, buf[:slots], swap(buf[slots:], "rep", 1), 1).reshape(
        slots, rows_dev, tile
    )

    low_right = right_bases.astype(BF)
    low_left = left_bases.astype(BF)
    cols = tile // seqs

    def to_columns(values):
        return values.reshape(slots, rows_dev, seqs, cols).transpose(2, 1, 0, 3)

    def from_columns(values):
        return values.reshape(seqs, rows_dev, slots, cols).transpose(2, 1, 0, 3).reshape(
            slots, rows_dev, tile
        )

    turned = jnp.einsum("src,scd->srd", rows, low_right, preferred_element_type=F32).astype(BF)
    turned = lax.all_to_all(to_columns(turned), "seq", 0, 0, tiled=True)
    turned = turned.reshape(seqs * rows_dev, slots, cols)
    turned = jnp.einsum("sir,isc->rsc", low_left, turned, preferred_element_type=F32)
    moments = jnp.concatenate(
        [
            to_columns(moment_one.astype(BF).transpose(1, 0, 2)),
            to_columns(moment_two.astype(BF).transpose(1, 0, 2)),
        ],
        axis=2,
    )
    moments = lax.all_to_all(moments, "seq", 0, 0, tiled=True).astype(F32)
    moments = moments.reshape(seqs * rows_dev, 2 * slots, cols)
    direction = adam_step(turned, moments[:, :slots], moments[:, slots:])[2]
    change = jnp.einsum("sir,rsc->isc", low_left, direction.astype(BF), preferred_element_type=F32)
    back = jnp.concatenate([change, turned], axis=1).astype(BF)
    back = back.reshape(seqs, rows_dev, 2 * slots, cols)
    back = lax.all_to_all(back, "seq", 0, 0, tiled=True)
    change = from_columns(back[:, :, :slots])
    change = jnp.einsum("src,sdc->rsd", change, low_right, preferred_element_type=F32)
    turned = from_columns(back[:, :, slots:]).transpose(1, 0, 2).astype(F32)
    first_new, second_new, _ = adam_step(turned, moment_one, moment_two)
    new_weights = weights - LEARN * (change + DECAY * weights)

    pos_part = jnp.sum(g_input, axis=0)
    pad = jnp.zeros((8 - d_norm.shape[0], width), F32)
    small = jnp.concatenate([pos_part, d_norm, pad], axis=0)
    bit = 1
    while bit < reps:
        small = small + swap(small, "rep", bit)
        bit *= 2
    bit = group
    while bit < seqs:
        small = small + swap(small, "seq", bit)
        bit *= 2
    small = small[None]
    bit = 1
    while bit < group:
        small = jnp.concatenate([small, swap(small, "seq", bit)], axis=0)
        bit *= 2
    grad_norms = jnp.sum(small[:, span : span + 4], axis=0)
    grad_pos = jnp.take(small[:, :span], jnp.arange(group) ^ place, axis=0).reshape(WIN, width)
    norm_first, norm_second, norm_dir = adam_step(grad_norms, norm_one, norm_two)
    pos_first, pos_second, pos_dir = adam_step(grad_pos, pos_one, pos_two)
    return (
        result,
        g_input,
        first_new,
        second_new,
        new_weights,
        norm_first,
        norm_second,
        norm_params - LEARN_SMALL * norm_dir,
        pos_first,
        pos_second,
        positions - LEARN_SMALL * pos_dir,
    )


def solution(mesh):
    tokens = P("rep", "seq", None)
    slots = P("seq", "rep", None)
    bases = P("rep", None, None)
    return jax.shard_map(
        body,
        mesh=mesh,
        in_specs=(
            tokens,
            tokens,
            P("rep", "seq"),
            P(),
            slots,
            bases,
            bases,
            slots,
            slots,
            P(),
            P(),
            P(),
            P(),
            P(),
            P(),
        ),
        out_specs=(tokens, tokens, slots, slots, slots, P(), P(), P(), P(), P(), P()),
        check_vma=False,
    )
```

```python
import functools

import jax
import jax.numpy as jnp
import numpy as np
from jax import lax
from jax.experimental import pallas as pl
from jax.experimental.pallas import tpu as pltpu
from jax.sharding import PartitionSpec as P

H = 8
WIN = 512
STEP = 10

EPS_NORM = 1e-05
EPS_ADAM = 1e-08
BETA = 0.5
LEARN = 0.02
LEARN_SMALL = 0.2
DECAY = 0.01
MASKED = -1e30

BF = jnp.bfloat16
F32 = jnp.float32
PARAMS = pltpu.CompilerParams(vmem_limit_bytes=58 * 1024 * 1024)
GELU_A = 0.7978845608028654
GELU_B = 0.044715


def nn(a, b):
    return lax.dot_general(a, b, (((1,), (0,)), ((), ())), preferred_element_type=F32)


def nt(a, b):
    return lax.dot_general(a, b, (((1,), (1,)), ((), ())), preferred_element_type=F32)


def tn(a, b):
    return lax.dot_general(a, b, (((0,), (0,)), ((), ())), preferred_element_type=F32)


def adam_step(gradient, first, second):
    first_new = BETA * first + (1.0 - BETA) * gradient
    second_new = BETA * second + (1.0 - BETA) * gradient * gradient
    fix = 1.0 - BETA**STEP
    direction = first_new / fix / (jnp.sqrt(second_new / fix) + EPS_ADAM)
    return (first_new, second_new, direction)


def row_norm(values):
    center = values - jnp.mean(values, axis=-1, keepdims=True)
    inverse = lax.rsqrt(jnp.mean(center * center, axis=-1, keepdims=True) + EPS_NORM)
    return center * inverse, inverse


def norm_pull(grad_rows, scaled, inverse, gain):
    scaled_grad = grad_rows * gain
    grad_input = inverse * (
        scaled_grad
        - jnp.mean(scaled_grad, axis=-1, keepdims=True)
        - scaled * jnp.mean(scaled_grad * scaled, axis=-1, keepdims=True)
    )
    grad_gain = jnp.sum(grad_rows * scaled, axis=0, keepdims=True)
    grad_shift = jnp.sum(grad_rows, axis=0, keepdims=True)
    return grad_input, grad_gain, grad_shift


def same(shape):
    return pl.BlockSpec(shape, lambda *_: (0,) * len(shape), pipeline_mode=pl.Buffered(1))


def whole(shape):
    return pl.BlockSpec(shape, lambda *_: (0,) * len(shape))


SCALARS = pl.BlockSpec(memory_space=pltpu.SMEM)


def takes(microseconds):
    return pl.CostEstimate(flops=int(microseconds * 1.1e9), bytes_accessed=0, transcendentals=0)


def gather_masks(order):
    masks = [(0, 0)]
    for axis, bit in order:
        step = (bit, 0) if axis == "seq" else (0, bit)
        masks = masks + [(s ^ step[0], t ^ step[1]) for s, t in masks]
    return tuple(masks)


def beyond(masks):
    return tuple((s, t ^ 1) for s, t in masks)


def block_at(me_ref, mask, reps, rows):
    block = (me_ref[0] ^ mask[0]) * reps + (me_ref[1] ^ mask[1])
    return pl.ds(pl.multiple_of(block * rows, rows), rows)


def place_blocks(me_ref, refs, target, plans, reps):
    if plans is None:
        target[...] = refs[0][...]
        return
    for ref, (first, last, masks) in zip(refs, plans):
        for k, mask in enumerate(masks):
            where = block_at(me_ref, mask, reps, ref.shape[2])
            target[first:last, where, :] = ref[k, : last - first]


def take_blocks(me_ref, source, outs, plans, reps, rows):
    if plans is None:
        outs[0][...] = source[...].astype(BF)
        return
    for out, parts in zip(outs, plans):
        at = 0
        for first, last, masks in parts:
            for mask in masks:
                where = block_at(me_ref, mask, reps, rows)
                out[at : at + last - first] = source[first:last, where, :].astype(BF)
                at += last - first


def attend_kernel(plans, reps, me_ref, x_ref, pos_ref, ids_row, ids_col, *refs):
    count = 1 if plans is None else len(plans)
    pieces = refs[:count]
    qkv_ref, mixed_ref, lse_ref, bias, w_ref = refs[count:]
    win, width = pos_ref.shape
    dim = width // H
    tile = w_ref.shape[2]

    place_blocks(me_ref, pieces, w_ref, plans, reps)
    hidden = x_ref[...].reshape(win, width).astype(F32) + pos_ref[...]
    low = hidden.astype(BF)
    for t in range(w_ref.shape[0]):
        qkv_ref[0, :, t * tile : (t + 1) * tile] = nn(low, w_ref[t]).astype(BF)
    row = lax.broadcasted_iota(jnp.int32, (win, win), 0)
    col = lax.broadcasted_iota(jnp.int32, (win, win), 1)
    allowed = (ids_col[0] == ids_row[0]) & (row >= col)
    bias[...] = jnp.where(allowed, 0.0, MASKED)
    half = win // 2
    sums = []
    for pair in range(H // 2):
        outs = []
        for h in (2 * pair, 2 * pair + 1):
            base = 3 * dim * h
            query = qkv_ref[0, :, base : base + dim] * (dim**-0.5)
            keys = qkv_ref[0, :, base + dim : base + 2 * dim]
            values = qkv_ref[0, :, base + 2 * dim : base + 3 * dim]
            parts, logs = [], []
            for lo, upto in ((0, half), (half, win)):
                scores = nt(query[lo : lo + half], keys[:upto]) + bias[lo : lo + half, :upto]
                highest = jnp.max(scores, axis=-1, keepdims=True)
                powers = jnp.exp(scores - highest)
                total = jnp.sum(powers, axis=-1, keepdims=True)
                parts.append(nn(powers.astype(BF), values[:upto]) / total)
                logs.append(highest + jnp.log(total))
            outs.append(jnp.concatenate(parts, axis=0))
            sums.append(jnp.concatenate(logs, axis=0))
        mixed_ref[0, :, pair * 2 * dim : (pair + 1) * 2 * dim] = jnp.concatenate(outs, axis=1).astype(BF)
    lanes = jnp.concatenate(sums + [jnp.zeros((win, 128 - H), F32)], axis=1)
    lse_ref[0] = lanes.T[:H]


def attend_forward(window, me, x, positions, ids, w, plans, tiles, tile, reps):
    group, span, width = x.shape
    win = group * span
    return pl.pallas_call(
        functools.partial(attend_kernel, plans, reps),
        grid=(1,),
        in_specs=[
            SCALARS,
            whole((group, span, width)),
            same((win, width)),
            pl.BlockSpec((1, 1, win), lambda i: (window, 0, 0)),
            pl.BlockSpec((1, win, 1), lambda i: (window, 0, 0)),
        ]
        + [same(piece.shape) for piece in w],
        out_specs=[whole((1, win, 3 * width)), whole((1, win, width)), whole((1, H, win))],
        out_shape=[
            jax.ShapeDtypeStruct((1, win, 3 * width), BF),
            jax.ShapeDtypeStruct((1, win, width), BF),
            jax.ShapeDtypeStruct((1, H, win), F32),
        ],
        scratch_shapes=[pltpu.VMEM((win, win), F32), pltpu.VMEM((tiles, width, tile), BF)],
        compiler_params=PARAMS,
        cost_estimate=takes(8),
        name="attend_forward",
    )(me, x, positions, ids[:, None, :], ids[:, :, None], *w)


def middle_kernel(
    plans, out_plans, reps, rows, outs, wins, me_ref, pos_ref, cot_ref, norm_ref, moments_ref, *refs
):
    x_refs = refs[:wins]
    mixed_refs = refs[wins : 2 * wins]
    refs = refs[2 * wins :]
    count = 1 if plans is None else len(plans)
    pieces = refs[:count]
    refs = refs[count:]
    result_ref, mid_ref, gmixed_ref, dnorm_ref = refs[:4]
    count = 1 if out_plans is None else 2
    grads = refs[4 : 4 + count]
    x_ref, mixed_ref, act, slope, gpre, w_ref, acc = refs[4 + count :]
    step = pl.program_id(0)
    last = pl.num_programs(0) - 1
    win, width = pos_ref.shape
    tile = w_ref.shape[2]
    ups = (w_ref.shape[0] - outs) // 2
    blocks = ups // 2
    up, down = outs, outs + ups

    @pl.when(step == 0)
    def _():
        place_blocks(me_ref, pieces, w_ref, plans, reps)
        acc[...] = jnp.zeros_like(acc)
        dnorm_ref[...] = jnp.zeros_like(dnorm_ref)

    for window in range(wins):

        @pl.when(step == window)
        def _():
            mixed_ref[...] = mixed_refs[window][0]
            x_ref[...] = x_refs[window][...].reshape(win, width)
            if window == 0 and result_ref.shape[2] > wins * width:
                result_ref[:, :, wins * width :] = moments_ref[...]

    mixed = mixed_ref[...]
    hidden = x_ref[...].astype(F32) + pos_ref[...]
    attn = jnp.concatenate([nn(mixed, w_ref[t]) for t in range(outs)], axis=1)
    scaled_one, inverse_one = row_norm(hidden + attn)
    normed = scaled_one * norm_ref[0:1] + norm_ref[1:2]
    low = normed.astype(BF)
    for t in range(ups):
        pre = nn(low, w_ref[up + t])
        square = pre * pre
        bent = jnp.tanh(GELU_A * pre * (1.0 + GELU_B * square))
        act[:, t * tile : (t + 1) * tile] = (0.5 * pre * (1.0 + bent)).astype(BF)
        slope[:, t * tile : (t + 1) * tile] = (
            0.5 * (1.0 + bent)
            + 0.5 * pre * (1.0 - bent * bent) * (GELU_A + 3.0 * GELU_A * GELU_B * square)
        ).astype(BF)
    branch = jnp.concatenate(
        [
            sum(nn(act[:, b * width : (b + 1) * width], w_ref[down + 2 * b + j]) for b in range(blocks))
            for j in range(2)
        ],
        axis=1,
    )
    scaled_two, inverse_two = row_norm(normed + branch)
    result = (scaled_two * norm_ref[2:3] + norm_ref[3:4]).astype(BF)
    result = result.reshape(*result_ref.shape[:2], width)
    for window in range(wins):

        @pl.when(step == window)
        def _():
            result_ref[:, :, window * width : (window + 1) * width] = result

    grad_resid, gain_two, shift_two = norm_pull(
        cot_ref[...].reshape(win, width).astype(F32), scaled_two, inverse_two, norm_ref[2:3]
    )
    gb = grad_resid.astype(BF)
    for b in range(blocks):
        cols = slice(b * width, (b + 1) * width)
        gact = nt(gb[:, :tile], w_ref[down + 2 * b]) + nt(gb[:, tile:], w_ref[down + 2 * b + 1])
        gpre[:, cols] = (gact * slope[:, cols].astype(F32)).astype(BF)
    grad_normed = grad_resid + sum(
        nt(gpre[:, t * tile : (t + 1) * tile], w_ref[up + t]) for t in range(ups)
    )
    grad_mid, gain_one, shift_one = norm_pull(grad_normed, scaled_one, inverse_one, norm_ref[0:1])
    mid_ref[0] = grad_mid
    ga = grad_mid.astype(BF)
    gmixed_ref[0] = sum(nt(ga[:, t * tile : (t + 1) * tile], w_ref[t]) for t in range(outs)).astype(BF)
    dnorm_ref[...] += jnp.concatenate([gain_one, shift_one, gain_two, shift_two], axis=0)
    for b in range(blocks):
        act_t = act[:, b * width : (b + 1) * width].T
        for j in range(2):
            acc[down + 2 * b + j] += nn(act_t, gb[:, j * tile : (j + 1) * tile])
    low_t = low.T
    for t in range(ups):
        acc[up + t] += nn(low_t, gpre[:, t * tile : (t + 1) * tile])
    mixed_t = mixed.T
    for t in range(outs):
        acc[t] += nn(mixed_t, ga[:, t * tile : (t + 1) * tile])

    @pl.when(step == last)
    def _():
        take_blocks(me_ref, acc, grads, out_plans, reps, rows)


def middle(me, x, positions, mixed, cot, norms, moments, together, w, plans, out_plans, grad_shapes, tiles, tile, reps, rows):
    group, span, width = x[0].shape
    wins = len(x)
    win = group * span
    outs = width // tile
    hidden = (tiles - outs) // 2 * tile
    sent = (group, span, wins * width + (moments.shape[2] if together else 0))
    seq_spec = pl.BlockSpec((group, 1, span, width), lambda i: (0, i, 0, 0))
    row_spec = pl.BlockSpec((1, win, width), lambda i: (i, 0, 0))
    return pl.pallas_call(
        functools.partial(middle_kernel, plans, out_plans, reps, rows, outs, wins),
        grid=(wins,),
        in_specs=[SCALARS, same((win, width)), seq_spec, same(norms.shape), same(moments.shape)]
        + [same(part.shape) for part in x]
        + [same(part.shape) for part in mixed]
        + [same(piece.shape) for piece in w],
        out_specs=[whole(sent), row_spec, row_spec, whole(norms.shape)]
        + [whole(shape) for shape in grad_shapes],
        out_shape=[
            jax.ShapeDtypeStruct(sent, BF),
            jax.ShapeDtypeStruct((wins, win, width), F32),
            jax.ShapeDtypeStruct((wins, win, width), BF),
            jax.ShapeDtypeStruct(norms.shape, F32),
        ]
        + [jax.ShapeDtypeStruct(shape, BF) for shape in grad_shapes],
        scratch_shapes=[
            pltpu.VMEM((win, width), BF),
            pltpu.VMEM((win, width), BF),
            pltpu.VMEM((win, hidden), BF),
            pltpu.VMEM((win, hidden), BF),
            pltpu.VMEM((win, hidden), BF),
            pltpu.VMEM((tiles, width, tile), BF),
            pltpu.VMEM((tiles, width, tile), F32),
        ],
        compiler_params=PARAMS,
        cost_estimate=takes(27),
        name="middle",
    )(me, positions, cot, norms, moments, *x, *mixed, *w)


def attend_back_kernel(
    plans, out_plans, reps, rows, last, me_ref, x_ref, pos_ref, ids_row, ids_col, qkv_ref, lse_ref, gmixed_ref,
    mid_ref, dnorm_ref, *refs,
):
    count = 1 if plans is None else len(plans)
    pieces = refs[:count]
    refs = refs[count:]
    if last:
        older, xs = refs[: 2 * last], refs[2 * last : 3 * last]
        ginput_ref = refs[3 * last]
        refs = refs[3 * last + 1 :]
        count = 1 if out_plans is None else 2
        grads = refs[:count]
        bias, w_ref, gproj, acc = refs[count:]
    else:
        ginput_ref, gproj, bias, w_ref = refs
    win, width = pos_ref.shape
    dim = width // H
    tiles, _, tile = w_ref.shape
    factor = dim**-0.5
    half = win // 2
    place_blocks(me_ref, pieces, w_ref, plans, reps)

    key = lax.broadcasted_iota(jnp.int32, (win, win), 0)
    query_at = lax.broadcasted_iota(jnp.int32, (win, win), 1)
    allowed = (ids_col[0] == ids_row[0]) & (query_at >= key)
    bias[...] = jnp.where(allowed, 0.0, MASKED)
    for pair in range(H // 2):
        packed = []
        for h in (2 * pair, 2 * pair + 1):
            base = 3 * dim * h
            query = qkv_ref[0, :, base : base + dim] * factor
            keys = qkv_ref[0, :, base + dim : base + 2 * dim]
            values = qkv_ref[0, :, base + 2 * dim : base + 3 * dim]
            gout = gmixed_ref[0, :, h * dim : (h + 1) * dim]
            lse = lse_ref[0, h : h + 1, :]
            parts = []
            for lo, first in ((half, half), (0, 0)):
                scores = nt(keys[lo : lo + half], query[first:]) + bias[lo : lo + half, first:]
                probs = jnp.exp(scores - lse[:, first:])
                gprobs = nt(values[lo : lo + half], gout[first:])
                inner = jnp.sum(probs * gprobs, axis=0, keepdims=True)
                parts.append((probs, gprobs, inner))
            (probs_b, gprobs_b, inner_b), (probs_a, gprobs_a, inner_a) = parts
            inner_late = inner_a[:, half:] + inner_b
            inner_full = jnp.concatenate([inner_a[:, :half], inner_late], axis=1)
            gs_a = (probs_a * (gprobs_a - inner_full)).astype(BF)
            gs_b = (probs_b * (gprobs_b - inner_late)).astype(BF)
            gvalues = jnp.concatenate(
                [nn(probs_a.astype(BF), gout), nn(probs_b.astype(BF), gout[half:])], axis=0
            )
            gkeys = jnp.concatenate([nn(gs_a, query), nn(gs_b, query[half:])], axis=0)
            gq_a = tn(gs_a, keys[:half])
            gq_b = tn(gs_b, keys[half:])
            gquery = jnp.concatenate([gq_a[:half], gq_a[half:] + gq_b], axis=0) * factor
            packed += [gquery.astype(BF), gkeys.astype(BF), gvalues.astype(BF)]
        gproj[:, pair * 6 * dim : (pair + 1) * 6 * dim] = jnp.concatenate(packed, axis=1)
    total = mid_ref[0]
    for t in range(tiles):
        total += nt(gproj[:, t * tile : (t + 1) * tile], w_ref[t])
    ginput_ref[...] = total.astype(BF).reshape(ginput_ref.shape)
    if not last:
        return

    hidden = [ref[...].reshape(win, width).astype(F32) + pos_ref[...] for ref in (*xs, x_ref)]
    low_t = [part.astype(BF).T for part in hidden]
    projs = list(older[:last]) + [gproj]
    for t in range(tiles):
        acc[t] = sum(nn(low, proj[:, t * tile : (t + 1) * tile]) for low, proj in zip(low_t, projs))
    for ref in older[last:]:
        total += ref[...].reshape(win, width).astype(F32)
    for j in range(width // tile):
        acc[tiles + j] = total[:, j * tile : (j + 1) * tile]
    if out_plans is not None:
        small = jnp.concatenate(
            [dnorm_ref[:, j * tile : (j + 1) * tile] for j in range(width // tile)], axis=0
        )
        small = jnp.concatenate([small, jnp.zeros((rows - small.shape[0], tile), F32)], axis=0)
        for b in range(win // rows):
            acc[acc.shape[0] - 1, b * rows : (b + 1) * rows] = small
    else:
        acc[acc.shape[0] - 1] = jnp.zeros((win, tile), F32)
    take_blocks(me_ref, acc, grads, out_plans, reps, rows)


def attend_backward(
    window, me, x, positions, ids, qkv, lse, gmixed, mid, dnorm, w, plans, tiles, tile, reps,
    older=None, out_plans=None, grad_shapes=(), rows=0,
):
    group, span, width = x[window].shape
    win = group * span
    last = len(older) // 2 if older is not None else 0
    row_spec = pl.BlockSpec((1, win, width), lambda i: (window, 0, 0))
    out_specs = [whole((group, span, width))]
    out_shape = [jax.ShapeDtypeStruct((group, span, width), BF)]
    scratch = [pltpu.VMEM((win, win), F32), pltpu.VMEM((tiles, width, tile), BF)]
    more = []
    if last:
        more = list(older) + list(x[:window])
        out_specs += [whole(shape) for shape in grad_shapes]
        out_shape += [jax.ShapeDtypeStruct(shape, BF) for shape in grad_shapes]
        scratch += [
            pltpu.VMEM((win, 3 * width), BF),
            pltpu.VMEM((tiles + width // tile + 1, width, tile), F32),
        ]
    else:
        out_specs.append(whole((win, 3 * width)))
        out_shape.append(jax.ShapeDtypeStruct((win, 3 * width), BF))
    return pl.pallas_call(
        functools.partial(attend_back_kernel, plans, out_plans, reps, rows, last),
        grid=(1,),
        in_specs=[
            SCALARS,
            whole((group, span, width)),
            same((win, width)),
            pl.BlockSpec((1, 1, win), lambda i: (window, 0, 0)),
            pl.BlockSpec((1, win, 1), lambda i: (window, 0, 0)),
            whole((1, win, 3 * width)),
            whole((1, H, win)),
            row_spec,
            row_spec,
            same(dnorm.shape),
        ]
        + [same(piece.shape) for piece in w]
        + [same(part.shape) for part in more],
        out_specs=out_specs,
        out_shape=out_shape,
        scratch_shapes=scratch,
        compiler_params=PARAMS,
        cost_estimate=takes(10),
        name="attend_backward",
    )(me, x[window], positions, ids[:, None, :], ids[:, :, None], qkv, lse, gmixed, mid, dnorm, *w, *more)


def right_kernel(rows_ref, right_ref, out_ref):
    seqs, _, _ = out_ref.shape
    slots, _, tile = rows_ref.shape
    cols = tile // seqs
    for s in range(slots):
        turned = nn(rows_ref[s], right_ref[s]).astype(BF)
        for j in range(seqs):
            out_ref[j, :, s * cols : (s + 1) * cols] = turned[:, j * cols : (j + 1) * cols]


def right_turn(rows, right, seqs):
    slots, rows_dev, tile = rows.shape
    return pl.pallas_call(
        right_kernel,
        out_shape=jax.ShapeDtypeStruct((seqs, rows_dev, slots * tile // seqs), BF),
        compiler_params=PARAMS,
        name="right_turn",
    )(rows, right)


def left_kernel(x_ref, moments_ref, left_ref, left_t_ref, out_ref):
    seqs, rows_dev, wide = x_ref.shape
    slots, width, _ = left_ref.shape
    cols = wide // slots
    x = x_ref[...].reshape(width, wide)
    moments = moments_ref[...].reshape(width, 2 * wide).astype(F32)
    turned = [nn(left_t_ref[s], x[:, s * cols : (s + 1) * cols]) for s in range(slots)]
    turned = jnp.concatenate(turned, axis=1)
    direction = adam_step(turned, moments[:, :wide], moments[:, wide:])[2].astype(BF)
    change = [nn(left_ref[s], direction[:, s * cols : (s + 1) * cols]) for s in range(slots)]
    out = jnp.concatenate(change + [turned], axis=1).astype(BF)
    out_ref[...] = out.reshape(out_ref.shape)


def left_turns(x, moments, left, left_t):
    seqs, rows_dev, wide = x.shape
    return pl.pallas_call(
        left_kernel,
        out_shape=jax.ShapeDtypeStruct((seqs, rows_dev, 2 * wide), BF),
        compiler_params=PARAMS,
        name="left_turns",
    )(x, moments, left, left_t)


def last_kernel(back_ref, right_ref, w_ref, one_ref, two_ref, new_one, new_two, new_w):
    seqs, rows_dev, _ = back_ref.shape
    slots, _, tile = w_ref.shape
    cols = tile // seqs
    for s in range(slots):

        def columns(first):
            return jnp.concatenate(
                [back_ref[j, :, first + s * cols : first + (s + 1) * cols] for j in range(seqs)], axis=1
            )

        change = nt(columns(0), right_ref[s])
        turned = columns(slots * cols).astype(F32)
        new_one[s], new_two[s], _ = adam_step(turned, one_ref[s], two_ref[s])
        old = w_ref[s]
        new_w[s] = old - LEARN * (change + DECAY * old)


def last_turn(back, right, weights, one, two):
    shape = jax.ShapeDtypeStruct(weights.shape, F32)
    return pl.pallas_call(
        last_kernel,
        out_shape=[shape, shape, shape],
        compiler_params=PARAMS,
        name="last_turn",
    )(back, right, weights, one, two)


def columns_kernel(one_ref, two_ref, out_ref):
    seqs = out_ref.shape[0]
    slots, _, tile = one_ref.shape
    cols = tile // seqs
    for first, ref in ((0, one_ref), (slots, two_ref)):
        for s in range(slots):
            values = ref[s].astype(BF)
            for j in range(seqs):
                at = (first + s) * cols
                out_ref[j, :, at : at + cols] = values[:, j * cols : (j + 1) * cols]


def moment_columns(one, two, seqs):
    slots, rows_dev, tile = one.shape
    return pl.pallas_call(
        columns_kernel,
        out_shape=jax.ShapeDtypeStruct((seqs, rows_dev, 2 * slots * tile // seqs), BF),
        compiler_params=PARAMS,
        name="moment_columns",
    )(one, two)


def bases_kernel(left_ref, right_ref, low_left, low_left_t, low_right):
    left = left_ref[0].astype(BF)
    low_left[0] = left
    low_left_t[0] = left.T
    low_right[0] = right_ref[0].astype(BF)


def low_bases(left, right):
    slots, width, _ = left.shape
    tile = right.shape[1]
    big = pl.BlockSpec((1, width, width), lambda i: (i, 0, 0))
    little = pl.BlockSpec((1, tile, tile), lambda i: (i, 0, 0))
    return pl.pallas_call(
        bases_kernel,
        grid=(slots,),
        in_specs=[big, little],
        out_specs=[big, big, little],
        out_shape=[
            jax.ShapeDtypeStruct(left.shape, BF),
            jax.ShapeDtypeStruct(left.shape, BF),
            jax.ShapeDtypeStruct(right.shape, BF),
        ],
        compiler_params=PARAMS,
        name="low_bases",
    )(left, right)


def swap(x, axis, bit):
    size = lax.axis_size(axis)
    return lax.ppermute(x, axis, [(i, i ^ bit) for i in range(size)])


def exchange(x, axis, group):
    size = lax.axis_size(axis)
    groups = None
    if group != size:
        groups = [[base + i for i in range(group)] for base in range(0, size, group)]
    return lax.all_to_all(x, axis, 0, 0, axis_index_groups=groups, tiled=True)


def after(x, *others):
    return lax.optimization_barrier((x,) + others)[0]


def powers(first, size):
    bits = []
    while first < size:
        bits.append(first)
        first *= 2
    return bits


def gather(block, order):
    own = block[None]
    for axis, bit in order[:-1]:
        own = jnp.concatenate([own, swap(own, axis, bit)], axis=0)
    return own, swap(own, *order[-1])


def add(a, b, *others):
    if others:
        b = after(b, *others)
    return (a.astype(F32) + b.astype(F32)).astype(BF)


def double(buf, axis, bit, *others):
    got = swap(buf, axis, bit)
    if others:
        got = after(got, *others)
    return jnp.concatenate([buf, got], axis=0)


def halve(buf, axis, bit, *others):
    cut = buf.shape[0] // 2
    return add(buf[:cut], swap(buf[cut:], axis, bit), *others)


def body(
    inputs,
    cotangent,
    segments,
    owners,
    weights,
    left_bases,
    right_bases,
    moment_one,
    moment_two,
    norm_params,
    norm_one,
    norm_two,
    positions,
    pos_one,
    pos_two,
):
    seqs = lax.axis_size("seq")
    reps = lax.axis_size("rep")
    me_s = lax.axis_index("seq")
    me_r = lax.axis_index("rep")
    me = jnp.stack([me_s, me_r]).astype(jnp.int32)
    seq_local, span, width = inputs.shape
    rows_dev, slots, tile = weights.shape
    tiles = owners.shape[0]
    rows = rows_dev // reps
    group = WIN // span
    place = me_s % group
    wins = seq_local // group
    aligned = rows % 16 == 0
    blocks = seqs * reps
    seq_bits = [("seq", b) for b in powers(1, seqs)[::-1]]
    far_bits = [("rep", b) for b in powers(2, reps)]
    core_bit = [("rep", 1)]

    by_window = inputs.reshape(group, wins, span, width)
    x = [exchange(by_window[:, 0], "seq", group)]

    low_w = weights.astype(BF).transpose(1, 0, 2).reshape(slots, reps, rows, tile).transpose(1, 0, 2, 3)
    near = [lax.dynamic_index_in_dim(low_w, me_r, 0, keepdims=False)]
    for k in range(1, reps):
        near.append(swap(lax.dynamic_index_in_dim(low_w, me_r ^ k, 0, keepdims=False), "rep", k))
    near = jnp.concatenate(near, axis=0)
    near = jnp.take(near, ((owners // slots) ^ me_r) * slots + owners % slots, axis=0)
    ids = segments.reshape(-1)
    id_tiles = -(-2 * ids.shape[0] // (rows * tile))
    ids = jnp.concatenate([ids // 64, ids % 64]).astype(BF)
    ids = jnp.pad(ids, (0, id_tiles * rows * tile - ids.shape[0])).reshape(id_tiles, rows, tile)

    qkv_tiles = 3 * width // tile
    rest_tiles = tiles - qkv_tiles
    qkv_at, rest_at = qkv_tiles // 2, rest_tiles // 2
    split = qkv_at + id_tiles
    by_slot = [values.transpose(1, 0, 2) for values in (weights, moment_one, moment_two)]
    rest = near[qkv_tiles:][None]
    near = jnp.concatenate([near[:qkv_at], ids, near[qkv_at:qkv_tiles]], axis=0)[None]
    moments = moment_columns(after(by_slot[1], near), by_slot[2], seqs)
    for i, step in enumerate(seq_bits[:-1]):
        near = double(near, *step, *([moments] if i == 0 else [x[0]]))
        rest = double(after(rest, moments) if i == 0 else rest, *step, near)
    for w in range(1, wins):
        x.append(exchange(after(by_window[:, w], near), "seq", group))
    cot = exchange(after(cotangent, x[-1]), "seq", group).reshape(group, wins, span, width)

    def table_of(masks):
        table = np.zeros(blocks, np.int32)
        for k, (s, t) in enumerate(masks):
            table[s * reps + t] = k
        return jnp.asarray(table)

    orders = [seq_bits[-1:] + far_bits, far_bits + seq_bits[-1:]]

    def pieces_of(bufs, ranges):
        pieces, plans = [], []
        for buf, order, (first, last) in zip(bufs, orders, ranges):
            masks = gather_masks(seq_bits[:-1] + order)
            pieces += [buf, swap(buf, *core_bit[0])]
            plans += [(first, last, masks), (first, last, beyond(masks))]
        return settle(pieces, plans)

    def settle(pieces, plans):
        if aligned:
            return pieces, plans
        at = jnp.arange(blocks)
        full = []
        for i in range(0, len(pieces), 2):
            count = plans[i][1] - plans[i][0]
            table = table_of(plans[i][2] + plans[i + 1][2])
            both = jnp.concatenate([pieces[i][:, :count], pieces[i + 1][:, :count]], axis=0)
            both = jnp.take(both, table[((at // reps) ^ me_s) * reps + ((at % reps) ^ me_r)], axis=0)
            full.append(both.transpose(1, 0, 2, 3).reshape(count, blocks * rows, tile))
        return [jnp.concatenate(full, axis=0)], None

    bufs = [near[:, :split], near[:, split:]]
    bufs = [double(buf, *order[0]) for buf, order in zip(bufs, orders)]
    ids = bufs[0][:, qkv_at:]
    rest = after(rest, *bufs)
    for i in range(1, len(orders[0])):
        bufs = [double(buf, *order[i]) for buf, order in zip(bufs, orders)]
    w_qkv, qkv_plans = pieces_of(bufs, [(0, qkv_at), (qkv_at, qkv_tiles)])
    rest = [rest[:, :rest_at], rest[:, rest_at:]]
    rest = [double(buf, *order[0], *bufs) for buf, order in zip(rest, orders)]

    ids = ids.reshape(seqs, -1)[:, : 2 * seq_local * span].astype(jnp.int32)
    ids = (ids[:, : seq_local * span] * 64 + ids[:, seq_local * span :]).reshape(seqs, seq_local, span)
    spots = [0] * seqs
    for k, (s, _) in enumerate(gather_masks(seq_bits[:-1] + seq_bits[-1:])):
        spots[s] = k
    ids = jnp.take(ids, jnp.asarray(spots[:group])[jnp.arange(group) ^ place], axis=0)
    ids = lax.dynamic_slice_in_dim(ids, place * wins, wins, 1)
    ids = ids.transpose(1, 0, 2).reshape(wins, WIN)

    def scatter_plans(parts):
        count = parts[-1][1]
        if not aligned:
            return None, [(count, blocks * rows, tile)]
        own = [(first, last, gather_masks(order[:0:-1])) for first, last, order in parts]
        other = [(first, last, beyond(masks)) for first, last, masks in own]
        shape = (count * blocks // 2, rows, tile)
        return [own, other], [shape, shape]

    def scatter_tiles(grads, parts, *others):
        if not aligned:
            plain = grads[0].reshape(-1, blocks, rows, tile).transpose(1, 0, 2, 3)
            own, other = [], []
            for first, last, order in parts:
                masks = gather_masks(order[:0:-1])
                for target, some in ((own, masks), (other, beyond(masks))):
                    spots = np.array([s * reps + t for s, t in some])
                    at = ((spots // reps) ^ me_s) * reps + ((spots % reps) ^ me_r)
                    target.append(jnp.take(plain[:, first:last], at, axis=0).reshape(-1, rows, tile))
            grads = [jnp.concatenate(own, axis=0), jnp.concatenate(other, axis=0)]
        return add(grads[0], swap(grads[1], *core_bit[0]), *others)

    def cut_parts(buf, parts):
        out, at = [], 0
        for first, last, _ in parts:
            size = (last - first) * blocks // 2
            out.append(buf[at : at + size])
            at += size
        return out

    def join(bufs, parts):
        entries = 2 ** len(seq_bits[:-1])
        return jnp.concatenate([buf.reshape(entries, -1, rows, tile) for buf in bufs], axis=1)

    zyxc = seq_bits + far_bits + core_bit
    zxyc = seq_bits[:-1] + far_bits + seq_bits[-1:] + core_bit
    ahead = []
    ids = after(ids, *rest)
    for w in range(wins):
        ahead.append(attend_forward(w, me, x[w], positions, ids, w_qkv, qkv_plans, qkv_tiles, tile, reps))
        if w == 0:
            for i in range(1, len(orders[0])):
                rest = [double(buf, *order[i], ahead[0][1]) for buf, order in zip(rest, orders)]
            ids = after(ids, *rest)
    w_rest, rest_plans = pieces_of(rest, [(0, rest_at), (rest_at, rest_tiles)])
    low_left, low_left_t, low_right = low_bases(after(left_bases, ahead[-1][1]), right_bases)
    cot = after(cot, low_left)
    rest_parts = [(0, rest_at, zyxc[::-1]), (rest_at, rest_tiles, zxyc[::-1])]
    out_plans, shapes = scatter_plans(rest_parts)
    result, mid, gmixed, d_norm, *d_rest = middle(
        me, x, positions, [part[1] for part in ahead], cot, norm_params, moments, group == seqs, w_rest, rest_plans, out_plans, shapes, rest_tiles, tile, reps, rows
    )
    result = exchange(result, "seq", group)
    if group == seqs:
        moments = result[:, :, wins * width :]
    else:
        moments = lax.all_to_all(after(moments, result), "seq", 0, 0, tiled=True)
    result = result[:, :, : wins * width].reshape(group, span, wins, width)
    result = result.transpose(0, 2, 1, 3).reshape(seq_local, span, width)
    rest_buf = scatter_tiles(d_rest, rest_parts)
    rest = cut_parts(rest_buf, rest_parts)

    qkv_total = qkv_tiles + width // tile + 1
    qkv_parts = [(0, 4, zyxc[::-1]), (4, qkv_total, zxyc[::-1])]
    out_plans, shapes = scatter_plans(qkv_parts)
    args = (w_qkv, qkv_plans, qkv_tiles, tile, reps)
    g_inputs, projs = [], []
    for w in range(wins - 1):
        qkv, _, lse = ahead[w]
        g_input, proj = attend_backward(w, me, x, positions, ids, qkv, lse, gmixed, mid, d_norm, *args)
        g_inputs.append(g_input)
        projs.append(proj)
    w = wins - 1
    qkv, _, lse = ahead[w]
    g_input, *d_qkv = attend_backward(
        w, me, x, positions, ids, qkv, lse, after(gmixed, rest_buf), mid, d_norm, *args,
        older=projs + g_inputs, out_plans=out_plans, grad_shapes=shapes, rows=rows,
    )
    steps = [[order[1 + i] for _, _, order in rest_parts] for i in range(len(orders[0]))]
    rest = [halve(buf, *step) for buf, step in zip(rest, steps[0])]
    d_qkv[-1] = after(d_qkv[-1], *rest)
    qkv_buf = scatter_tiles(d_qkv, qkv_parts)
    mine = cut_parts(qkv_buf, qkv_parts)
    for some in steps[1:]:
        rest = [halve(buf, *step, qkv_buf) for buf, step in zip(rest, some)]
    rest = join(rest, rest_parts)
    for i, some in enumerate(steps):
        mine = [halve(buf, *step, rest) for buf, step in zip(mine, some)]
    mine = join(mine, qkv_parts)
    for step in seq_bits[-2::-1]:
        rest = halve(rest, *step, mine)
        mine = halve(mine, *step, rest)
    rest, mine = rest[0], mine[0]
    g_input = jnp.stack(g_inputs + [g_input], axis=1).reshape(seq_local, span, width)
    g_input = exchange(after(g_input, result), "seq", group)

    small = mine[qkv_tiles:]
    sums = jnp.concatenate([mine[:qkv_tiles], rest], axis=0)
    tile_of = jnp.sum(
        jnp.where(owners[None, :] == jnp.arange(tiles)[:, None], jnp.arange(tiles)[None, :], 0), axis=1
    )
    sums = jnp.take(sums, tile_of, axis=0).reshape(reps, slots, rows, tile)
    sums = lax.all_to_all(after(sums, g_input), "rep", 0, 0, tiled=True)
    sums = sums.transpose(1, 0, 2, 3).reshape(slots, rows_dev, tile)

    turned = right_turn(sums, low_right, seqs)
    small = after(small, turned)
    turned = lax.all_to_all(turned, "seq", 0, 0, tiled=True)
    back = left_turns(turned, moments, low_left, low_left_t)
    back = lax.all_to_all(back, "seq", 0, 0, tiled=True)
    news = last_turn(back, low_right, *by_slot)
    first_new, second_new, new_weights = [values.transpose(1, 0, 2) for values in news]

    pos_order = zyxc
    own, other = gather(small[: width // tile], pos_order)
    masks = gather_masks(pos_order[:-1])
    table = table_of(masks + beyond(masks))
    at = jnp.arange(blocks)
    grad_pos = jnp.concatenate([own, other], axis=0)
    grad_pos = jnp.take(grad_pos, table[((at // reps) ^ me_s) * reps + ((at % reps) ^ me_r)], axis=0)
    grad_pos = grad_pos.transpose(0, 2, 1, 3).reshape(WIN, width).astype(F32)
    if aligned:
        grad_norms = small[-1, : 4 * width // tile].astype(F32)
        grad_norms = grad_norms.reshape(width // tile, 4, tile).transpose(1, 0, 2).reshape(4, width)
    else:
        grad_norms = lax.psum(d_norm, ("seq", "rep"))
    norm_first, norm_second, norm_dir = adam_step(grad_norms, norm_one, norm_two)
    pos_first, pos_second, pos_dir = adam_step(grad_pos, pos_one, pos_two)
    return (
        result,
        g_input.astype(F32),
        first_new,
        second_new,
        new_weights,
        norm_first,
        norm_second,
        norm_params - LEARN_SMALL * norm_dir,
        pos_first,
        pos_second,
        positions - LEARN_SMALL * pos_dir,
    )


def solution(mesh):
    tokens = P("rep", "seq", None)
    slots = P("seq", "rep", None)
    bases = P("rep", None, None)
    return jax.shard_map(
        body,
        mesh=mesh,
        in_specs=(
            tokens,
            tokens,
            P("rep", "seq"),
            P(),
            slots,
            bases,
            bases,
            slots,
            slots,
            P(),
            P(),
            P(),
            P(),
            P(),
            P(),
        ),
        out_specs=(tokens, tokens, slots, slots, slots, P(), P(), P(), P(), P(), P()),
        check_vma=False,
    )
```

```python
import functools

import jax
import jax.numpy as jnp
import numpy as np
from jax import lax
from jax.experimental import pallas as pl
from jax.experimental.pallas import tpu as pltpu
from jax.sharding import PartitionSpec as P

H = 8
WIN = 512
STEP = 10

EPS_NORM = 1e-05
EPS_ADAM = 1e-08
BETA = 0.5
LEARN = 0.02
LEARN_SMALL = 0.2
DECAY = 0.01
MASKED = -1e30

BF = jnp.bfloat16
F32 = jnp.float32
PARAMS = pltpu.CompilerParams(vmem_limit_bytes=58 * 1024 * 1024)
GELU_A = 0.7978845608028654
GELU_B = 0.044715


def nn(a, b):
    return lax.dot_general(a, b, (((1,), (0,)), ((), ())), preferred_element_type=F32)


def nt(a, b):
    return lax.dot_general(a, b, (((1,), (1,)), ((), ())), preferred_element_type=F32)


def tn(a, b):
    return lax.dot_general(a, b, (((0,), (0,)), ((), ())), preferred_element_type=F32)


def adam_step(gradient, first, second):
    first_new = BETA * first + (1.0 - BETA) * gradient
    second_new = BETA * second + (1.0 - BETA) * gradient * gradient
    fix = 1.0 - BETA**STEP
    direction = first_new / fix / (jnp.sqrt(second_new / fix) + EPS_ADAM)
    return (first_new, second_new, direction)


def row_norm(values):
    center = values - jnp.mean(values, axis=-1, keepdims=True)
    inverse = lax.rsqrt(jnp.mean(center * center, axis=-1, keepdims=True) + EPS_NORM)
    return center * inverse, inverse


def norm_pull(grad_rows, scaled, inverse, gain):
    scaled_grad = grad_rows * gain
    grad_input = inverse * (
        scaled_grad
        - jnp.mean(scaled_grad, axis=-1, keepdims=True)
        - scaled * jnp.mean(scaled_grad * scaled, axis=-1, keepdims=True)
    )
    grad_gain = jnp.sum(grad_rows * scaled, axis=0, keepdims=True)
    grad_shift = jnp.sum(grad_rows, axis=0, keepdims=True)
    return grad_input, grad_gain, grad_shift


def same(shape):
    return pl.BlockSpec(shape, lambda *_: (0,) * len(shape), pipeline_mode=pl.Buffered(1))


def whole(shape):
    return pl.BlockSpec(shape, lambda *_: (0,) * len(shape))


SCALARS = pl.BlockSpec(memory_space=pltpu.SMEM)


def takes(microseconds):
    return pl.CostEstimate(flops=int(microseconds * 1e6), bytes_accessed=0, transcendentals=0)


def gather_masks(order):
    masks = [(0, 0)]
    for axis, bit in order:
        step = (bit, 0) if axis == "seq" else (0, bit)
        masks = masks + [(s ^ step[0], t ^ step[1]) for s, t in masks]
    return tuple(masks)


def beyond(masks):
    return tuple((s, t ^ 1) for s, t in masks)


def block_at(me_ref, mask, reps, rows):
    block = (me_ref[0] ^ mask[0]) * reps + (me_ref[1] ^ mask[1])
    return pl.ds(pl.multiple_of(block * rows, rows), rows)


def place_blocks(me_ref, refs, target, plans, reps):
    if plans is None:
        target[...] = refs[0][...]
        return
    for ref, (first, last, masks) in zip(refs, plans):
        for k, mask in enumerate(masks):
            where = block_at(me_ref, mask, reps, ref.shape[2])
            target[first:last, where, :] = ref[k, : last - first]


def take_blocks(me_ref, source, outs, plans, reps, rows):
    if plans is None:
        outs[0][...] = source[...].astype(BF)
        return
    for out, parts in zip(outs, plans):
        at = 0
        for first, last, masks in parts:
            for mask in masks:
                where = block_at(me_ref, mask, reps, rows)
                out[at : at + last - first] = source[first:last, where, :].astype(BF)
                at += last - first


def attend_kernel(plans, reps, me_ref, x_ref, pos_ref, ids_row, ids_col, *refs):
    count = 1 if plans is None else len(plans)
    pieces = refs[:count]
    qkv_ref, mixed_ref, lse_ref, bias, w_ref = refs[count:]
    win, width = pos_ref.shape
    dim = width // H
    tile = w_ref.shape[2]


    @pl.when(pl.program_id(0) == 0)
    def _():
        place_blocks(me_ref, pieces, w_ref, plans, reps)

    hidden = x_ref[...].reshape(win, width).astype(F32) + pos_ref[...]
    low = hidden.astype(BF)
    for t in range(w_ref.shape[0]):
        qkv_ref[0, :, t * tile : (t + 1) * tile] = nn(low, w_ref[t]).astype(BF)
    row = lax.broadcasted_iota(jnp.int32, (win, win), 0)
    col = lax.broadcasted_iota(jnp.int32, (win, win), 1)
    allowed = (ids_col[0] == ids_row[0]) & (row >= col)
    bias[...] = jnp.where(allowed, 0.0, MASKED)
    half = win // 2
    sums = []
    for pair in range(H // 2):
        outs = []
        for h in (2 * pair, 2 * pair + 1):
            base = 3 * dim * h
            query = qkv_ref[0, :, base : base + dim] * (dim**-0.5)
            keys = qkv_ref[0, :, base + dim : base + 2 * dim]
            values = qkv_ref[0, :, base + 2 * dim : base + 3 * dim]
            parts, logs = [], []
            for lo, upto in ((0, half), (half, win)):
                scores = nt(query[lo : lo + half], keys[:upto]) + bias[lo : lo + half, :upto]
                highest = jnp.max(scores, axis=-1, keepdims=True)
                powers = jnp.exp(scores - highest)
                total = jnp.sum(powers, axis=-1, keepdims=True)
                parts.append(nn(powers.astype(BF), values[:upto]) / total)
                logs.append(highest + jnp.log(total))
            outs.append(jnp.concatenate(parts, axis=0))
            sums.append(jnp.concatenate(logs, axis=0))
        mixed_ref[0, :, pair * 2 * dim : (pair + 1) * 2 * dim] = jnp.concatenate(outs, axis=1).astype(BF)
    lanes = jnp.concatenate(sums + [jnp.zeros((win, 128 - H), F32)], axis=1)
    lse_ref[0] = lanes.T[:H]


def attend_forward(me, x, positions, ids, w, plans, tiles, tile, reps):
    group, wins, span, width = x.shape
    win = group * span
    return pl.pallas_call(
        functools.partial(attend_kernel, plans, reps),
        grid=(wins,),
        in_specs=[
            SCALARS,
            pl.BlockSpec((group, 1, span, width), lambda i: (0, i, 0, 0)),
            same((win, width)),
            pl.BlockSpec((1, 1, win), lambda i: (i, 0, 0)),
            pl.BlockSpec((1, win, 1), lambda i: (i, 0, 0)),
        ]
        + [same(piece.shape) for piece in w],
        out_specs=[
            pl.BlockSpec((1, win, 3 * width), lambda i: (i, 0, 0)),
            pl.BlockSpec((1, win, width), lambda i: (i, 0, 0)),
            pl.BlockSpec((1, H, win), lambda i: (i, 0, 0)),
        ],
        out_shape=[
            jax.ShapeDtypeStruct((wins, win, 3 * width), BF),
            jax.ShapeDtypeStruct((wins, win, width), BF),
            jax.ShapeDtypeStruct((wins, H, win), F32),
        ],
        scratch_shapes=[pltpu.VMEM((win, win), F32), pltpu.VMEM((tiles, width, tile), BF)],
        compiler_params=PARAMS,
        cost_estimate=takes(18),
        name="attend_forward",
    )(me, x, positions, ids[:, None, :], ids[:, :, None], *w)


def middle_kernel(
    plans, out_plans, reps, rows, outs, wins, me_ref, x_ref, pos_ref, mixed_ref, cot_ref, norm_ref, moments_ref, *refs
):
    count = 1 if plans is None else len(plans)
    pieces = refs[:count]
    refs = refs[count:]
    result_ref, mid_ref, gmixed_ref, dnorm_ref = refs[:4]
    count = 1 if out_plans is None else 2
    grads = refs[4 : 4 + count]
    act, slope, gpre, w_ref, acc = refs[4 + count :]
    step = pl.program_id(0)
    last = wins - 1
    win, width = pos_ref.shape
    tile = w_ref.shape[2]
    ups = (w_ref.shape[0] - outs) // 2
    blocks = ups // 2
    up, down = outs, outs + ups

    @pl.when(step == 0)
    def _():
        place_blocks(me_ref, pieces, w_ref, plans, reps)
        acc[...] = jnp.zeros_like(acc)
        dnorm_ref[...] = jnp.zeros_like(dnorm_ref)
        if result_ref.shape[2] > (last + 1) * width:
            result_ref[:, :, (last + 1) * width :] = moments_ref[...]

    mixed = mixed_ref[0]
    hidden = x_ref[...].reshape(win, width).astype(F32) + pos_ref[...]
    attn = jnp.concatenate([nn(mixed, w_ref[t]) for t in range(outs)], axis=1)
    scaled_one, inverse_one = row_norm(hidden + attn)
    normed = scaled_one * norm_ref[0:1] + norm_ref[1:2]
    low = normed.astype(BF)
    for t in range(ups):
        pre = nn(low, w_ref[up + t])
        square = pre * pre
        bent = jnp.tanh(GELU_A * pre * (1.0 + GELU_B * square))
        act[:, t * tile : (t + 1) * tile] = (0.5 * pre * (1.0 + bent)).astype(BF)
        slope[:, t * tile : (t + 1) * tile] = (
            0.5 * (1.0 + bent)
            + 0.5 * pre * (1.0 - bent * bent) * (GELU_A + 3.0 * GELU_A * GELU_B * square)
        ).astype(BF)
    branch = jnp.concatenate(
        [
            sum(nn(act[:, b * width : (b + 1) * width], w_ref[down + 2 * b + j]) for b in range(blocks))
            for j in range(2)
        ],
        axis=1,
    )
    scaled_two, inverse_two = row_norm(normed + branch)
    result = scaled_two * norm_ref[2:3] + norm_ref[3:4]
    result = result.astype(BF).reshape(*result_ref.shape[:2], width)
    for window in range(wins):

        @pl.when(step == window)
        def _():
            result_ref[:, :, window * width : (window + 1) * width] = result

    grad_resid, gain_two, shift_two = norm_pull(
        cot_ref[...].reshape(win, width).astype(F32), scaled_two, inverse_two, norm_ref[2:3]
    )
    gb = grad_resid.astype(BF)
    for b in range(blocks):
        cols = slice(b * width, (b + 1) * width)
        gact = nt(gb[:, :tile], w_ref[down + 2 * b]) + nt(gb[:, tile:], w_ref[down + 2 * b + 1])
        gpre[:, cols] = (gact * slope[:, cols].astype(F32)).astype(BF)
    grad_normed = grad_resid + sum(
        nt(gpre[:, t * tile : (t + 1) * tile], w_ref[up + t]) for t in range(ups)
    )
    grad_mid, gain_one, shift_one = norm_pull(grad_normed, scaled_one, inverse_one, norm_ref[0:1])
    mid_ref[0] = grad_mid
    ga = grad_mid.astype(BF)
    gmixed_ref[0] = sum(nt(ga[:, t * tile : (t + 1) * tile], w_ref[t]) for t in range(outs)).astype(BF)
    dnorm_ref[...] += jnp.concatenate([gain_one, shift_one, gain_two, shift_two], axis=0)
    for b in range(blocks):
        act_t = act[:, b * width : (b + 1) * width].T
        for j in range(2):
            acc[down + 2 * b + j] += nn(act_t, gb[:, j * tile : (j + 1) * tile])
    low_t = low.T
    for t in range(ups):
        acc[up + t] += nn(low_t, gpre[:, t * tile : (t + 1) * tile])
    mixed_t = mixed.T
    for t in range(outs):
        acc[t] += nn(mixed_t, ga[:, t * tile : (t + 1) * tile])

    @pl.when(step == last)
    def _():
        take_blocks(me_ref, acc, grads, out_plans, reps, rows)


def middle(me, x, positions, mixed, cot, norms, moments, together, w, plans, out_plans, grad_shapes, tiles, tile, reps, rows):
    group, wins, span, width = x.shape
    win = group * span
    outs = width // tile
    hidden = (tiles - outs) // 2 * tile
    sent = (group, span, wins * width + (moments.shape[2] if together else 0))
    seq_spec = pl.BlockSpec((group, 1, span, width), lambda i: (0, i, 0, 0))
    row_spec = pl.BlockSpec((1, win, width), lambda i: (i, 0, 0))
    return pl.pallas_call(
        functools.partial(middle_kernel, plans, out_plans, reps, rows, outs, wins),
        grid=(wins,),
        in_specs=[
            SCALARS,
            seq_spec,
            same((win, width)),
            row_spec,
            seq_spec,
            same(norms.shape),
            same(moments.shape),
        ]
        + [same(piece.shape) for piece in w],
        out_specs=[whole(sent), row_spec, row_spec, whole(norms.shape)]
        + [whole(shape) for shape in grad_shapes],
        out_shape=[
            jax.ShapeDtypeStruct(sent, BF),
            jax.ShapeDtypeStruct((wins, win, width), F32),
            jax.ShapeDtypeStruct((wins, win, width), BF),
            jax.ShapeDtypeStruct(norms.shape, F32),
        ]
        + [jax.ShapeDtypeStruct(shape, BF) for shape in grad_shapes],
        scratch_shapes=[
            pltpu.VMEM((win, hidden), BF),
            pltpu.VMEM((win, hidden), BF),
            pltpu.VMEM((win, hidden), BF),
            pltpu.VMEM((tiles, width, tile), BF),
            pltpu.VMEM((tiles, width, tile), F32),
        ],
        compiler_params=PARAMS,
        cost_estimate=takes(27),
        name="middle",
    )(me, x, positions, mixed, cot, norms, moments, *w)


def attend_back_kernel(
    plans,
    out_plans,
    reps,
    rows,
    me_ref,
    x_ref,
    pos_ref,
    ids_row,
    ids_col,
    qkv_ref,
    lse_ref,
    gmixed_ref,
    mid_ref,
    dnorm_ref,
    *refs,
):
    count = 1 if plans is None else len(plans)
    pieces = refs[:count]
    ginput_ref = refs[count]
    refs = refs[count + 1 :]
    count = 1 if out_plans is None else 2
    grads = refs[:count]
    bias, gproj, w_ref, acc = refs[count:]
    step = pl.program_id(0)
    last = pl.num_programs(0) - 1
    win, width = pos_ref.shape
    dim = width // H
    tiles, _, tile = w_ref.shape
    factor = dim**-0.5
    half = win // 2

    @pl.when(step == 0)
    def _():
        place_blocks(me_ref, pieces, w_ref, plans, reps)
        acc[...] = jnp.zeros_like(acc)

    key = lax.broadcasted_iota(jnp.int32, (win, win), 0)
    query_at = lax.broadcasted_iota(jnp.int32, (win, win), 1)
    allowed = (ids_col[0] == ids_row[0]) & (query_at >= key)
    bias[...] = jnp.where(allowed, 0.0, MASKED)
    for pair in range(H // 2):
        packed = []
        for h in (2 * pair, 2 * pair + 1):
            base = 3 * dim * h
            query = qkv_ref[0, :, base : base + dim] * factor
            keys = qkv_ref[0, :, base + dim : base + 2 * dim]
            values = qkv_ref[0, :, base + 2 * dim : base + 3 * dim]
            gout = gmixed_ref[0, :, h * dim : (h + 1) * dim]
            lse = lse_ref[0, h : h + 1, :]
            parts = []
            for lo, first in ((half, half), (0, 0)):
                scores = nt(keys[lo : lo + half], query[first:]) + bias[lo : lo + half, first:]
                probs = jnp.exp(scores - lse[:, first:])
                gprobs = nt(values[lo : lo + half], gout[first:])
                inner = jnp.sum(probs * gprobs, axis=0, keepdims=True)
                parts.append((probs, gprobs, inner))
            (probs_b, gprobs_b, inner_b), (probs_a, gprobs_a, inner_a) = parts
            inner_late = inner_a[:, half:] + inner_b
            inner_full = jnp.concatenate([inner_a[:, :half], inner_late], axis=1)
            gs_a = (probs_a * (gprobs_a - inner_full)).astype(BF)
            gs_b = (probs_b * (gprobs_b - inner_late)).astype(BF)
            gvalues = jnp.concatenate(
                [nn(probs_a.astype(BF), gout), nn(probs_b.astype(BF), gout[half:])], axis=0
            )
            gkeys = jnp.concatenate([nn(gs_a, query), nn(gs_b, query[half:])], axis=0)
            gq_a = tn(gs_a, keys[:half])
            gq_b = tn(gs_b, keys[half:])
            gquery = jnp.concatenate([gq_a[:half], gq_a[half:] + gq_b], axis=0) * factor
            packed += [gquery.astype(BF), gkeys.astype(BF), gvalues.astype(BF)]
        gproj[:, pair * 6 * dim : (pair + 1) * 6 * dim] = jnp.concatenate(packed, axis=1)
    hidden = x_ref[...].reshape(win, width).astype(F32) + pos_ref[...]
    low_t = hidden.astype(BF).T
    total = mid_ref[0]
    for t in range(tiles):
        part = gproj[:, t * tile : (t + 1) * tile]
        acc[t] += nn(low_t, part)
        total += nt(part, w_ref[t])
    ginput_ref[...] = total.astype(BF).reshape(ginput_ref.shape)
    for j in range(width // tile):
        acc[tiles + j] += total[:, j * tile : (j + 1) * tile]

    @pl.when(step == last)
    def _():
        if out_plans is not None:
            small = jnp.concatenate(
                [dnorm_ref[:, j * tile : (j + 1) * tile] for j in range(width // tile)], axis=0
            )
            small = jnp.concatenate([small, jnp.zeros((rows - small.shape[0], tile), F32)], axis=0)
            for b in range(win // rows):
                acc[acc.shape[0] - 1, b * rows : (b + 1) * rows] = small
        take_blocks(me_ref, acc, grads, out_plans, reps, rows)


def attend_backward(
    me, x, positions, ids, qkv, lse, gmixed, mid, dnorm, w, plans, out_plans, grad_shapes, tiles, tile, reps, rows
):
    group, wins, span, width = x.shape
    win = group * span
    seq_spec = pl.BlockSpec((group, 1, span, width), lambda i: (0, i, 0, 0))
    row_spec = pl.BlockSpec((1, win, width), lambda i: (i, 0, 0))
    return pl.pallas_call(
        functools.partial(attend_back_kernel, plans, out_plans, reps, rows),
        grid=(wins,),
        in_specs=[
            SCALARS,
            seq_spec,
            same((win, width)),
            pl.BlockSpec((1, 1, win), lambda i: (i, 0, 0)),
            pl.BlockSpec((1, win, 1), lambda i: (i, 0, 0)),
            pl.BlockSpec((1, win, 3 * width), lambda i: (i, 0, 0)),
            pl.BlockSpec((1, H, win), lambda i: (i, 0, 0)),
            row_spec,
            row_spec,
            same(dnorm.shape),
        ]
        + [same(piece.shape) for piece in w],
        out_specs=[seq_spec] + [whole(shape) for shape in grad_shapes],
        out_shape=[jax.ShapeDtypeStruct(x.shape, BF)]
        + [jax.ShapeDtypeStruct(shape, BF) for shape in grad_shapes],
        scratch_shapes=[
            pltpu.VMEM((win, win), F32),
            pltpu.VMEM((win, 3 * width), BF),
            pltpu.VMEM((tiles, width, tile), BF),
            pltpu.VMEM((tiles + width // tile + 1, width, tile), F32),
        ],
        compiler_params=PARAMS,
        cost_estimate=takes(22),
        name="attend_backward",
    )(me, x, positions, ids[:, None, :], ids[:, :, None], qkv, lse, gmixed, mid, dnorm, *w)


def right_kernel(rows_ref, right_ref, out_ref):
    seqs, _, _ = out_ref.shape
    slots, _, tile = rows_ref.shape
    cols = tile // seqs
    for s in range(slots):
        turned = nn(rows_ref[s], right_ref[s]).astype(BF)
        for j in range(seqs):
            out_ref[j, :, s * cols : (s + 1) * cols] = turned[:, j * cols : (j + 1) * cols]


def right_turn(rows, right, seqs):
    slots, rows_dev, tile = rows.shape
    return pl.pallas_call(
        right_kernel,
        out_shape=jax.ShapeDtypeStruct((seqs, rows_dev, slots * tile // seqs), BF),
        compiler_params=PARAMS,
        cost_estimate=takes(3),
        name="right_turn",
    )(rows, right)


def left_kernel(x_ref, moments_ref, left_ref, left_t_ref, out_ref):
    seqs, rows_dev, wide = x_ref.shape
    slots, width, _ = left_ref.shape
    cols = wide // slots
    x = x_ref[...].reshape(width, wide)
    at = moments_ref.shape[2] - 2 * wide
    moments = moments_ref[:, :, at:].reshape(width, 2 * wide).astype(F32)
    turned = [nn(left_t_ref[s], x[:, s * cols : (s + 1) * cols]) for s in range(slots)]
    turned = jnp.concatenate(turned, axis=1)
    direction = adam_step(turned, moments[:, :wide], moments[:, wide:])[2].astype(BF)
    change = [nn(left_ref[s], direction[:, s * cols : (s + 1) * cols]) for s in range(slots)]
    out = jnp.concatenate(change + [turned], axis=1).astype(BF)
    out_ref[...] = out.reshape(out_ref.shape)


def left_turns(x, moments, left, left_t):
    seqs, rows_dev, wide = x.shape
    return pl.pallas_call(
        left_kernel,
        out_shape=jax.ShapeDtypeStruct((seqs, rows_dev, 2 * wide), BF),
        compiler_params=PARAMS,
        cost_estimate=takes(3),
        name="left_turns",
    )(x, moments, left, left_t)


def last_kernel(back_ref, right_ref, w_ref, one_ref, two_ref, new_one, new_two, new_w):
    seqs, rows_dev, _ = back_ref.shape
    slots, _, tile = w_ref.shape
    cols = tile // seqs
    for s in range(slots):

        def columns(first):
            return jnp.concatenate(
                [back_ref[j, :, first + s * cols : first + (s + 1) * cols] for j in range(seqs)], axis=1
            )

        change = nt(columns(0), right_ref[s])
        turned = columns(slots * cols).astype(F32)
        new_one[s], new_two[s], _ = adam_step(turned, one_ref[s], two_ref[s])
        old = w_ref[s]
        new_w[s] = old - LEARN * (change + DECAY * old)


def last_turn(back, right, weights, one, two):
    shape = jax.ShapeDtypeStruct(weights.shape, F32)
    return pl.pallas_call(
        last_kernel,
        out_shape=[shape, shape, shape],
        compiler_params=PARAMS,
        cost_estimate=takes(3),
        name="last_turn",
    )(back, right, weights, one, two)


def columns_kernel(one_ref, two_ref, out_ref):
    seqs = out_ref.shape[0]
    slots, _, tile = one_ref.shape
    cols = tile // seqs
    for first, ref in ((0, one_ref), (slots, two_ref)):
        for s in range(slots):
            values = ref[s].astype(BF)
            for j in range(seqs):
                at = (first + s) * cols
                out_ref[j, :, at : at + cols] = values[:, j * cols : (j + 1) * cols]


def moment_columns(one, two, seqs):
    slots, rows_dev, tile = one.shape
    return pl.pallas_call(
        columns_kernel,
        out_shape=jax.ShapeDtypeStruct((seqs, rows_dev, 2 * slots * tile // seqs), BF),
        compiler_params=PARAMS,
        cost_estimate=takes(3000),
        name="moment_columns",
    )(one, two)


def bases_kernel(left_ref, right_ref, low_left, low_left_t, low_right):
    left = left_ref[0].astype(BF)
    low_left[0] = left
    low_left_t[0] = left.T
    low_right[0] = right_ref[0].astype(BF)


def low_bases(left, right):
    slots, width, _ = left.shape
    tile = right.shape[1]
    big = pl.BlockSpec((1, width, width), lambda i: (i, 0, 0))
    little = pl.BlockSpec((1, tile, tile), lambda i: (i, 0, 0))
    return pl.pallas_call(
        bases_kernel,
        grid=(slots,),
        in_specs=[big, little],
        out_specs=[big, big, little],
        out_shape=[
            jax.ShapeDtypeStruct(left.shape, BF),
            jax.ShapeDtypeStruct(left.shape, BF),
            jax.ShapeDtypeStruct(right.shape, BF),
        ],
        compiler_params=PARAMS,
        cost_estimate=takes(3),
        name="low_bases",
    )(left, right)


def swap(x, axis, bit):
    size = lax.axis_size(axis)
    return lax.ppermute(x, axis, [(i, i ^ bit) for i in range(size)])


def exchange(x, axis, group):
    size = lax.axis_size(axis)
    groups = None
    if group != size:
        groups = [[base + i for i in range(group)] for base in range(0, size, group)]
    return lax.all_to_all(x, axis, 0, 0, axis_index_groups=groups, tiled=True)


def after(x, *others):
    return lax.optimization_barrier((x,) + others)[0]


def powers(first, size):
    bits = []
    while first < size:
        bits.append(first)
        first *= 2
    return bits


def gather(block, order):
    own = block[None]
    for axis, bit in order[:-1]:
        own = jnp.concatenate([own, swap(own, axis, bit)], axis=0)
    return own, swap(own, *order[-1])


def add(a, b, *others):
    if others:
        b = after(b, *others)
    return (a.astype(F32) + b.astype(F32)).astype(BF)


def double(buf, axis, bit, *others):
    got = swap(buf, axis, bit)
    if others:
        got = after(got, *others)
    return jnp.concatenate([buf, got], axis=0)


def halve(buf, axis, bit, *others):
    cut = buf.shape[0] // 2
    return add(buf[:cut], swap(buf[cut:], axis, bit), *others)


def body(
    inputs,
    cotangent,
    segments,
    owners,
    weights,
    left_bases,
    right_bases,
    moment_one,
    moment_two,
    norm_params,
    norm_one,
    norm_two,
    positions,
    pos_one,
    pos_two,
):
    seqs = lax.axis_size("seq")
    reps = lax.axis_size("rep")
    me_s = lax.axis_index("seq")
    me_r = lax.axis_index("rep")
    me = jnp.stack([me_s, me_r]).astype(jnp.int32)
    seq_local, span, width = inputs.shape
    rows_dev, slots, tile = weights.shape
    tiles = owners.shape[0]
    rows = rows_dev // reps
    group = WIN // span
    place = me_s % group
    wins = seq_local // group
    aligned = rows % 16 == 0
    blocks = seqs * reps
    seq_bits = [("seq", b) for b in powers(1, seqs)[::-1]]
    far_bits = [("rep", b) for b in powers(2, reps)]
    core_bit = [("rep", 1)]

    low_w = weights.astype(BF).transpose(1, 0, 2).reshape(slots, reps, rows, tile).transpose(1, 0, 2, 3)
    near = [lax.dynamic_index_in_dim(low_w, me_r, 0, keepdims=False)]
    for k in range(1, reps):
        near.append(swap(lax.dynamic_index_in_dim(low_w, me_r ^ k, 0, keepdims=False), "rep", k))
    near = jnp.concatenate(near, axis=0)
    near = jnp.take(near, ((owners // slots) ^ me_r) * slots + owners % slots, axis=0)
    ids = segments.reshape(-1)
    id_tiles = -(-2 * ids.shape[0] // (rows * tile))
    ids = jnp.concatenate([ids // 64, ids % 64]).astype(BF)
    ids = jnp.pad(ids, (0, id_tiles * rows * tile - ids.shape[0])).reshape(id_tiles, rows, tile)

    qkv_tiles = 3 * width // tile
    rest_tiles = tiles - qkv_tiles
    qkv_at, rest_at = qkv_tiles // 2, rest_tiles // 2
    split = qkv_at + id_tiles
    by_slot = [values.transpose(1, 0, 2) for values in (weights, moment_one, moment_two)]
    rest = near[qkv_tiles:][None]
    near = jnp.concatenate([near[:qkv_at], ids, near[qkv_at:qkv_tiles]], axis=0)[None]
    moments = moment_columns(after(by_slot[1], near), by_slot[2], seqs)
    for i, step in enumerate(seq_bits[:-1]):
        near = double(near, *step, *([moments] if i == 0 else []))
        rest = double(after(rest, moments) if i == 0 else rest, *step, near)
        if i == 0:
            x = after(inputs, near)
    x = exchange(x, "seq", group)
    cot = exchange(after(cotangent, x), "seq", group).reshape(group, wins, span, width)
    x = x.reshape(group, wins, span, width)

    def table_of(masks):
        table = np.zeros(blocks, np.int32)
        for k, (s, t) in enumerate(masks):
            table[s * reps + t] = k
        return jnp.asarray(table)

    orders = [seq_bits[-1:] + far_bits, far_bits + seq_bits[-1:]]

    def pieces_of(bufs, ranges):
        pieces, plans = [], []
        for buf, order, (first, last) in zip(bufs, orders, ranges):
            masks = gather_masks(seq_bits[:-1] + order)
            pieces += [buf, swap(buf, *core_bit[0])]
            plans += [(first, last, masks), (first, last, beyond(masks))]
        return settle(pieces, plans)

    def settle(pieces, plans):
        if aligned:
            return pieces, plans
        at = jnp.arange(blocks)
        full = []
        for i in range(0, len(pieces), 2):
            count = plans[i][1] - plans[i][0]
            table = table_of(plans[i][2] + plans[i + 1][2])
            both = jnp.concatenate([pieces[i][:, :count], pieces[i + 1][:, :count]], axis=0)
            both = jnp.take(both, table[((at // reps) ^ me_s) * reps + ((at % reps) ^ me_r)], axis=0)
            full.append(both.transpose(1, 0, 2, 3).reshape(count, blocks * rows, tile))
        return [jnp.concatenate(full, axis=0)], None

    bufs = [near[:, :split], near[:, split:]]
    bufs = [double(buf, *order[0]) for buf, order in zip(bufs, orders)]
    ids = bufs[0][:, qkv_at:]
    rest = after(rest, *bufs)
    for i in range(1, len(orders[0])):
        bufs = [double(buf, *order[i]) for buf, order in zip(bufs, orders)]
    w_qkv, qkv_plans = pieces_of(bufs, [(0, qkv_at), (qkv_at, qkv_tiles)])
    rest = [rest[:, :rest_at], rest[:, rest_at:]]
    rest = [double(buf, *order[0], *bufs) for buf, order in zip(rest, orders)]

    ids = ids.reshape(seqs, -1)[:, : 2 * seq_local * span].astype(jnp.int32)
    ids = (ids[:, : seq_local * span] * 64 + ids[:, seq_local * span :]).reshape(seqs, seq_local, span)
    spots = [0] * seqs
    for k, (s, _) in enumerate(gather_masks(seq_bits[:-1] + seq_bits[-1:])):
        spots[s] = k
    ids = jnp.take(ids, jnp.asarray(spots[:group])[jnp.arange(group) ^ place], axis=0)
    ids = lax.dynamic_slice_in_dim(ids, place * wins, wins, 1)
    ids = ids.transpose(1, 0, 2).reshape(wins, WIN)

    def scatter_plans(parts):
        count = parts[-1][1]
        if not aligned:
            return None, [(count, blocks * rows, tile)]
        own = [(first, last, gather_masks(order[:0:-1])) for first, last, order in parts]
        other = [(first, last, beyond(masks)) for first, last, masks in own]
        shape = (count * blocks // 2, rows, tile)
        return [own, other], [shape, shape]

    def scatter_tiles(grads, parts, *others):
        if not aligned:
            plain = grads[0].reshape(-1, blocks, rows, tile).transpose(1, 0, 2, 3)
            own, other = [], []
            for first, last, order in parts:
                masks = gather_masks(order[:0:-1])
                for target, some in ((own, masks), (other, beyond(masks))):
                    spots = np.array([s * reps + t for s, t in some])
                    at = ((spots // reps) ^ me_s) * reps + ((spots % reps) ^ me_r)
                    target.append(jnp.take(plain[:, first:last], at, axis=0).reshape(-1, rows, tile))
            grads = [jnp.concatenate(own, axis=0), jnp.concatenate(other, axis=0)]
        return add(grads[0], swap(grads[1], *core_bit[0]), *others)

    def cut_parts(buf, parts):
        out, at = [], 0
        for first, last, _ in parts:
            size = (last - first) * blocks // 2
            out.append(buf[at : at + size])
            at += size
        return out

    def join(bufs, parts):
        entries = 2 ** len(seq_bits[:-1])
        return jnp.concatenate([buf.reshape(entries, -1, rows, tile) for buf in bufs], axis=1)

    zyxc = seq_bits + far_bits + core_bit
    zxyc = seq_bits[:-1] + far_bits + seq_bits[-1:] + core_bit
    ids = after(ids, *rest)
    ahead = attend_forward(me, x, positions, ids, w_qkv, qkv_plans, qkv_tiles, tile, reps)
    for i in range(1, len(orders[0])):
        got = [swap(buf, *order[i]) for buf, order in zip(rest, orders)]
        qkv, mixed, lse, *got = lax.optimization_barrier((*ahead, *got))
        rest = [jnp.concatenate([buf, part], axis=0) for buf, part in zip(rest, got)]
    w_rest, rest_plans = pieces_of(rest, [(0, rest_at), (rest_at, rest_tiles)])
    rest_parts = [(0, rest_at, zyxc[::-1]), (rest_at, rest_tiles, zxyc[::-1])]
    out_plans, shapes = scatter_plans(rest_parts)
    result, mid, gmixed, d_norm, *d_rest = middle(
        me, x, positions, mixed, cot, norm_params, moments, group == seqs, w_rest, rest_plans, out_plans, shapes, rest_tiles, tile, reps, rows
    )
    result = exchange(result, "seq", group)
    rest = cut_parts(scatter_tiles(d_rest, rest_parts), rest_parts)
    gmixed = after(gmixed, *rest)
    steps = [[order[1 + i] for _, _, order in rest_parts] for i in range(len(orders[0]))]
    cuts = [buf.shape[0] // 2 for buf in rest]
    got = [swap(buf[cut:], *step) for buf, cut, step in zip(rest, cuts, steps[0])]

    qkv_total = qkv_tiles + width // tile + 1
    qkv_parts = [(0, 4, zyxc[::-1]), (4, qkv_total, zxyc[::-1])]
    out_plans, shapes = scatter_plans(qkv_parts)
    g_input, *d_qkv = attend_backward(
        me, x, positions, ids, qkv, lse, gmixed, mid, d_norm,
        w_qkv, qkv_plans, out_plans, shapes, qkv_tiles, tile, reps, rows,
    )
    count = len(d_qkv)
    g_input, *some = lax.optimization_barrier((g_input, *d_qkv, *got, result))
    d_qkv, got, result = some[:count], some[count:-1], some[-1]
    if group == seqs:
        moments = result
    else:
        moments = lax.all_to_all(after(moments, result), "seq", 0, 0, tiled=True)
    result = result[:, :, : wins * width].reshape(group, span, wins, width)
    result = result.transpose(0, 2, 1, 3).reshape(seq_local, span, width)
    rest = [add(buf[:cut], part) for buf, cut, part in zip(rest, cuts, got)]

    qkv_buf = scatter_tiles(d_qkv, qkv_parts)
    mine = cut_parts(qkv_buf, qkv_parts)
    low_left, low_left_t, low_right = low_bases(after(left_bases, qkv_buf), right_bases)
    mine = [halve(buf, *step, low_left) for buf, step in zip(mine, steps[0])]
    for some in steps[1:]:
        rest = [halve(buf, *step, *mine) for buf, step in zip(rest, some)]
        mine = [halve(buf, *step, *rest) for buf, step in zip(mine, some)]
    rest, mine = join(rest, rest_parts), join(mine, qkv_parts)
    for step in seq_bits[-2::-1]:
        rest = halve(rest, *step, mine)
        mine = halve(mine, *step, rest)
    rest, mine = rest[0], mine[0]
    g_input = exchange(g_input.reshape(seq_local, span, width), "seq", group)

    small = mine[qkv_tiles:]
    grad_norms = small[-1, : 4 * width // tile].astype(F32)
    sums = jnp.concatenate([mine[:qkv_tiles], rest], axis=0)
    tile_of = jnp.sum(
        jnp.where(owners[None, :] == jnp.arange(tiles)[:, None], jnp.arange(tiles)[None, :], 0), axis=1
    )
    sums = jnp.take(sums, tile_of, axis=0).reshape(reps, slots, rows, tile)
    small = small[: width // tile]
    near = []
    for k in range(reps):
        part = lax.dynamic_index_in_dim(sums, me_r ^ k, 0, keepdims=False)
        part = jnp.concatenate([part, small], axis=0)
        near.append(swap(part, "rep", k) if k else part)
    sums = jnp.take(jnp.stack(near), jnp.arange(reps) ^ me_r, axis=0)
    sums = sums.transpose(1, 0, 2, 3).reshape(-1, rows_dev, tile)
    small = sums[slots:]
    sums = sums[:slots]

    turned = right_turn(sums, low_right, seqs)
    small = after(small, turned)
    turned = lax.all_to_all(after(turned, g_input), "seq", 0, 0, tiled=True)
    back = left_turns(turned, moments, low_left, low_left_t)
    news = last_turn(lax.all_to_all(back, "seq", 0, 0, tiled=True), low_right, *by_slot)
    first_new, second_new, new_weights = [values.transpose(1, 0, 2) for values in news]

    own = small[None]
    for step in seq_bits:
        own = double(own, *step, back)
    masks = gather_masks(seq_bits)
    table = np.zeros(seqs, np.int32)
    for k, (i, _) in enumerate(masks):
        table[i] = k
    grad_pos = jnp.take(own, jnp.asarray(table)[jnp.arange(seqs) ^ me_s], axis=0)
    grad_pos = grad_pos.transpose(0, 2, 1, 3).reshape(WIN, width).astype(F32)
    if aligned:
        grad_norms = grad_norms.reshape(width // tile, 4, tile).transpose(1, 0, 2).reshape(4, width)
    else:
        grad_norms = lax.psum(d_norm, ("seq", "rep"))
    norm_first, norm_second, norm_dir = adam_step(grad_norms, norm_one, norm_two)
    pos_first, pos_second, pos_dir = adam_step(grad_pos, pos_one, pos_two)
    return (
        result,
        after(g_input, back).astype(F32),
        first_new,
        second_new,
        new_weights,
        norm_first,
        norm_second,
        norm_params - LEARN_SMALL * norm_dir,
        pos_first,
        pos_second,
        positions - LEARN_SMALL * pos_dir,
    )


def solution(mesh):
    tokens = P("rep", "seq", None)
    slots = P("seq", "rep", None)
    bases = P("rep", None, None)
    return jax.shard_map(
        body,
        mesh=mesh,
        in_specs=(
            tokens,
            tokens,
            P("rep", "seq"),
            P(),
            slots,
            bases,
            bases,
            slots,
            slots,
            P(),
            P(),
            P(),
            P(),
            P(),
            P(),
        ),
        out_specs=(tokens, tokens, slots, slots, slots, P(), P(), P(), P(), P(), P()),
        check_vma=False,
    )
```

```python
import functools

import jax
import jax.numpy as jnp
import numpy as np
from jax import lax
from jax.experimental import pallas as pl
from jax.experimental.pallas import tpu as pltpu
from jax.sharding import PartitionSpec as P

H = 8
WIN = 512
STEP = 10

EPS_NORM = 1e-05
EPS_ADAM = 1e-08
BETA = 0.5
LEARN = 0.02
LEARN_SMALL = 0.2
DECAY = 0.01
MASKED = -1e30
QUERIES = 128

BF = jnp.bfloat16
F32 = jnp.float32
PARAMS = pltpu.CompilerParams(vmem_limit_bytes=58 * 1024 * 1024)
GELU_A = 0.7978845608028654
GELU_B = 0.044715


def nn(a, b):
    return lax.dot_general(a, b, (((1,), (0,)), ((), ())), preferred_element_type=F32)


def nt(a, b):
    return lax.dot_general(a, b, (((1,), (1,)), ((), ())), preferred_element_type=F32)


def tn(a, b):
    return lax.dot_general(a, b, (((0,), (0,)), ((), ())), preferred_element_type=F32)


def adam_step(gradient, first, second):
    first_new = BETA * first + (1.0 - BETA) * gradient
    second_new = BETA * second + (1.0 - BETA) * gradient * gradient
    fix = 1.0 - BETA**STEP
    direction = first_new / fix / (jnp.sqrt(second_new / fix) + EPS_ADAM)
    return (first_new, second_new, direction)


def row_norm(values):
    center = values - jnp.mean(values, axis=-1, keepdims=True)
    inverse = lax.rsqrt(jnp.mean(center * center, axis=-1, keepdims=True) + EPS_NORM)
    return center * inverse, inverse


def norm_pull(grad_rows, scaled, inverse, gain):
    scaled_grad = grad_rows * gain
    grad_input = inverse * (
        scaled_grad
        - jnp.mean(scaled_grad, axis=-1, keepdims=True)
        - scaled * jnp.mean(scaled_grad * scaled, axis=-1, keepdims=True)
    )
    grad_gain = jnp.sum(grad_rows * scaled, axis=0, keepdims=True)
    grad_shift = jnp.sum(grad_rows, axis=0, keepdims=True)
    return grad_input, grad_gain, grad_shift


def memory(mebibytes):
    return pltpu.CompilerParams(vmem_limit_bytes=mebibytes * 1024 * 1024)


def same(shape):
    return pl.BlockSpec(shape, lambda *_: (0,) * len(shape), pipeline_mode=pl.Buffered(1))


def whole(shape):
    return pl.BlockSpec(shape, lambda *_: (0,) * len(shape))


SCALARS = pl.BlockSpec(memory_space=pltpu.SMEM)


def takes(microseconds):
    return pl.CostEstimate(flops=int(microseconds * 1e6), bytes_accessed=0, transcendentals=0)


def gather_masks(order):
    masks = [(0, 0)]
    for axis, bit in order:
        step = (bit, 0) if axis == "seq" else (0, bit)
        masks = masks + [(s ^ step[0], t ^ step[1]) for s, t in masks]
    return tuple(masks)


def beyond(masks):
    return tuple((s, t ^ 1) for s, t in masks)


def block_at(me_ref, mask, reps, rows):
    block = (me_ref[0] ^ mask[0]) * reps + (me_ref[1] ^ mask[1])
    return pl.ds(pl.multiple_of(block * rows, rows), rows)


def place_blocks(me_ref, refs, target, plans, reps):
    if plans is None:
        target[...] = refs[0][...]
        return
    for ref, (first, last, masks) in zip(refs, plans):
        for k, mask in enumerate(masks):
            where = block_at(me_ref, mask, reps, ref.shape[2])
            target[first:last, where, :] = ref[k, : last - first]


def take_blocks(me_ref, source, outs, plans, reps, rows):
    if plans is None:
        outs[0][...] = source[...].astype(BF)
        return
    for out, parts in zip(outs, plans):
        at = 0
        for first, last, masks in parts:
            for mask in masks:
                where = block_at(me_ref, mask, reps, rows)
                out[at : at + last - first] = source[first:last, where, :].astype(BF)
                at += last - first


def attend_kernel(plans, reps, me_ref, x_ref, pos_ref, ids_row, ids_col, *refs):
    count = 1 if plans is None else len(plans)
    pieces = refs[:count]
    qkv_ref, mixed_ref, lse_ref, bias, w_ref = refs[count:]
    win, width = pos_ref.shape
    dim = width // H
    tile = w_ref.shape[2]


    @pl.when(pl.program_id(0) == 0)
    def _():
        place_blocks(me_ref, pieces, w_ref, plans, reps)

    hidden = x_ref[...].reshape(win, width).astype(F32) + pos_ref[...]
    low = hidden.astype(BF)
    for t in range(w_ref.shape[0]):
        qkv_ref[0, :, t * tile : (t + 1) * tile] = nn(low, w_ref[t]).astype(BF)
    row = lax.broadcasted_iota(jnp.int32, (win, win), 0)
    col = lax.broadcasted_iota(jnp.int32, (win, win), 1)
    allowed = (ids_col[0] == ids_row[0]) & (col >= row)
    bias[...] = jnp.where(allowed, 0.0, MASKED)
    ones = jnp.ones((win, dim), BF)
    blocks = [(lo, lo + QUERIES) for lo in range(0, win, QUERIES)]

    def score(h):
        base = 3 * dim * h
        query = qkv_ref[0, :, base : base + dim] * (dim**-0.5)
        keys = qkv_ref[0, :, base + dim : base + 2 * dim]
        return [nt(keys[:hi], query[lo:hi]) + bias[:hi, lo:hi] for lo, hi in blocks]

    def mix(h, scores):
        base = 3 * dim * h
        values = jnp.concatenate([qkv_ref[0, :, base + 2 * dim : base + 3 * dim], ones], axis=1)
        values = values.T[: dim + 16]
        parts, logs = [], []
        for some in scores:
            highest = jnp.max(some, axis=0, keepdims=True)
            both = nn(values[:, : some.shape[0]], jnp.exp(some - highest).astype(BF))
            total = both[dim : dim + 1]
            parts.append(both[:dim] / total)
            logs.append(highest + jnp.log(total))
        lse_ref[0, h : h + 1] = jnp.concatenate(logs, axis=1)
        return jnp.concatenate(parts, axis=1).astype(BF)

    outs = []
    scores = score(0)
    for h in range(H):
        later = score(h + 1) if h + 1 < H else None
        outs.append(mix(h, scores))
        scores = later
    mixed_ref[0] = jnp.concatenate(outs, axis=0).T


def attend_forward(me, x, positions, ids, w, plans, tiles, tile, reps):
    group, wins, span, width = x.shape
    win = group * span
    return pl.pallas_call(
        functools.partial(attend_kernel, plans, reps),
        grid=(wins,),
        in_specs=[
            SCALARS,
            pl.BlockSpec((group, 1, span, width), lambda i: (0, i, 0, 0)),
            same((win, width)),
            pl.BlockSpec((1, 1, win), lambda i: (i, 0, 0)),
            pl.BlockSpec((1, win, 1), lambda i: (i, 0, 0)),
        ]
        + [same(piece.shape) for piece in w],
        out_specs=[
            pl.BlockSpec((1, win, 3 * width), lambda i: (i, 0, 0)),
            pl.BlockSpec((1, win, width), lambda i: (i, 0, 0)),
            pl.BlockSpec((1, H, win), lambda i: (i, 0, 0)),
        ],
        out_shape=[
            jax.ShapeDtypeStruct((wins, win, 3 * width), BF),
            jax.ShapeDtypeStruct((wins, win, width), BF),
            jax.ShapeDtypeStruct((wins, H, win), F32),
        ],
        scratch_shapes=[pltpu.VMEM((win, win), F32), pltpu.VMEM((tiles, width, tile), BF)],
        compiler_params=memory(32),
        cost_estimate=takes(18),
        name="attend_forward",
    )(me, x, positions, ids[:, None, :], ids[:, :, None], *w)


def middle_kernel(
    plans, out_plans, reps, rows, outs, wins, me_ref, x_ref, pos_ref, mixed_ref, cot_ref, norm_ref, moments_ref, *refs
):
    count = 1 if plans is None else len(plans)
    pieces = refs[:count]
    refs = refs[count:]
    result_ref, mid_ref, gmixed_ref, dnorm_ref = refs[:4]
    count = 1 if out_plans is None else 2
    grads = refs[4 : 4 + count]
    act, slope, gpre, w_ref, acc = refs[4 + count :]
    step = pl.program_id(0)
    last = wins - 1
    win, width = pos_ref.shape
    tile = w_ref.shape[2]
    ups = (w_ref.shape[0] - outs) // 2
    blocks = ups // 2
    up, down = outs, outs + ups

    @pl.when(step == 0)
    def _():
        place_blocks(me_ref, pieces, w_ref, plans, reps)
        acc[...] = jnp.zeros_like(acc)
        dnorm_ref[...] = jnp.zeros_like(dnorm_ref)
        if result_ref.shape[2] > (last + 1) * width:
            result_ref[:, :, (last + 1) * width :] = moments_ref[...]

    mixed = mixed_ref[0]
    hidden = x_ref[...].reshape(win, width).astype(F32) + pos_ref[...]
    attn = jnp.concatenate([nn(mixed, w_ref[t]) for t in range(outs)], axis=1)
    scaled_one, inverse_one = row_norm(hidden + attn)
    normed = scaled_one * norm_ref[0:1] + norm_ref[1:2]
    low = normed.astype(BF)
    for t in range(ups):
        pre = nn(low, w_ref[up + t])
        square = pre * pre
        bent = jnp.tanh(GELU_A * pre * (1.0 + GELU_B * square))
        act[:, t * tile : (t + 1) * tile] = (0.5 * pre * (1.0 + bent)).astype(BF)
        slope[:, t * tile : (t + 1) * tile] = (
            0.5 * (1.0 + bent)
            + 0.5 * pre * (1.0 - bent * bent) * (GELU_A + 3.0 * GELU_A * GELU_B * square)
        ).astype(BF)
    branch = jnp.concatenate(
        [
            sum(nn(act[:, b * width : (b + 1) * width], w_ref[down + 2 * b + j]) for b in range(blocks))
            for j in range(2)
        ],
        axis=1,
    )
    scaled_two, inverse_two = row_norm(normed + branch)
    result = scaled_two * norm_ref[2:3] + norm_ref[3:4]
    result = result.astype(BF).reshape(*result_ref.shape[:2], width)
    for window in range(wins):

        @pl.when(step == window)
        def _():
            result_ref[:, :, window * width : (window + 1) * width] = result

    grad_resid, gain_two, shift_two = norm_pull(
        cot_ref[...].reshape(win, width).astype(F32), scaled_two, inverse_two, norm_ref[2:3]
    )
    gb = grad_resid.astype(BF)
    for b in range(blocks):
        cols = slice(b * width, (b + 1) * width)
        gact = nt(gb[:, :tile], w_ref[down + 2 * b]) + nt(gb[:, tile:], w_ref[down + 2 * b + 1])
        gpre[:, cols] = (gact * slope[:, cols].astype(F32)).astype(BF)
    grad_normed = grad_resid + sum(
        nt(gpre[:, t * tile : (t + 1) * tile], w_ref[up + t]) for t in range(ups)
    )
    grad_mid, gain_one, shift_one = norm_pull(grad_normed, scaled_one, inverse_one, norm_ref[0:1])
    mid_ref[0] = grad_mid
    ga = grad_mid.astype(BF)
    gmixed_ref[0] = sum(nt(ga[:, t * tile : (t + 1) * tile], w_ref[t]) for t in range(outs)).astype(BF)
    dnorm_ref[...] += jnp.concatenate([gain_one, shift_one, gain_two, shift_two], axis=0)
    for b in range(blocks):
        act_t = act[:, b * width : (b + 1) * width].T
        for j in range(2):
            acc[down + 2 * b + j] += nn(act_t, gb[:, j * tile : (j + 1) * tile])
    low_t = low.T
    for t in range(ups):
        acc[up + t] += nn(low_t, gpre[:, t * tile : (t + 1) * tile])
    mixed_t = mixed.T
    for t in range(outs):
        acc[t] += nn(mixed_t, ga[:, t * tile : (t + 1) * tile])

    @pl.when(step == last)
    def _():
        take_blocks(me_ref, acc, grads, out_plans, reps, rows)


def middle(me, x, positions, mixed, cot, norms, moments, together, w, plans, out_plans, grad_shapes, tiles, tile, reps, rows):
    group, wins, span, width = x.shape
    win = group * span
    outs = width // tile
    hidden = (tiles - outs) // 2 * tile
    sent = (group, span, wins * width + (moments.shape[2] if together else 0))
    seq_spec = pl.BlockSpec((group, 1, span, width), lambda i: (0, i, 0, 0))
    row_spec = pl.BlockSpec((1, win, width), lambda i: (i, 0, 0))
    return pl.pallas_call(
        functools.partial(middle_kernel, plans, out_plans, reps, rows, outs, wins),
        grid=(wins,),
        in_specs=[
            SCALARS,
            seq_spec,
            same((win, width)),
            row_spec,
            seq_spec,
            same(norms.shape),
            same(moments.shape),
        ]
        + [same(piece.shape) for piece in w],
        out_specs=[whole(sent), row_spec, row_spec, whole(norms.shape)]
        + [whole(shape) for shape in grad_shapes],
        out_shape=[
            jax.ShapeDtypeStruct(sent, BF),
            jax.ShapeDtypeStruct((wins, win, width), F32),
            jax.ShapeDtypeStruct((wins, win, width), BF),
            jax.ShapeDtypeStruct(norms.shape, F32),
        ]
        + [jax.ShapeDtypeStruct(shape, BF) for shape in grad_shapes],
        scratch_shapes=[
            pltpu.VMEM((win, hidden), BF),
            pltpu.VMEM((win, hidden), BF),
            pltpu.VMEM((win, hidden), BF),
            pltpu.VMEM((tiles, width, tile), BF),
            pltpu.VMEM((tiles, width, tile), F32),
        ],
        compiler_params=PARAMS,
        cost_estimate=takes(27),
        name="middle",
    )(me, x, positions, mixed, cot, norms, moments, *w)


def attend_back_kernel(
    plans,
    out_plans,
    reps,
    rows,
    behind,
    me_ref,
    x_ref,
    pos_ref,
    ids_row,
    ids_col,
    qkv_ref,
    lse_ref,
    gmixed_ref,
    mid_ref,
    dnorm_ref,
    *refs,
):
    count = 1 if plans is None else len(plans)
    pieces = refs[:count]
    ginput_ref = refs[count + behind]
    refs = refs[count + behind + 1 :]
    count = 1 if out_plans is None else 2
    grads = refs[:count]
    bias, gproj, w_ref, acc = refs[count:]
    step = pl.program_id(0)
    last = pl.num_programs(0) - 1
    win, width = pos_ref.shape
    dim = width // H
    tiles, _, tile = w_ref.shape
    factor = dim**-0.5
    half = win // 2

    @pl.when(step == 0)
    def _():
        place_blocks(me_ref, pieces, w_ref, plans, reps)
        acc[...] = jnp.zeros_like(acc)

    key = lax.broadcasted_iota(jnp.int32, (win, win), 0)
    query_at = lax.broadcasted_iota(jnp.int32, (win, win), 1)
    allowed = (ids_col[0] == ids_row[0]) & (query_at >= key)
    bias[...] = jnp.where(allowed, 0.0, MASKED)
    blocks = [(lo, lo + QUERIES) for lo in range(0, win, QUERIES)]

    def operands(h):
        base = 3 * dim * h
        query = qkv_ref[0, :, base : base + dim] * factor
        keys = qkv_ref[0, :, base + dim : base + 2 * dim]
        values = qkv_ref[0, :, base + 2 * dim : base + 3 * dim]
        return query, keys, values, gmixed_ref[0, :, h * dim : (h + 1) * dim]

    def score(h):
        query, keys, values, gout = operands(h)
        return [
            (nt(keys[:hi], query[lo:hi]) + bias[:hi, lo:hi], nt(values[:hi], gout[lo:hi])) for lo, hi in blocks
        ]

    def pull(h, scores):
        query, keys, _, gout = operands(h)
        keys_t = jnp.concatenate([keys, keys], axis=1).T[:dim]
        probs, gscores, gqueries = [], [], []
        for (lo, hi), (some, gprobs) in zip(blocks, scores):
            weights = jnp.exp(some - lse_ref[0, h : h + 1, lo:hi])
            inner = jnp.sum(weights * gprobs, axis=0, keepdims=True)
            gscore = (weights * (gprobs - inner)).astype(BF)
            probs.append(weights.astype(BF))
            gscores.append(gscore)
            gqueries.append(nn(keys_t[:, :hi], gscore))
        gkeys, gvalues = [], []
        for lo, hi in blocks:
            later = [i for i, (_, end) in enumerate(blocks) if end >= hi]
            gkeys.append(nn(jnp.concatenate([gscores[i][lo:hi] for i in later], axis=1), query[lo:]))
            gvalues.append(nn(jnp.concatenate([probs[i][lo:hi] for i in later], axis=1), gout[lo:]))
        gquery = jnp.concatenate(gqueries, axis=1) * factor
        return gquery.astype(BF), [jnp.concatenate(part, axis=0).astype(BF) for part in (gkeys, gvalues)]

    done = []
    scores = score(0)
    for h in range(H):
        later = score(h + 1) if h + 1 < H else None
        done.append(pull(h, scores))
        scores = later
        if h % 2:
            packed = jnp.concatenate([done[-2][0], done[-1][0]], axis=0).T
            parts = [packed[:, :dim], *done[-2][1], packed[:, dim:], *done[-1][1]]
            gproj[:, 3 * dim * (h - 1) : 3 * dim * (h + 1)] = jnp.concatenate(parts, axis=1)
    hidden = x_ref[...].reshape(win, width).astype(F32) + pos_ref[...]
    low_t = hidden.astype(BF).T
    total = mid_ref[0]
    for t in range(tiles):
        part = gproj[:, t * tile : (t + 1) * tile]
        acc[t] += nn(low_t, part)
        total += nt(part, w_ref[t])
    ginput_ref[...] = total.astype(BF).reshape(ginput_ref.shape)
    for j in range(width // tile):
        acc[tiles + j] += total[:, j * tile : (j + 1) * tile]

    @pl.when(step == last)
    def _():
        if out_plans is not None:
            small = jnp.concatenate(
                [dnorm_ref[:, j * tile : (j + 1) * tile] for j in range(width // tile)], axis=0
            )
            small = jnp.concatenate([small, jnp.zeros((rows - small.shape[0], tile), F32)], axis=0)
            for b in range(win // rows):
                acc[acc.shape[0] - 1, b * rows : (b + 1) * rows] = small
        take_blocks(me_ref, acc, grads, out_plans, reps, rows)


def attend_backward(
    me, x, positions, ids, qkv, lse, gmixed, mid, dnorm, behind, w, plans, out_plans, grad_shapes, tiles, tile, reps, rows
):
    group, wins, span, width = x.shape
    win = group * span
    seq_spec = pl.BlockSpec((group, 1, span, width), lambda i: (0, i, 0, 0))
    row_spec = pl.BlockSpec((1, win, width), lambda i: (i, 0, 0))
    return pl.pallas_call(
        functools.partial(attend_back_kernel, plans, out_plans, reps, rows, len(behind)),
        grid=(wins,),
        in_specs=[
            SCALARS,
            seq_spec,
            same((win, width)),
            pl.BlockSpec((1, 1, win), lambda i: (i, 0, 0)),
            pl.BlockSpec((1, win, 1), lambda i: (i, 0, 0)),
            pl.BlockSpec((1, win, 3 * width), lambda i: (i, 0, 0)),
            pl.BlockSpec((1, H, win), lambda i: (i, 0, 0)),
            row_spec,
            row_spec,
            same(dnorm.shape),
        ]
        + [same(piece.shape) for piece in w]
        + [pl.BlockSpec(memory_space=pl.ANY) for _ in behind],
        out_specs=[seq_spec] + [whole(shape) for shape in grad_shapes],
        out_shape=[jax.ShapeDtypeStruct(x.shape, BF)]
        + [jax.ShapeDtypeStruct(shape, BF) for shape in grad_shapes],
        scratch_shapes=[
            pltpu.VMEM((win, win), F32),
            pltpu.VMEM((win, 3 * width), BF),
            pltpu.VMEM((tiles, width, tile), BF),
            pltpu.VMEM((tiles + width // tile + 1, width, tile), F32),
        ],
        compiler_params=memory(36),
        cost_estimate=takes(22),
        name="attend_backward",
    )(me, x, positions, ids[:, None, :], ids[:, :, None], qkv, lse, gmixed, mid, dnorm, *w, *behind)


def right_kernel(rows_ref, right_ref, out_ref):
    seqs, _, _ = out_ref.shape
    slots, _, tile = rows_ref.shape
    cols = tile // seqs
    for s in range(slots):
        turned = nn(rows_ref[s], right_ref[s]).astype(BF)
        for j in range(seqs):
            out_ref[j, :, s * cols : (s + 1) * cols] = turned[:, j * cols : (j + 1) * cols]


def right_turn(rows, right, seqs):
    slots, rows_dev, tile = rows.shape
    return pl.pallas_call(
        right_kernel,
        out_shape=jax.ShapeDtypeStruct((seqs, rows_dev, slots * tile // seqs), BF),
        compiler_params=PARAMS,
        cost_estimate=takes(3),
        name="right_turn",
    )(rows, right)


def left_kernel(x_ref, moments_ref, left_ref, left_t_ref, out_ref):
    seqs, rows_dev, wide = x_ref.shape
    slots, width, _ = left_ref.shape
    cols = wide // slots
    x = x_ref[...].reshape(width, wide)
    at = moments_ref.shape[2] - 2 * wide
    moments = moments_ref[:, :, at:].reshape(width, 2 * wide).astype(F32)
    turned = [nn(left_t_ref[s], x[:, s * cols : (s + 1) * cols]) for s in range(slots)]
    turned = jnp.concatenate(turned, axis=1)
    direction = adam_step(turned, moments[:, :wide], moments[:, wide:])[2].astype(BF)
    change = [nn(left_ref[s], direction[:, s * cols : (s + 1) * cols]) for s in range(slots)]
    out = jnp.concatenate(change + [turned], axis=1).astype(BF)
    out_ref[...] = out.reshape(out_ref.shape)


def left_turns(x, moments, left, left_t):
    seqs, rows_dev, wide = x.shape
    return pl.pallas_call(
        left_kernel,
        out_shape=jax.ShapeDtypeStruct((seqs, rows_dev, 2 * wide), BF),
        compiler_params=PARAMS,
        cost_estimate=takes(3),
        name="left_turns",
    )(x, moments, left, left_t)


def last_kernel(back_ref, right_ref, w_ref, one_ref, two_ref, new_one, new_two, new_w):
    seqs, rows_dev, _ = back_ref.shape
    slots, _, tile = w_ref.shape
    cols = tile // seqs
    for s in range(slots):

        def columns(first):
            return jnp.concatenate(
                [back_ref[j, :, first + s * cols : first + (s + 1) * cols] for j in range(seqs)], axis=1
            )

        change = nt(columns(0), right_ref[s])
        turned = columns(slots * cols).astype(F32)
        new_one[s], new_two[s], _ = adam_step(turned, one_ref[s], two_ref[s])
        old = w_ref[s]
        new_w[s] = old - LEARN * (change + DECAY * old)


def last_turn(back, right, weights, one, two):
    shape = jax.ShapeDtypeStruct(weights.shape, F32)
    return pl.pallas_call(
        last_kernel,
        out_shape=[shape, shape, shape],
        compiler_params=PARAMS,
        cost_estimate=takes(3),
        name="last_turn",
    )(back, right, weights, one, two)


def columns_kernel(one_ref, two_ref, out_ref):
    seqs = out_ref.shape[0]
    slots, _, tile = one_ref.shape
    cols = tile // seqs
    for first, ref in ((0, one_ref), (slots, two_ref)):
        for s in range(slots):
            values = ref[s].astype(BF)
            for j in range(seqs):
                at = (first + s) * cols
                out_ref[j, :, at : at + cols] = values[:, j * cols : (j + 1) * cols]


def moment_columns(one, two, seqs):
    slots, rows_dev, tile = one.shape
    return pl.pallas_call(
        columns_kernel,
        out_shape=jax.ShapeDtypeStruct((seqs, rows_dev, 2 * slots * tile // seqs), BF),
        compiler_params=PARAMS,
        cost_estimate=takes(3000),
        name="moment_columns",
    )(one, two)


def bases_kernel(left_ref, right_ref, low_left, low_left_t, low_right):
    left = left_ref[0].astype(BF)
    low_left[0] = left
    low_left_t[0] = left.T
    low_right[0] = right_ref[0].astype(BF)


def low_bases(left, right):
    slots, width, _ = left.shape
    tile = right.shape[1]
    big = pl.BlockSpec((1, width, width), lambda i: (i, 0, 0))
    little = pl.BlockSpec((1, tile, tile), lambda i: (i, 0, 0))
    return pl.pallas_call(
        bases_kernel,
        grid=(slots,),
        in_specs=[big, little],
        out_specs=[big, big, little],
        out_shape=[
            jax.ShapeDtypeStruct(left.shape, BF),
            jax.ShapeDtypeStruct(left.shape, BF),
            jax.ShapeDtypeStruct(right.shape, BF),
        ],
        compiler_params=PARAMS,
        cost_estimate=takes(3),
        name="low_bases",
    )(left, right)


def swap(x, axis, bit):
    size = lax.axis_size(axis)
    return lax.ppermute(x, axis, [(i, i ^ bit) for i in range(size)])


def exchange(x, axis, group):
    size = lax.axis_size(axis)
    groups = None
    if group != size:
        groups = [[base + i for i in range(group)] for base in range(0, size, group)]
    return lax.all_to_all(x, axis, 0, 0, axis_index_groups=groups, tiled=True)


def after(x, *others):
    return lax.optimization_barrier((x,) + others)[0]


def powers(first, size):
    bits = []
    while first < size:
        bits.append(first)
        first *= 2
    return bits


def gather(block, order):
    own = block[None]
    for axis, bit in order[:-1]:
        own = jnp.concatenate([own, swap(own, axis, bit)], axis=0)
    return own, swap(own, *order[-1])


def add(a, b, *others):
    if others:
        b = after(b, *others)
    return (a.astype(F32) + b.astype(F32)).astype(BF)


def double(buf, axis, bit, *others):
    got = swap(buf, axis, bit)
    if others:
        got = after(got, *others)
    return jnp.concatenate([buf, got], axis=0)


def halve(buf, axis, bit, *others):
    cut = buf.shape[0] // 2
    return add(buf[:cut], swap(buf[cut:], axis, bit), *others)


def body(
    inputs,
    cotangent,
    segments,
    owners,
    weights,
    left_bases,
    right_bases,
    moment_one,
    moment_two,
    norm_params,
    norm_one,
    norm_two,
    positions,
    pos_one,
    pos_two,
):
    seqs = lax.axis_size("seq")
    reps = lax.axis_size("rep")
    me_s = lax.axis_index("seq")
    me_r = lax.axis_index("rep")
    me = jnp.stack([me_s, me_r]).astype(jnp.int32)
    seq_local, span, width = inputs.shape
    rows_dev, slots, tile = weights.shape
    tiles = owners.shape[0]
    rows = rows_dev // reps
    group = WIN // span
    place = me_s % group
    wins = seq_local // group
    aligned = rows % 16 == 0
    blocks = seqs * reps
    seq_bits = [("seq", b) for b in powers(1, seqs)[::-1]]
    far_bits = [("rep", b) for b in powers(2, reps)]
    core_bit = [("rep", 1)]

    low_w = weights.astype(BF).transpose(1, 0, 2).reshape(slots, reps, rows, tile).transpose(1, 0, 2, 3)
    near = [lax.dynamic_index_in_dim(low_w, me_r, 0, keepdims=False)]
    for k in range(1, reps):
        near.append(swap(lax.dynamic_index_in_dim(low_w, me_r ^ k, 0, keepdims=False), "rep", k))
    near = jnp.concatenate(near, axis=0)
    near = jnp.take(near, ((owners // slots) ^ me_r) * slots + owners % slots, axis=0)
    ids = segments.reshape(-1)
    id_tiles = -(-2 * ids.shape[0] // (rows * tile))
    ids = jnp.concatenate([ids // 64, ids % 64]).astype(BF)
    ids = jnp.pad(ids, (0, id_tiles * rows * tile - ids.shape[0])).reshape(id_tiles, rows, tile)

    qkv_tiles = 3 * width // tile
    rest_tiles = tiles - qkv_tiles
    qkv_at, rest_at = qkv_tiles // 2, rest_tiles // 2
    split = qkv_at + id_tiles
    by_slot = [values.transpose(1, 0, 2) for values in (weights, moment_one, moment_two)]
    rest = near[qkv_tiles:][None]
    near = jnp.concatenate([near[:qkv_at], ids, near[qkv_at:qkv_tiles]], axis=0)[None]
    moments = moment_columns(after(by_slot[1], near), by_slot[2], seqs)
    for i, step in enumerate(seq_bits[:-1]):
        near = double(near, *step, *([moments] if i == 0 else []))
        rest = double(after(rest, moments) if i == 0 else rest, *step, near)
        if i == 0:
            x = after(inputs, near)
    x = exchange(x, "seq", group)
    cot = exchange(after(cotangent, x), "seq", group).reshape(group, wins, span, width)
    x = x.reshape(group, wins, span, width)

    def table_of(masks):
        table = np.zeros(blocks, np.int32)
        for k, (s, t) in enumerate(masks):
            table[s * reps + t] = k
        return jnp.asarray(table)

    orders = [seq_bits[-1:] + far_bits, far_bits + seq_bits[-1:]]

    def pieces_of(bufs, ranges):
        pieces, plans = [], []
        for buf, order, (first, last) in zip(bufs, orders, ranges):
            masks = gather_masks(seq_bits[:-1] + order)
            pieces += [buf, swap(buf, *core_bit[0])]
            plans += [(first, last, masks), (first, last, beyond(masks))]
        return settle(pieces, plans)

    def settle(pieces, plans):
        if aligned:
            return pieces, plans
        at = jnp.arange(blocks)
        full = []
        for i in range(0, len(pieces), 2):
            count = plans[i][1] - plans[i][0]
            table = table_of(plans[i][2] + plans[i + 1][2])
            both = jnp.concatenate([pieces[i][:, :count], pieces[i + 1][:, :count]], axis=0)
            both = jnp.take(both, table[((at // reps) ^ me_s) * reps + ((at % reps) ^ me_r)], axis=0)
            full.append(both.transpose(1, 0, 2, 3).reshape(count, blocks * rows, tile))
        return [jnp.concatenate(full, axis=0)], None

    bufs = [near[:, :split], near[:, split:]]
    bufs = [double(buf, *order[0]) for buf, order in zip(bufs, orders)]
    ids = bufs[0][:, qkv_at:]
    rest = after(rest, *bufs)
    for i in range(1, len(orders[0])):
        bufs = [double(buf, *order[i]) for buf, order in zip(bufs, orders)]
    w_qkv, qkv_plans = pieces_of(bufs, [(0, qkv_at), (qkv_at, qkv_tiles)])
    rest = [rest[:, :rest_at], rest[:, rest_at:]]
    rest = [double(buf, *order[0], *bufs) for buf, order in zip(rest, orders)]

    ids = ids.reshape(seqs, -1)[:, : 2 * seq_local * span].astype(jnp.int32)
    ids = (ids[:, : seq_local * span] * 64 + ids[:, seq_local * span :]).reshape(seqs, seq_local, span)
    spots = [0] * seqs
    for k, (s, _) in enumerate(gather_masks(seq_bits[:-1] + seq_bits[-1:])):
        spots[s] = k
    ids = jnp.take(ids, jnp.asarray(spots[:group])[jnp.arange(group) ^ place], axis=0)
    ids = lax.dynamic_slice_in_dim(ids, place * wins, wins, 1)
    ids = ids.transpose(1, 0, 2).reshape(wins, WIN)

    def scatter_plans(parts):
        count = parts[-1][1]
        if not aligned:
            return None, [(count, blocks * rows, tile)]
        own = [(first, last, gather_masks(order[:0:-1])) for first, last, order in parts]
        other = [(first, last, beyond(masks)) for first, last, masks in own]
        shape = (count * blocks // 2, rows, tile)
        return [own, other], [shape, shape]

    def scatter_tiles(grads, parts, *others):
        if not aligned:
            plain = grads[0].reshape(-1, blocks, rows, tile).transpose(1, 0, 2, 3)
            own, other = [], []
            for first, last, order in parts:
                masks = gather_masks(order[:0:-1])
                for target, some in ((own, masks), (other, beyond(masks))):
                    spots = np.array([s * reps + t for s, t in some])
                    at = ((spots // reps) ^ me_s) * reps + ((spots % reps) ^ me_r)
                    target.append(jnp.take(plain[:, first:last], at, axis=0).reshape(-1, rows, tile))
            grads = [jnp.concatenate(own, axis=0), jnp.concatenate(other, axis=0)]
        return add(grads[0], swap(grads[1], *core_bit[0]), *others)

    def cut_parts(buf, parts):
        out, at = [], 0
        for first, last, _ in parts:
            size = (last - first) * blocks // 2
            out.append(buf[at : at + size])
            at += size
        return out

    def join(bufs, parts):
        entries = 2 ** len(seq_bits[:-1])
        return jnp.concatenate([buf.reshape(entries, -1, rows, tile) for buf in bufs], axis=1)

    zyxc = seq_bits + far_bits + core_bit
    zxyc = seq_bits[:-1] + far_bits + seq_bits[-1:] + core_bit
    ids = after(ids, *rest)
    ahead = attend_forward(me, x, positions, ids, w_qkv, qkv_plans, qkv_tiles, tile, reps)
    for i in range(1, len(orders[0])):
        got = [swap(buf, *order[i]) for buf, order in zip(rest, orders)]
        qkv, mixed, lse, *got = lax.optimization_barrier((*ahead, *got))
        rest = [jnp.concatenate([buf, part], axis=0) for buf, part in zip(rest, got)]
    w_rest, rest_plans = pieces_of(rest, [(0, rest_at), (rest_at, rest_tiles)])
    rest_parts = [(0, rest_at, zyxc[::-1]), (rest_at, rest_tiles, zxyc[::-1])]
    out_plans, shapes = scatter_plans(rest_parts)
    result, mid, gmixed, d_norm, *d_rest = middle(
        me, x, positions, mixed, cot, norm_params, moments, group == seqs, w_rest, rest_plans, out_plans, shapes, rest_tiles, tile, reps, rows
    )
    result = exchange(result, "seq", group)
    rest = cut_parts(scatter_tiles(d_rest, rest_parts), rest_parts)
    steps = [[order[1 + i] for _, _, order in rest_parts] for i in range(len(orders[0]))]
    cuts = [buf.shape[0] // 2 for buf in rest]
    got = [swap(buf[cut:], *step) for buf, cut, step in zip(rest, cuts, steps[0])]

    qkv_total = qkv_tiles + width // tile + 1
    qkv_parts = [(0, 4, zyxc[::-1]), (4, qkv_total, zxyc[::-1])]
    out_plans, shapes = scatter_plans(qkv_parts)
    g_input, *d_qkv = attend_backward(
        me, x, positions, ids, qkv, lse, gmixed, mid, d_norm, rest,
        w_qkv, qkv_plans, out_plans, shapes, qkv_tiles, tile, reps, rows,
    )
    count = len(d_qkv)
    g_input, *some = lax.optimization_barrier((g_input, *d_qkv, *got))
    d_qkv, got = some[:count], some[count:]
    g_input = after(g_input, result)
    if group == seqs:
        moments = result
    else:
        moments = lax.all_to_all(after(moments, result), "seq", 0, 0, tiled=True)
    result = result[:, :, : wins * width].reshape(group, span, wins, width)
    result = result.transpose(0, 2, 1, 3).reshape(seq_local, span, width)
    rest = [add(buf[:cut], part) for buf, cut, part in zip(rest, cuts, got)]

    qkv_buf = scatter_tiles(d_qkv, qkv_parts)
    mine = cut_parts(qkv_buf, qkv_parts)
    low_left, low_left_t, low_right = low_bases(after(left_bases, qkv_buf), right_bases)
    mine = [halve(buf, *step, low_left) for buf, step in zip(mine, steps[0])]
    for some in steps[1:]:
        rest = [halve(buf, *step, *mine) for buf, step in zip(rest, some)]
        mine = [halve(buf, *step, *rest) for buf, step in zip(mine, some)]
    rest, mine = join(rest, rest_parts), join(mine, qkv_parts)
    for step in seq_bits[-2::-1]:
        rest = halve(rest, *step, mine)
        mine = halve(mine, *step, rest)
    rest, mine = rest[0], mine[0]
    g_input = exchange(g_input.reshape(seq_local, span, width), "seq", group)

    small = mine[qkv_tiles:]
    grad_norms = small[-1, : 4 * width // tile].astype(F32)
    sums = jnp.concatenate([mine[:qkv_tiles], rest], axis=0)
    tile_of = jnp.sum(
        jnp.where(owners[None, :] == jnp.arange(tiles)[:, None], jnp.arange(tiles)[None, :], 0), axis=1
    )
    sums = jnp.take(sums, tile_of, axis=0).reshape(reps, slots, rows, tile)
    small = small[: width // tile]
    near = []
    for k in range(reps):
        part = lax.dynamic_index_in_dim(sums, me_r ^ k, 0, keepdims=False)
        part = jnp.concatenate([part, small], axis=0)
        near.append(swap(part, "rep", k) if k else part)
    sums = jnp.take(jnp.stack(near), jnp.arange(reps) ^ me_r, axis=0)
    sums = sums.transpose(1, 0, 2, 3).reshape(-1, rows_dev, tile)
    small = sums[slots:]
    sums = sums[:slots]

    turned = right_turn(sums, low_right, seqs)
    small = after(small, turned)
    turned = lax.all_to_all(after(turned, g_input), "seq", 0, 0, tiled=True)
    back = left_turns(turned, moments, low_left, low_left_t)
    news = last_turn(lax.all_to_all(back, "seq", 0, 0, tiled=True), low_right, *by_slot)
    first_new, second_new, new_weights = [values.transpose(1, 0, 2) for values in news]

    own = small[None]
    for step in seq_bits:
        own = double(own, *step, back)
    masks = gather_masks(seq_bits)
    table = np.zeros(seqs, np.int32)
    for k, (i, _) in enumerate(masks):
        table[i] = k
    grad_pos = jnp.take(own, jnp.asarray(table)[jnp.arange(seqs) ^ me_s], axis=0)
    grad_pos = grad_pos.transpose(0, 2, 1, 3).reshape(WIN, width).astype(F32)
    if aligned:
        grad_norms = grad_norms.reshape(width // tile, 4, tile).transpose(1, 0, 2).reshape(4, width)
    else:
        grad_norms = lax.psum(d_norm, ("seq", "rep"))
    norm_first, norm_second, norm_dir = adam_step(grad_norms, norm_one, norm_two)
    pos_first, pos_second, pos_dir = adam_step(grad_pos, pos_one, pos_two)
    return (
        result,
        after(g_input, back).astype(F32),
        first_new,
        second_new,
        new_weights,
        norm_first,
        norm_second,
        norm_params - LEARN_SMALL * norm_dir,
        pos_first,
        pos_second,
        positions - LEARN_SMALL * pos_dir,
    )


def solution(mesh):
    tokens = P("rep", "seq", None)
    slots = P("seq", "rep", None)
    bases = P("rep", None, None)
    return jax.shard_map(
        body,
        mesh=mesh,
        in_specs=(
            tokens,
            tokens,
            P("rep", "seq"),
            P(),
            slots,
            bases,
            bases,
            slots,
            slots,
            P(),
            P(),
            P(),
            P(),
            P(),
            P(),
        ),
        out_specs=(tokens, tokens, slots, slots, slots, P(), P(), P(), P(), P(), P()),
        check_vma=False,
    )
```

```python
import functools

import jax
import jax.numpy as jnp
import numpy as np
from jax import lax
from jax.experimental import pallas as pl
from jax.experimental.pallas import tpu as pltpu
from jax.sharding import PartitionSpec as P

H = 8
WIN = 512
STEP = 10

EPS_NORM = 1e-05
EPS_ADAM = 1e-08
BETA = 0.5
LEARN = 0.02
LEARN_SMALL = 0.2
DECAY = 0.01
MASKED = -1e30
QUERIES = 128

BF = jnp.bfloat16
F32 = jnp.float32
PARAMS = pltpu.CompilerParams(vmem_limit_bytes=58 * 1024 * 1024)
GELU_A = 0.7978845608028654
GELU_B = 0.044715


def nn(a, b):
    return lax.dot_general(a, b, (((1,), (0,)), ((), ())), preferred_element_type=F32)


def nt(a, b):
    return lax.dot_general(a, b, (((1,), (1,)), ((), ())), preferred_element_type=F32)


def tn(a, b):
    return lax.dot_general(a, b, (((0,), (0,)), ((), ())), preferred_element_type=F32)


def adam_step(gradient, first, second):
    first_new = BETA * first + (1.0 - BETA) * gradient
    second_new = BETA * second + (1.0 - BETA) * gradient * gradient
    fix = 1.0 - BETA**STEP
    direction = first_new / fix / (jnp.sqrt(second_new / fix) + EPS_ADAM)
    return (first_new, second_new, direction)


def row_norm(values):
    center = values - jnp.mean(values, axis=-1, keepdims=True)
    inverse = lax.rsqrt(jnp.mean(center * center, axis=-1, keepdims=True) + EPS_NORM)
    return center * inverse, inverse


def norm_pull(grad_rows, scaled, inverse, gain):
    scaled_grad = grad_rows * gain
    grad_input = inverse * (
        scaled_grad
        - jnp.mean(scaled_grad, axis=-1, keepdims=True)
        - scaled * jnp.mean(scaled_grad * scaled, axis=-1, keepdims=True)
    )
    grad_gain = jnp.sum(grad_rows * scaled, axis=0, keepdims=True)
    grad_shift = jnp.sum(grad_rows, axis=0, keepdims=True)
    return grad_input, grad_gain, grad_shift


def memory(mebibytes):
    return pltpu.CompilerParams(vmem_limit_bytes=mebibytes * 1024 * 1024)


def same(shape):
    return pl.BlockSpec(shape, lambda *_: (0,) * len(shape), pipeline_mode=pl.Buffered(1))


def whole(shape):
    return pl.BlockSpec(shape, lambda *_: (0,) * len(shape))


SCALARS = pl.BlockSpec(memory_space=pltpu.SMEM)


def takes(microseconds):
    return pl.CostEstimate(flops=int(microseconds * 1e6), bytes_accessed=0, transcendentals=0)


def gather_masks(order):
    masks = [(0, 0)]
    for axis, bit in order:
        step = (bit, 0) if axis == "seq" else (0, bit)
        masks = masks + [(s ^ step[0], t ^ step[1]) for s, t in masks]
    return tuple(masks)


def beyond(masks):
    return tuple((s, t ^ 1) for s, t in masks)


def block_at(me_ref, mask, reps, rows):
    block = (me_ref[0] ^ mask[0]) * reps + (me_ref[1] ^ mask[1])
    return pl.ds(pl.multiple_of(block * rows, rows), rows)


def place_blocks(me_ref, refs, target, plans, reps):
    if plans is None:
        target[...] = refs[0][...]
        return
    for ref, (first, last, masks) in zip(refs, plans):
        for k, mask in enumerate(masks):
            where = block_at(me_ref, mask, reps, ref.shape[2])
            target[first:last, where, :] = ref[k, : last - first]


def take_blocks(me_ref, source, outs, plans, reps, rows):
    if plans is None:
        outs[0][...] = source[...].astype(BF)
        return
    for out, parts in zip(outs, plans):
        at = 0
        for first, last, masks in parts:
            for mask in masks:
                where = block_at(me_ref, mask, reps, rows)
                out[at : at + last - first] = source[first:last, where, :].astype(BF)
                at += last - first


def attend_kernel(plans, reps, me_ref, x_ref, pos_ref, ids_row, ids_col, *refs):
    count = 1 if plans is None else len(plans)
    pieces = refs[:count]
    qkv_ref, mixed_ref, lse_ref, bias, w_ref = refs[count:]
    win, width = pos_ref.shape
    dim = width // H
    tile = w_ref.shape[2]


    @pl.when(pl.program_id(0) == 0)
    def _():
        place_blocks(me_ref, pieces, w_ref, plans, reps)

    hidden = x_ref[...].reshape(win, width).astype(F32) + pos_ref[...]
    low = hidden.astype(BF)
    for t in range(w_ref.shape[0]):
        qkv_ref[0, :, t * tile : (t + 1) * tile] = nn(low, w_ref[t]).astype(BF)
    row = lax.broadcasted_iota(jnp.int32, (win, win), 0)
    col = lax.broadcasted_iota(jnp.int32, (win, win), 1)
    allowed = (ids_col[0] == ids_row[0]) & (col >= row)
    bias[...] = jnp.where(allowed, 0.0, MASKED)
    ones = jnp.ones((win, dim), BF)
    blocks = [(lo, lo + QUERIES) for lo in range(0, win, QUERIES)]

    def score(h):
        base = 3 * dim * h
        query = qkv_ref[0, :, base : base + dim] * (dim**-0.5)
        keys = qkv_ref[0, :, base + dim : base + 2 * dim]
        return [nt(keys[:hi], query[lo:hi]) + bias[:hi, lo:hi] for lo, hi in blocks]

    def mix(h, scores):
        base = 3 * dim * h
        values = jnp.concatenate([qkv_ref[0, :, base + 2 * dim : base + 3 * dim], ones], axis=1)
        values = values.T[: dim + 16]
        parts, logs = [], []
        for some in scores:
            highest = jnp.max(some, axis=0, keepdims=True)
            both = nn(values[:, : some.shape[0]], jnp.exp(some - highest).astype(BF))
            total = both[dim : dim + 1]
            parts.append(both[:dim] / total)
            logs.append(highest + jnp.log(total))
        lse_ref[0, h : h + 1] = jnp.concatenate(logs, axis=1)
        return jnp.concatenate(parts, axis=1).astype(BF)

    outs = []
    scores = score(0)
    for h in range(H):
        later = score(h + 1) if h + 1 < H else None
        outs.append(mix(h, scores))
        scores = later
    mixed_ref[0] = jnp.concatenate(outs, axis=0).T


def attend_forward(me, x, positions, ids, w, plans, tiles, tile, reps):
    group, wins, span, width = x.shape
    win = group * span
    return pl.pallas_call(
        functools.partial(attend_kernel, plans, reps),
        grid=(wins,),
        in_specs=[
            SCALARS,
            pl.BlockSpec((group, 1, span, width), lambda i: (0, i, 0, 0)),
            same((win, width)),
            pl.BlockSpec((1, 1, win), lambda i: (i, 0, 0)),
            pl.BlockSpec((1, win, 1), lambda i: (i, 0, 0)),
        ]
        + [same(piece.shape) for piece in w],
        out_specs=[
            pl.BlockSpec((1, win, 3 * width), lambda i: (i, 0, 0)),
            pl.BlockSpec((1, win, width), lambda i: (i, 0, 0)),
            pl.BlockSpec((1, H, win), lambda i: (i, 0, 0)),
        ],
        out_shape=[
            jax.ShapeDtypeStruct((wins, win, 3 * width), BF),
            jax.ShapeDtypeStruct((wins, win, width), BF),
            jax.ShapeDtypeStruct((wins, H, win), F32),
        ],
        scratch_shapes=[pltpu.VMEM((win, win), F32), pltpu.VMEM((tiles, width, tile), BF)],
        compiler_params=memory(32),
        cost_estimate=takes(18),
        name="attend_forward",
    )(me, x, positions, ids[:, None, :], ids[:, :, None], *w)


def middle_kernel(
    plans, out_plans, reps, rows, outs, wins, me_ref, x_ref, pos_ref, mixed_ref, cot_ref, norm_ref, moments_ref, *refs
):
    count = 1 if plans is None else len(plans)
    pieces = refs[:count]
    refs = refs[count:]
    result_ref, mid_ref, gmixed_ref, dnorm_ref = refs[:4]
    count = 1 if out_plans is None else 2
    grads = refs[4 : 4 + count]
    act, slope, gpre, w_ref, acc = refs[4 + count :]
    step = pl.program_id(0)
    last = wins - 1
    win, width = pos_ref.shape
    tile = w_ref.shape[2]
    ups = (w_ref.shape[0] - outs) // 2
    blocks = ups // 2
    up, down = outs, outs + ups

    @pl.when(step == 0)
    def _():
        place_blocks(me_ref, pieces, w_ref, plans, reps)
        acc[...] = jnp.zeros_like(acc)
        dnorm_ref[...] = jnp.zeros_like(dnorm_ref)
        if result_ref.shape[2] > (last + 1) * width:
            result_ref[:, :, (last + 1) * width :] = moments_ref[...]

    mixed = mixed_ref[0]
    hidden = x_ref[...].reshape(win, width).astype(F32) + pos_ref[...]
    attn = jnp.concatenate([nn(mixed, w_ref[t]) for t in range(outs)], axis=1)
    scaled_one, inverse_one = row_norm(hidden + attn)
    normed = scaled_one * norm_ref[0:1] + norm_ref[1:2]
    low = normed.astype(BF)
    for t in range(ups):
        pre = nn(low, w_ref[up + t])
        square = pre * pre
        bent = jnp.tanh(GELU_A * pre * (1.0 + GELU_B * square))
        act[:, t * tile : (t + 1) * tile] = (0.5 * pre * (1.0 + bent)).astype(BF)
        slope[:, t * tile : (t + 1) * tile] = (
            0.5 * (1.0 + bent)
            + 0.5 * pre * (1.0 - bent * bent) * (GELU_A + 3.0 * GELU_A * GELU_B * square)
        ).astype(BF)
    branch = jnp.concatenate(
        [
            sum(nn(act[:, b * width : (b + 1) * width], w_ref[down + 2 * b + j]) for b in range(blocks))
            for j in range(2)
        ],
        axis=1,
    )
    scaled_two, inverse_two = row_norm(normed + branch)
    result = scaled_two * norm_ref[2:3] + norm_ref[3:4]
    result = result.astype(BF).reshape(*result_ref.shape[:2], width)
    for window in range(wins):

        @pl.when(step == window)
        def _():
            result_ref[:, :, window * width : (window + 1) * width] = result

    grad_resid, gain_two, shift_two = norm_pull(
        cot_ref[...].reshape(win, width).astype(F32), scaled_two, inverse_two, norm_ref[2:3]
    )
    gb = grad_resid.astype(BF)
    for b in range(blocks):
        cols = slice(b * width, (b + 1) * width)
        gact = nt(gb[:, :tile], w_ref[down + 2 * b]) + nt(gb[:, tile:], w_ref[down + 2 * b + 1])
        gpre[:, cols] = (gact * slope[:, cols].astype(F32)).astype(BF)
    grad_normed = grad_resid + sum(
        nt(gpre[:, t * tile : (t + 1) * tile], w_ref[up + t]) for t in range(ups)
    )
    grad_mid, gain_one, shift_one = norm_pull(grad_normed, scaled_one, inverse_one, norm_ref[0:1])
    mid_ref[0] = grad_mid
    ga = grad_mid.astype(BF)
    gmixed_ref[0] = sum(nt(ga[:, t * tile : (t + 1) * tile], w_ref[t]) for t in range(outs)).astype(BF)
    dnorm_ref[...] += jnp.concatenate([gain_one, shift_one, gain_two, shift_two], axis=0)
    for b in range(blocks):
        act_t = act[:, b * width : (b + 1) * width].T
        for j in range(2):
            acc[down + 2 * b + j] += nn(act_t, gb[:, j * tile : (j + 1) * tile])
    low_t = low.T
    for t in range(ups):
        acc[up + t] += nn(low_t, gpre[:, t * tile : (t + 1) * tile])
    mixed_t = mixed.T
    for t in range(outs):
        acc[t] += nn(mixed_t, ga[:, t * tile : (t + 1) * tile])

    @pl.when(step == last)
    def _():
        take_blocks(me_ref, acc, grads, out_plans, reps, rows)


def middle(me, x, positions, mixed, cot, norms, moments, together, w, plans, out_plans, grad_shapes, tiles, tile, reps, rows):
    group, wins, span, width = x.shape
    win = group * span
    outs = width // tile
    hidden = (tiles - outs) // 2 * tile
    sent = (group, span, wins * width + (moments.shape[2] if together else 0))
    seq_spec = pl.BlockSpec((group, 1, span, width), lambda i: (0, i, 0, 0))
    row_spec = pl.BlockSpec((1, win, width), lambda i: (i, 0, 0))
    return pl.pallas_call(
        functools.partial(middle_kernel, plans, out_plans, reps, rows, outs, wins),
        grid=(wins,),
        in_specs=[
            SCALARS,
            seq_spec,
            same((win, width)),
            row_spec,
            seq_spec,
            same(norms.shape),
            same(moments.shape),
        ]
        + [same(piece.shape) for piece in w],
        out_specs=[whole(sent), row_spec, row_spec, whole(norms.shape)]
        + [whole(shape) for shape in grad_shapes],
        out_shape=[
            jax.ShapeDtypeStruct(sent, BF),
            jax.ShapeDtypeStruct((wins, win, width), F32),
            jax.ShapeDtypeStruct((wins, win, width), BF),
            jax.ShapeDtypeStruct(norms.shape, F32),
        ]
        + [jax.ShapeDtypeStruct(shape, BF) for shape in grad_shapes],
        scratch_shapes=[
            pltpu.VMEM((win, hidden), BF),
            pltpu.VMEM((win, hidden), BF),
            pltpu.VMEM((win, hidden), BF),
            pltpu.VMEM((tiles, width, tile), BF),
            pltpu.VMEM((tiles, width, tile), F32),
        ],
        compiler_params=PARAMS,
        cost_estimate=takes(27),
        name="middle",
    )(me, x, positions, mixed, cot, norms, moments, *w)


def attend_back_kernel(
    plans,
    out_plans,
    reps,
    rows,
    behind,
    me_ref,
    x_ref,
    pos_ref,
    ids_row,
    ids_col,
    qkv_ref,
    lse_ref,
    gmixed_ref,
    mid_ref,
    dnorm_ref,
    *refs,
):
    count = 1 if plans is None else len(plans)
    pieces = refs[:count]
    ginput_ref = refs[count + behind]
    refs = refs[count + behind + 1 :]
    count = 1 if out_plans is None else 2
    grads = refs[:count]
    bias, gproj, w_ref, acc = refs[count:]
    step = pl.program_id(0)
    last = pl.num_programs(0) - 1
    win, width = pos_ref.shape
    dim = width // H
    tiles, _, tile = w_ref.shape
    factor = dim**-0.5
    half = win // 2

    @pl.when(step == 0)
    def _():
        place_blocks(me_ref, pieces, w_ref, plans, reps)
        acc[...] = jnp.zeros_like(acc)

    key = lax.broadcasted_iota(jnp.int32, (win, win), 0)
    query_at = lax.broadcasted_iota(jnp.int32, (win, win), 1)
    allowed = (ids_col[0] == ids_row[0]) & (query_at >= key)
    bias[...] = jnp.where(allowed, 0.0, MASKED)
    blocks = [(lo, lo + QUERIES) for lo in range(0, win, QUERIES)]

    def operands(h):
        base = 3 * dim * h
        query = qkv_ref[0, :, base : base + dim] * factor
        keys = qkv_ref[0, :, base + dim : base + 2 * dim]
        values = qkv_ref[0, :, base + 2 * dim : base + 3 * dim]
        return query, keys, values, gmixed_ref[0, :, h * dim : (h + 1) * dim]

    def score(h):
        query, keys, values, gout = operands(h)
        return [
            (nt(keys[:hi], query[lo:hi]) + bias[:hi, lo:hi], nt(values[:hi], gout[lo:hi])) for lo, hi in blocks
        ]

    def pull(h, scores):
        query, keys, _, gout = operands(h)
        keys_t = jnp.concatenate([keys, keys], axis=1).T[:dim]
        probs, gscores, gqueries = [], [], []
        for (lo, hi), (some, gprobs) in zip(blocks, scores):
            weights = jnp.exp(some - lse_ref[0, h : h + 1, lo:hi])
            inner = jnp.sum(weights * gprobs, axis=0, keepdims=True)
            gscore = (weights * (gprobs - inner)).astype(BF)
            probs.append(weights.astype(BF))
            gscores.append(gscore)
            gqueries.append(nn(keys_t[:, :hi], gscore))
        gkeys, gvalues = [], []
        for lo, hi in blocks:
            later = [i for i, (_, end) in enumerate(blocks) if end >= hi]
            gkeys.append(nn(jnp.concatenate([gscores[i][lo:hi] for i in later], axis=1), query[lo:]))
            gvalues.append(nn(jnp.concatenate([probs[i][lo:hi] for i in later], axis=1), gout[lo:]))
        gquery = jnp.concatenate(gqueries, axis=1) * factor
        return gquery.astype(BF), [jnp.concatenate(part, axis=0).astype(BF) for part in (gkeys, gvalues)]

    done = []
    scores = score(0)
    for h in range(H):
        later = score(h + 1) if h + 1 < H else None
        done.append(pull(h, scores))
        scores = later
        if h % 2:
            packed = jnp.concatenate([done[-2][0], done[-1][0]], axis=0).T
            parts = [packed[:, :dim], *done[-2][1], packed[:, dim:], *done[-1][1]]
            gproj[:, 3 * dim * (h - 1) : 3 * dim * (h + 1)] = jnp.concatenate(parts, axis=1)
    hidden = x_ref[...].reshape(win, width).astype(F32) + pos_ref[...]
    low_t = hidden.astype(BF).T
    total = mid_ref[0]
    for t in range(tiles):
        part = gproj[:, t * tile : (t + 1) * tile]
        acc[t] += nn(low_t, part)
        total += nt(part, w_ref[t])
    ginput_ref[...] = total.astype(BF).reshape(ginput_ref.shape)
    for j in range(width // tile):
        acc[tiles + j] += total[:, j * tile : (j + 1) * tile]

    @pl.when(step == last)
    def _():
        if out_plans is not None:
            small = jnp.concatenate(
                [dnorm_ref[:, j * tile : (j + 1) * tile] for j in range(width // tile)], axis=0
            )
            small = jnp.concatenate([small, jnp.zeros((rows - small.shape[0], tile), F32)], axis=0)
            for b in range(win // rows):
                acc[acc.shape[0] - 1, b * rows : (b + 1) * rows] = small
        take_blocks(me_ref, acc, grads, out_plans, reps, rows)


def attend_backward(
    me, x, positions, ids, qkv, lse, gmixed, mid, dnorm, behind, w, plans, out_plans, grad_shapes, tiles, tile, reps, rows
):
    group, wins, span, width = x.shape
    win = group * span
    seq_spec = pl.BlockSpec((group, 1, span, width), lambda i: (0, i, 0, 0))
    row_spec = pl.BlockSpec((1, win, width), lambda i: (i, 0, 0))
    return pl.pallas_call(
        functools.partial(attend_back_kernel, plans, out_plans, reps, rows, len(behind)),
        grid=(wins,),
        in_specs=[
            SCALARS,
            seq_spec,
            same((win, width)),
            pl.BlockSpec((1, 1, win), lambda i: (i, 0, 0)),
            pl.BlockSpec((1, win, 1), lambda i: (i, 0, 0)),
            pl.BlockSpec((1, win, 3 * width), lambda i: (i, 0, 0)),
            pl.BlockSpec((1, H, win), lambda i: (i, 0, 0)),
            row_spec,
            row_spec,
            same(dnorm.shape),
        ]
        + [same(piece.shape) for piece in w]
        + [pl.BlockSpec(memory_space=pl.ANY) for _ in behind],
        out_specs=[seq_spec] + [whole(shape) for shape in grad_shapes],
        out_shape=[jax.ShapeDtypeStruct(x.shape, BF)]
        + [jax.ShapeDtypeStruct(shape, BF) for shape in grad_shapes],
        scratch_shapes=[
            pltpu.VMEM((win, win), F32),
            pltpu.VMEM((win, 3 * width), BF),
            pltpu.VMEM((tiles, width, tile), BF),
            pltpu.VMEM((tiles + width // tile + 1, width, tile), F32),
        ],
        compiler_params=memory(36),
        cost_estimate=takes(22),
        name="attend_backward",
    )(me, x, positions, ids[:, None, :], ids[:, :, None], qkv, lse, gmixed, mid, dnorm, *w, *behind)


def right_kernel(rows_ref, right_ref, out_ref):
    seqs, _, _ = out_ref.shape
    slots, _, tile = rows_ref.shape
    cols = tile // seqs
    for s in range(slots):
        turned = nn(rows_ref[s], right_ref[s]).astype(BF)
        for j in range(seqs):
            out_ref[j, :, s * cols : (s + 1) * cols] = turned[:, j * cols : (j + 1) * cols]


def right_turn(rows, right, seqs):
    slots, rows_dev, tile = rows.shape
    return pl.pallas_call(
        right_kernel,
        out_shape=jax.ShapeDtypeStruct((seqs, rows_dev, slots * tile // seqs), BF),
        compiler_params=memory(16),
        cost_estimate=takes(3),
        name="right_turn",
    )(rows, right)


def left_kernel(x_ref, moments_ref, left_ref, out_ref):
    seqs, rows_dev, wide = x_ref.shape
    slots, width, _ = left_ref.shape
    cols = wide // slots
    x = x_ref[...].reshape(width, wide)
    at = moments_ref.shape[2] - 2 * wide
    moments = moments_ref[:, :, at:].reshape(width, 2 * wide).astype(F32)
    spare = -wide % 128
    x_t = jnp.concatenate([x, jnp.zeros((width, spare), BF)], axis=1).T
    turned = [nn(x_t[s * cols : (s + 1) * cols], left_ref[s]) for s in range(slots)]
    turned = jnp.concatenate(turned + [jnp.zeros((spare, width), F32)], axis=0).T[:, :wide]
    direction = adam_step(turned, moments[:, :wide], moments[:, wide:])[2].astype(BF)
    change = [nn(left_ref[s], direction[:, s * cols : (s + 1) * cols]) for s in range(slots)]
    out = jnp.concatenate(change + [turned], axis=1).astype(BF)
    out_ref[...] = out.reshape(out_ref.shape)


def left_turns(x, moments, left):
    seqs, rows_dev, wide = x.shape
    return pl.pallas_call(
        left_kernel,
        out_shape=jax.ShapeDtypeStruct((seqs, rows_dev, 2 * wide), BF),
        compiler_params=PARAMS,
        cost_estimate=takes(3),
        name="left_turns",
    )(x, moments, left)


def last_kernel(back_ref, right_ref, w_ref, one_ref, two_ref, new_one, new_two, new_w):
    seqs, rows_dev, _ = back_ref.shape
    slots, _, tile = w_ref.shape
    cols = tile // seqs
    for s in range(slots):

        def columns(first):
            return jnp.concatenate(
                [back_ref[j, :, first + s * cols : first + (s + 1) * cols] for j in range(seqs)], axis=1
            )

        change = nt(columns(0), right_ref[s])
        turned = columns(slots * cols).astype(F32)
        new_one[s], new_two[s], _ = adam_step(turned, one_ref[s], two_ref[s])
        old = w_ref[s]
        new_w[s] = old - LEARN * (change + DECAY * old)


def last_turn(back, right, weights, one, two):
    shape = jax.ShapeDtypeStruct(weights.shape, F32)
    return pl.pallas_call(
        last_kernel,
        out_shape=[shape, shape, shape],
        compiler_params=memory(16),
        cost_estimate=takes(3),
        name="last_turn",
    )(back, right, weights, one, two)


def columns_kernel(one_ref, two_ref, out_ref):
    seqs = out_ref.shape[0]
    slots, _, tile = one_ref.shape
    cols = tile // seqs
    for first, ref in ((0, one_ref), (slots, two_ref)):
        for s in range(slots):
            values = ref[s].astype(BF)
            for j in range(seqs):
                at = (first + s) * cols
                out_ref[j, :, at : at + cols] = values[:, j * cols : (j + 1) * cols]


def moment_columns(one, two, seqs):
    slots, rows_dev, tile = one.shape
    return pl.pallas_call(
        columns_kernel,
        out_shape=jax.ShapeDtypeStruct((seqs, rows_dev, 2 * slots * tile // seqs), BF),
        compiler_params=PARAMS,
        cost_estimate=takes(3000),
        name="moment_columns",
    )(one, two)


def bases_kernel(left_ref, right_ref, low_left, low_right):
    low_left[...] = left_ref[...].astype(BF)
    low_right[...] = right_ref[...].astype(BF)


def low_bases(left, right):
    slots, width, _ = left.shape
    tile = right.shape[1]
    some = 3 if slots % 3 == 0 else 1
    big = pl.BlockSpec((some, width, width), lambda i: (i, 0, 0))
    little = pl.BlockSpec((some, tile, tile), lambda i: (i, 0, 0))
    return pl.pallas_call(
        bases_kernel,
        grid=(slots // some,),
        in_specs=[big, little],
        out_specs=[big, little],
        out_shape=[
            jax.ShapeDtypeStruct(left.shape, BF),
            jax.ShapeDtypeStruct(right.shape, BF),
        ],
        compiler_params=PARAMS,
        cost_estimate=takes(3),
        name="low_bases",
    )(left, right)


def swap(x, axis, bit):
    size = lax.axis_size(axis)
    return lax.ppermute(x, axis, [(i, i ^ bit) for i in range(size)])


def exchange(x, axis, group):
    size = lax.axis_size(axis)
    groups = None
    if group != size:
        groups = [[base + i for i in range(group)] for base in range(0, size, group)]
    return lax.all_to_all(x, axis, 0, 0, axis_index_groups=groups, tiled=True)


def after(x, *others):
    return lax.optimization_barrier((x,) + others)[0]


def powers(first, size):
    bits = []
    while first < size:
        bits.append(first)
        first *= 2
    return bits


def gather(block, order):
    own = block[None]
    for axis, bit in order[:-1]:
        own = jnp.concatenate([own, swap(own, axis, bit)], axis=0)
    return own, swap(own, *order[-1])


def add(a, b, *others):
    if others:
        b = after(b, *others)
    return (a.astype(F32) + b.astype(F32)).astype(BF)


def double(buf, axis, bit, *others):
    got = swap(buf, axis, bit)
    if others:
        got = after(got, *others)
    return jnp.concatenate([buf, got], axis=0)


def halve(buf, axis, bit, *others):
    cut = buf.shape[0] // 2
    return add(buf[:cut], swap(buf[cut:], axis, bit), *others)


def body(
    inputs,
    cotangent,
    segments,
    owners,
    weights,
    left_bases,
    right_bases,
    moment_one,
    moment_two,
    norm_params,
    norm_one,
    norm_two,
    positions,
    pos_one,
    pos_two,
):
    seqs = lax.axis_size("seq")
    reps = lax.axis_size("rep")
    me_s = lax.axis_index("seq")
    me_r = lax.axis_index("rep")
    me = jnp.stack([me_s, me_r]).astype(jnp.int32)
    seq_local, span, width = inputs.shape
    rows_dev, slots, tile = weights.shape
    tiles = owners.shape[0]
    rows = rows_dev // reps
    group = WIN // span
    place = me_s % group
    wins = seq_local // group
    aligned = rows % 16 == 0
    blocks = seqs * reps
    seq_bits = [("seq", b) for b in powers(1, seqs)[::-1]]
    far_bits = [("rep", b) for b in powers(2, reps)]
    core_bit = [("rep", 1)]

    low_w = weights.astype(BF).transpose(1, 0, 2).reshape(slots, reps, rows, tile).transpose(1, 0, 2, 3)
    near = [lax.dynamic_index_in_dim(low_w, me_r, 0, keepdims=False)]
    for k in range(1, reps):
        near.append(swap(lax.dynamic_index_in_dim(low_w, me_r ^ k, 0, keepdims=False), "rep", k))
    near = jnp.concatenate(near, axis=0)
    near = jnp.take(near, ((owners // slots) ^ me_r) * slots + owners % slots, axis=0)
    ids = segments.reshape(-1)
    id_tiles = -(-2 * ids.shape[0] // (rows * tile))
    ids = jnp.concatenate([ids // 64, ids % 64]).astype(BF)
    ids = jnp.pad(ids, (0, id_tiles * rows * tile - ids.shape[0])).reshape(id_tiles, rows, tile)

    qkv_tiles = 3 * width // tile
    rest_tiles = tiles - qkv_tiles
    qkv_at, rest_at = qkv_tiles // 2, rest_tiles // 2
    split = qkv_at + id_tiles
    by_slot = [values.transpose(1, 0, 2) for values in (weights, moment_one, moment_two)]
    rest = near[qkv_tiles:][None]
    near = jnp.concatenate([near[:qkv_at], ids, near[qkv_at:qkv_tiles]], axis=0)[None]
    moments = moment_columns(after(by_slot[1], near), by_slot[2], seqs)
    for i, step in enumerate(seq_bits[:-1]):
        near = double(near, *step, *([moments] if i == 0 else []))
        rest = double(after(rest, moments) if i == 0 else rest, *step, near)
        if i == 0:
            x = after(inputs, near)
    x = exchange(x, "seq", group)
    cot = exchange(after(cotangent, x), "seq", group).reshape(group, wins, span, width)
    x = x.reshape(group, wins, span, width)

    def table_of(masks):
        table = np.zeros(blocks, np.int32)
        for k, (s, t) in enumerate(masks):
            table[s * reps + t] = k
        return jnp.asarray(table)

    orders = [seq_bits[-1:] + far_bits, far_bits + seq_bits[-1:]]

    def pieces_of(bufs, ranges):
        pieces, plans = [], []
        for buf, order, (first, last) in zip(bufs, orders, ranges):
            masks = gather_masks(seq_bits[:-1] + order)
            pieces += [buf, swap(buf, *core_bit[0])]
            plans += [(first, last, masks), (first, last, beyond(masks))]
        return settle(pieces, plans)

    def settle(pieces, plans):
        if aligned:
            return pieces, plans
        at = jnp.arange(blocks)
        full = []
        for i in range(0, len(pieces), 2):
            count = plans[i][1] - plans[i][0]
            table = table_of(plans[i][2] + plans[i + 1][2])
            both = jnp.concatenate([pieces[i][:, :count], pieces[i + 1][:, :count]], axis=0)
            both = jnp.take(both, table[((at // reps) ^ me_s) * reps + ((at % reps) ^ me_r)], axis=0)
            full.append(both.transpose(1, 0, 2, 3).reshape(count, blocks * rows, tile))
        return [jnp.concatenate(full, axis=0)], None

    bufs = [near[:, :split], near[:, split:]]
    bufs = [double(buf, *order[0]) for buf, order in zip(bufs, orders)]
    ids = bufs[0][:, qkv_at:]
    rest = after(rest, *bufs)
    for i in range(1, len(orders[0])):
        bufs = [double(buf, *order[i]) for buf, order in zip(bufs, orders)]
    w_qkv, qkv_plans = pieces_of(bufs, [(0, qkv_at), (qkv_at, qkv_tiles)])
    rest = [rest[:, :rest_at], rest[:, rest_at:]]
    rest = [double(buf, *order[0], *bufs) for buf, order in zip(rest, orders)]

    ids = ids.reshape(seqs, -1)[:, : 2 * seq_local * span].astype(jnp.int32)
    ids = (ids[:, : seq_local * span] * 64 + ids[:, seq_local * span :]).reshape(seqs, seq_local, span)
    spots = [0] * seqs
    for k, (s, _) in enumerate(gather_masks(seq_bits[:-1] + seq_bits[-1:])):
        spots[s] = k
    ids = jnp.take(ids, jnp.asarray(spots[:group])[jnp.arange(group) ^ place], axis=0)
    ids = lax.dynamic_slice_in_dim(ids, place * wins, wins, 1)
    ids = ids.transpose(1, 0, 2).reshape(wins, WIN)

    def scatter_plans(parts):
        count = parts[-1][1]
        if not aligned:
            return None, [(count, blocks * rows, tile)]
        own = [(first, last, gather_masks(order[:0:-1])) for first, last, order in parts]
        other = [(first, last, beyond(masks)) for first, last, masks in own]
        shape = (count * blocks // 2, rows, tile)
        return [own, other], [shape, shape]

    def scatter_tiles(grads, parts, *others):
        if not aligned:
            plain = grads[0].reshape(-1, blocks, rows, tile).transpose(1, 0, 2, 3)
            own, other = [], []
            for first, last, order in parts:
                masks = gather_masks(order[:0:-1])
                for target, some in ((own, masks), (other, beyond(masks))):
                    spots = np.array([s * reps + t for s, t in some])
                    at = ((spots // reps) ^ me_s) * reps + ((spots % reps) ^ me_r)
                    target.append(jnp.take(plain[:, first:last], at, axis=0).reshape(-1, rows, tile))
            grads = [jnp.concatenate(own, axis=0), jnp.concatenate(other, axis=0)]
        return add(grads[0], swap(grads[1], *core_bit[0]), *others)

    def cut_parts(buf, parts):
        out, at = [], 0
        for first, last, _ in parts:
            size = (last - first) * blocks // 2
            out.append(buf[at : at + size])
            at += size
        return out

    def join(bufs, parts):
        entries = 2 ** len(seq_bits[:-1])
        return jnp.concatenate([buf.reshape(entries, -1, rows, tile) for buf in bufs], axis=1)

    zyxc = seq_bits + far_bits + core_bit
    zxyc = seq_bits[:-1] + far_bits + seq_bits[-1:] + core_bit
    ids = after(ids, *rest)
    ahead = attend_forward(me, x, positions, ids, w_qkv, qkv_plans, qkv_tiles, tile, reps)
    for i in range(1, len(orders[0])):
        got = [swap(buf, *order[i]) for buf, order in zip(rest, orders)]
        qkv, mixed, lse, *got = lax.optimization_barrier((*ahead, *got))
        rest = [jnp.concatenate([buf, part], axis=0) for buf, part in zip(rest, got)]
    w_rest, rest_plans = pieces_of(rest, [(0, rest_at), (rest_at, rest_tiles)])
    rest_parts = [(0, rest_at, zyxc[::-1]), (rest_at, rest_tiles, zxyc[::-1])]
    out_plans, shapes = scatter_plans(rest_parts)
    result, mid, gmixed, d_norm, *d_rest = middle(
        me, x, positions, mixed, cot, norm_params, moments, group == seqs, w_rest, rest_plans, out_plans, shapes, rest_tiles, tile, reps, rows
    )
    result = exchange(result, "seq", group)
    rest = cut_parts(scatter_tiles(d_rest, rest_parts), rest_parts)
    steps = [[order[1 + i] for _, _, order in rest_parts] for i in range(len(orders[0]))]
    cuts = [buf.shape[0] // 2 for buf in rest]
    got = [swap(buf[cut:], *step) for buf, cut, step in zip(rest, cuts, steps[0])]

    qkv_total = qkv_tiles + width // tile + 1
    qkv_parts = [(0, 6, zyxc[::-1]), (6, qkv_total, zxyc[::-1])]
    out_plans, shapes = scatter_plans(qkv_parts)
    g_input, *d_qkv = attend_backward(
        me, x, positions, ids, qkv, lse, gmixed, mid, d_norm, rest,
        w_qkv, qkv_plans, out_plans, shapes, qkv_tiles, tile, reps, rows,
    )
    count = len(d_qkv)
    g_input, *some = lax.optimization_barrier((g_input, *d_qkv, *got))
    d_qkv, got = some[:count], some[count:]
    g_input = after(g_input, result)
    if group == seqs:
        moments = result
    else:
        moments = lax.all_to_all(after(moments, result), "seq", 0, 0, tiled=True)
    result = result[:, :, : wins * width].reshape(group, span, wins, width)
    result = result.transpose(0, 2, 1, 3).reshape(seq_local, span, width)
    rest = [add(buf[:cut], part) for buf, cut, part in zip(rest, cuts, got)]

    qkv_buf = scatter_tiles(d_qkv, qkv_parts)
    mine = cut_parts(qkv_buf, qkv_parts)
    low_left, low_right = low_bases(after(left_bases, qkv_buf), right_bases)
    mine = [halve(buf, *step, low_left) for buf, step in zip(mine, steps[0])]
    for some in steps[1:]:
        rest = [halve(buf, *step, *mine) for buf, step in zip(rest, some)]
        mine = [halve(buf, *step, *rest) for buf, step in zip(mine, some)]
    rest, mine = join(rest, rest_parts), join(mine, qkv_parts)
    for step in seq_bits[-2::-1]:
        rest = halve(rest, *step, mine)
        mine = halve(mine, *step, rest)
    rest, mine = rest[0], mine[0]
    g_input = exchange(g_input.reshape(seq_local, span, width), "seq", group)

    small = mine[qkv_tiles:]
    grad_norms = small[-1, : 4 * width // tile].astype(F32)
    sums = jnp.concatenate([mine[:qkv_tiles], rest], axis=0)
    tile_of = jnp.sum(
        jnp.where(owners[None, :] == jnp.arange(tiles)[:, None], jnp.arange(tiles)[None, :], 0), axis=1
    )
    sums = jnp.take(sums, tile_of, axis=0).reshape(reps, slots, rows, tile)
    g_input = after(g_input, sums).astype(F32)
    small = small[: width // tile]
    near = []
    for k in range(reps):
        part = lax.dynamic_index_in_dim(sums, me_r ^ k, 0, keepdims=False)
        part = jnp.concatenate([part, small], axis=0)
        near.append(swap(part, "rep", k) if k else part)
    sums = jnp.take(jnp.stack(near), jnp.arange(reps) ^ me_r, axis=0)
    sums = sums.transpose(1, 0, 2, 3).reshape(-1, rows_dev, tile)
    small = sums[slots:]
    sums = sums[:slots]

    turned = right_turn(sums, low_right, seqs)
    small = after(small, turned)
    turned = lax.all_to_all(after(turned, g_input), "seq", 0, 0, tiled=True)
    back = left_turns(turned, moments, low_left)
    news = last_turn(lax.all_to_all(back, "seq", 0, 0, tiled=True), low_right, *by_slot)
    first_new, second_new, new_weights = [values.transpose(1, 0, 2) for values in news]

    own = small[None]
    for i, step in enumerate(seq_bits):
        own = double(own, *step, *([turned] if i == 0 else [back]))
    masks = gather_masks(seq_bits)
    table = np.zeros(seqs, np.int32)
    for k, (i, _) in enumerate(masks):
        table[i] = k
    grad_pos = jnp.take(own, jnp.asarray(table)[jnp.arange(seqs) ^ me_s], axis=0)
    grad_pos = grad_pos.transpose(0, 2, 1, 3).reshape(WIN, width).astype(F32)
    if aligned:
        grad_norms = grad_norms.reshape(width // tile, 4, tile).transpose(1, 0, 2).reshape(4, width)
    else:
        grad_norms = lax.psum(d_norm, ("seq", "rep"))
    norm_first, norm_second, norm_dir = adam_step(grad_norms, norm_one, norm_two)
    pos_first, pos_second, pos_dir = adam_step(grad_pos, pos_one, pos_two)
    return (
        result,
        g_input,
        first_new,
        second_new,
        new_weights,
        norm_first,
        norm_second,
        norm_params - LEARN_SMALL * norm_dir,
        pos_first,
        pos_second,
        positions - LEARN_SMALL * pos_dir,
    )


def solution(mesh):
    tokens = P("rep", "seq", None)
    slots = P("seq", "rep", None)
    bases = P("rep", None, None)
    return jax.shard_map(
        body,
        mesh=mesh,
        in_specs=(
            tokens,
            tokens,
            P("rep", "seq"),
            P(),
            slots,
            bases,
            bases,
            slots,
            slots,
            P(),
            P(),
            P(),
            P(),
            P(),
            P(),
        ),
        out_specs=(tokens, tokens, slots, slots, slots, P(), P(), P(), P(), P(), P()),
        check_vma=False,
    )
```

```python
import functools

import jax
import jax.numpy as jnp
import numpy as np
from jax import lax
from jax.experimental import pallas as pl
from jax.experimental.pallas import tpu as pltpu
from jax.sharding import PartitionSpec as P

H = 8
WIN = 512
STEP = 10

EPS_NORM = 1e-05
EPS_ADAM = 1e-08
BETA = 0.5
LEARN = 0.02
LEARN_SMALL = 0.2
DECAY = 0.01
MASKED = -1e30
QUERIES = 128

BF = jnp.bfloat16
F32 = jnp.float32
PARAMS = pltpu.CompilerParams(vmem_limit_bytes=58 * 1024 * 1024)
GELU_A = 0.7978845608028654
GELU_B = 0.044715


def nn(a, b):
    return lax.dot_general(a, b, (((1,), (0,)), ((), ())), preferred_element_type=F32)


def nt(a, b):
    return lax.dot_general(a, b, (((1,), (1,)), ((), ())), preferred_element_type=F32)


def tn(a, b):
    return lax.dot_general(a, b, (((0,), (0,)), ((), ())), preferred_element_type=F32)


def adam_step(gradient, first, second):
    first_new = BETA * first + (1.0 - BETA) * gradient
    second_new = BETA * second + (1.0 - BETA) * gradient * gradient
    fix = 1.0 - BETA**STEP
    direction = first_new / fix / (jnp.sqrt(second_new / fix) + EPS_ADAM)
    return (first_new, second_new, direction)


def row_norm(values):
    center = values - jnp.mean(values, axis=-1, keepdims=True)
    inverse = lax.rsqrt(jnp.mean(center * center, axis=-1, keepdims=True) + EPS_NORM)
    return center * inverse, inverse


def norm_pull(grad_rows, scaled, inverse, gain):
    scaled_grad = grad_rows * gain
    grad_input = inverse * (
        scaled_grad
        - jnp.mean(scaled_grad, axis=-1, keepdims=True)
        - scaled * jnp.mean(scaled_grad * scaled, axis=-1, keepdims=True)
    )
    grad_gain = jnp.sum(grad_rows * scaled, axis=0, keepdims=True)
    grad_shift = jnp.sum(grad_rows, axis=0, keepdims=True)
    return grad_input, grad_gain, grad_shift


def memory(mebibytes):
    return pltpu.CompilerParams(vmem_limit_bytes=mebibytes * 1024 * 1024)


def same(shape):
    return pl.BlockSpec(shape, lambda *_: (0,) * len(shape), pipeline_mode=pl.Buffered(1))


def whole(shape):
    return pl.BlockSpec(shape, lambda *_: (0,) * len(shape))


SCALARS = pl.BlockSpec(memory_space=pltpu.SMEM)


def takes(microseconds):
    return pl.CostEstimate(flops=int(microseconds * 1e6), bytes_accessed=0, transcendentals=0)


def gather_masks(order):
    masks = [(0, 0)]
    for axis, bit in order:
        step = (bit, 0) if axis == "seq" else (0, bit)
        masks = masks + [(s ^ step[0], t ^ step[1]) for s, t in masks]
    return tuple(masks)


def beyond(masks):
    return tuple((s, t ^ 1) for s, t in masks)


def block_at(me_ref, mask, reps, rows):
    block = (me_ref[0] ^ mask[0]) * reps + (me_ref[1] ^ mask[1])
    return pl.ds(pl.multiple_of(block * rows, rows), rows)


def place_blocks(me_ref, refs, target, plans, reps):
    if plans is None:
        target[...] = refs[0][...]
        return
    for ref, (first, last, masks) in zip(refs, plans):
        for k, mask in enumerate(masks):
            where = block_at(me_ref, mask, reps, ref.shape[2])
            target[first:last, where, :] = ref[k, : last - first]


def take_blocks(me_ref, source, outs, plans, reps, rows):
    if plans is None:
        outs[0][...] = source[...].astype(BF)
        return
    for out, parts in zip(outs, plans):
        at = 0
        for first, last, masks in parts:
            for mask in masks:
                where = block_at(me_ref, mask, reps, rows)
                out[at : at + last - first] = source[first:last, where, :].astype(BF)
                at += last - first


def attend_kernel(plans, reps, me_ref, x_ref, pos_ref, ids_row, ids_col, *refs):
    count = 1 if plans is None else len(plans)
    pieces = refs[:count]
    qkv_ref, mixed_ref, lse_ref, bias, w_ref = refs[count:]
    win, width = pos_ref.shape
    dim = width // H
    tile = w_ref.shape[2]


    @pl.when(pl.program_id(0) == 0)
    def _():
        place_blocks(me_ref, pieces, w_ref, plans, reps)

    hidden = x_ref[...].reshape(win, width).astype(F32) + pos_ref[...]
    low = hidden.astype(BF)
    for t in range(w_ref.shape[0]):
        qkv_ref[0, :, t * tile : (t + 1) * tile] = nn(low, w_ref[t]).astype(BF)
    row = lax.broadcasted_iota(jnp.int32, (win, win), 0)
    col = lax.broadcasted_iota(jnp.int32, (win, win), 1)
    allowed = (ids_col[0] == ids_row[0]) & (col >= row)
    bias[...] = jnp.where(allowed, 0.0, MASKED)
    ones = jnp.ones((win, dim), BF)
    blocks = [(lo, lo + QUERIES) for lo in range(0, win, QUERIES)]

    def score(h):
        base = 3 * dim * h
        query = qkv_ref[0, :, base : base + dim] * (dim**-0.5)
        keys = qkv_ref[0, :, base + dim : base + 2 * dim]
        return [nt(keys[:hi], query[lo:hi]) + bias[:hi, lo:hi] for lo, hi in blocks]

    def mix(h, scores):
        base = 3 * dim * h
        values = jnp.concatenate([qkv_ref[0, :, base + 2 * dim : base + 3 * dim], ones], axis=1)
        values = values.T[: dim + 16]
        parts, logs = [], []
        for some in scores:
            highest = jnp.max(some, axis=0, keepdims=True)
            both = nn(values[:, : some.shape[0]], jnp.exp(some - highest).astype(BF))
            total = both[dim : dim + 1]
            parts.append(both[:dim] / total)
            logs.append(highest + jnp.log(total))
        lse_ref[0, h : h + 1] = jnp.concatenate(logs, axis=1)
        return jnp.concatenate(parts, axis=1).astype(BF)

    outs = []
    scores = score(0)
    for h in range(H):
        later = score(h + 1) if h + 1 < H else None
        outs.append(mix(h, scores))
        scores = later
    mixed_ref[0] = jnp.concatenate(outs, axis=0).T


def attend_forward(me, x, positions, ids, w, plans, tiles, tile, reps):
    group, wins, span, width = x.shape
    win = group * span
    return pl.pallas_call(
        functools.partial(attend_kernel, plans, reps),
        grid=(wins,),
        in_specs=[
            SCALARS,
            pl.BlockSpec((group, 1, span, width), lambda i: (0, i, 0, 0)),
            same((win, width)),
            pl.BlockSpec((1, 1, win), lambda i: (i, 0, 0)),
            pl.BlockSpec((1, win, 1), lambda i: (i, 0, 0)),
        ]
        + [same(piece.shape) for piece in w],
        out_specs=[
            pl.BlockSpec((1, win, 3 * width), lambda i: (i, 0, 0)),
            pl.BlockSpec((1, win, width), lambda i: (i, 0, 0)),
            pl.BlockSpec((1, H, win), lambda i: (i, 0, 0)),
        ],
        out_shape=[
            jax.ShapeDtypeStruct((wins, win, 3 * width), BF),
            jax.ShapeDtypeStruct((wins, win, width), BF),
            jax.ShapeDtypeStruct((wins, H, win), F32),
        ],
        scratch_shapes=[pltpu.VMEM((win, win), F32), pltpu.VMEM((tiles, width, tile), BF)],
        compiler_params=memory(28),
        cost_estimate=takes(18),
        name="attend_forward",
    )(me, x, positions, ids[:, None, :], ids[:, :, None], *w)


def middle_kernel(
    plans, out_plans, reps, rows, outs, wins, me_ref, x_ref, pos_ref, mixed_ref, cot_ref, norm_ref, moments_ref, *refs
):
    count = 1 if plans is None else len(plans)
    pieces = refs[:count]
    refs = refs[count:]
    result_ref, mid_ref, gmixed_ref, dnorm_ref = refs[:4]
    count = 1 if out_plans is None else 2
    grads = refs[4 : 4 + count]
    act, slope, gpre, w_ref, acc = refs[4 + count :]
    step = pl.program_id(0)
    last = wins - 1
    win, width = pos_ref.shape
    tile = w_ref.shape[2]
    ups = (w_ref.shape[0] - outs) // 2
    blocks = ups // 2
    up, down = outs, outs + ups

    @pl.when(step == 0)
    def _():
        place_blocks(me_ref, pieces, w_ref, plans, reps)
        acc[...] = jnp.zeros_like(acc)
        dnorm_ref[...] = jnp.zeros_like(dnorm_ref)
        if result_ref.shape[2] > (last + 1) * width:
            result_ref[:, :, (last + 1) * width :] = moments_ref[...]

    mixed = mixed_ref[0]
    hidden = x_ref[...].reshape(win, width).astype(F32) + pos_ref[...]
    attn = jnp.concatenate([nn(mixed, w_ref[t]) for t in range(outs)], axis=1)
    scaled_one, inverse_one = row_norm(hidden + attn)
    normed = scaled_one * norm_ref[0:1] + norm_ref[1:2]
    low = normed.astype(BF)
    for t in range(ups):
        pre = nn(low, w_ref[up + t])
        square = pre * pre
        lifted = 1.0 + jnp.tanh(pre * (GELU_A + GELU_A * GELU_B * square))
        halved = 0.5 * pre
        steep = halved * (GELU_A + 3.0 * GELU_A * GELU_B * square)
        act[:, t * tile : (t + 1) * tile] = (halved * lifted).astype(BF)
        slope[:, t * tile : (t + 1) * tile] = (lifted * (0.5 + steep * (2.0 - lifted))).astype(BF)
    branch = jnp.concatenate(
        [
            sum(nn(act[:, b * width : (b + 1) * width], w_ref[down + 2 * b + j]) for b in range(blocks))
            for j in range(2)
        ],
        axis=1,
    )
    scaled_two, inverse_two = row_norm(normed + branch)
    result = scaled_two * norm_ref[2:3] + norm_ref[3:4]
    result = result.astype(BF).reshape(*result_ref.shape[:2], width)
    for window in range(wins):

        @pl.when(step == window)
        def _():
            result_ref[:, :, window * width : (window + 1) * width] = result

    grad_resid, gain_two, shift_two = norm_pull(
        cot_ref[...].reshape(win, width).astype(F32), scaled_two, inverse_two, norm_ref[2:3]
    )
    gb = grad_resid.astype(BF)
    for b in range(blocks):
        cols = slice(b * width, (b + 1) * width)
        gact = nt(gb[:, :tile], w_ref[down + 2 * b]) + nt(gb[:, tile:], w_ref[down + 2 * b + 1])
        gpre[:, cols] = (gact * slope[:, cols].astype(F32)).astype(BF)
    grad_normed = grad_resid + sum(
        nt(gpre[:, t * tile : (t + 1) * tile], w_ref[up + t]) for t in range(ups)
    )
    grad_mid, gain_one, shift_one = norm_pull(grad_normed, scaled_one, inverse_one, norm_ref[0:1])
    mid_ref[0] = grad_mid
    ga = grad_mid.astype(BF)
    gmixed_ref[0] = sum(nt(ga[:, t * tile : (t + 1) * tile], w_ref[t]) for t in range(outs)).astype(BF)
    dnorm_ref[...] += jnp.concatenate([gain_one, shift_one, gain_two, shift_two], axis=0)
    for b in range(blocks):
        act_t = act[:, b * width : (b + 1) * width].T
        for j in range(2):
            acc[down + 2 * b + j] += nn(act_t, gb[:, j * tile : (j + 1) * tile])
    low_t = low.T
    for t in range(ups):
        acc[up + t] += nn(low_t, gpre[:, t * tile : (t + 1) * tile])
    mixed_t = mixed.T
    for t in range(outs):
        acc[t] += nn(mixed_t, ga[:, t * tile : (t + 1) * tile])

    @pl.when(step == last)
    def _():
        take_blocks(me_ref, acc, grads, out_plans, reps, rows)


def middle(me, x, positions, mixed, cot, norms, moments, together, w, plans, out_plans, grad_shapes, tiles, tile, reps, rows):
    group, wins, span, width = x.shape
    win = group * span
    outs = width // tile
    hidden = (tiles - outs) // 2 * tile
    sent = (group, span, wins * width + (moments.shape[2] if together else 0))
    seq_spec = pl.BlockSpec((group, 1, span, width), lambda i: (0, i, 0, 0))
    row_spec = pl.BlockSpec((1, win, width), lambda i: (i, 0, 0))
    return pl.pallas_call(
        functools.partial(middle_kernel, plans, out_plans, reps, rows, outs, wins),
        grid=(wins,),
        in_specs=[
            SCALARS,
            seq_spec,
            same((win, width)),
            row_spec,
            seq_spec,
            same(norms.shape),
            same(moments.shape),
        ]
        + [same(piece.shape) for piece in w],
        out_specs=[whole(sent), row_spec, row_spec, whole(norms.shape)]
        + [whole(shape) for shape in grad_shapes],
        out_shape=[
            jax.ShapeDtypeStruct(sent, BF),
            jax.ShapeDtypeStruct((wins, win, width), F32),
            jax.ShapeDtypeStruct((wins, win, width), BF),
            jax.ShapeDtypeStruct(norms.shape, F32),
        ]
        + [jax.ShapeDtypeStruct(shape, BF) for shape in grad_shapes],
        scratch_shapes=[
            pltpu.VMEM((win, hidden), BF),
            pltpu.VMEM((win, hidden), BF),
            pltpu.VMEM((win, hidden), BF),
            pltpu.VMEM((tiles, width, tile), BF),
            pltpu.VMEM((tiles, width, tile), F32),
        ],
        compiler_params=PARAMS,
        cost_estimate=takes(27),
        name="middle",
    )(me, x, positions, mixed, cot, norms, moments, *w)


def attend_back_kernel(
    plans,
    out_plans,
    reps,
    rows,
    behind,
    me_ref,
    x_ref,
    pos_ref,
    ids_row,
    ids_col,
    qkv_ref,
    lse_ref,
    gmixed_ref,
    mid_ref,
    dnorm_ref,
    *refs,
):
    count = 1 if plans is None else len(plans)
    pieces = refs[:count]
    ginput_ref = refs[count + behind]
    refs = refs[count + behind + 1 :]
    count = 1 if out_plans is None else 2
    grads = refs[:count]
    bias, gproj, w_ref, acc = refs[count:]
    step = pl.program_id(0)
    last = pl.num_programs(0) - 1
    win, width = pos_ref.shape
    dim = width // H
    tiles, _, tile = w_ref.shape
    factor = dim**-0.5
    half = win // 2

    @pl.when(step == 0)
    def _():
        place_blocks(me_ref, pieces, w_ref, plans, reps)
        acc[...] = jnp.zeros_like(acc)

    key = lax.broadcasted_iota(jnp.int32, (win, win), 0)
    query_at = lax.broadcasted_iota(jnp.int32, (win, win), 1)
    allowed = (ids_col[0] == ids_row[0]) & (query_at >= key)
    bias[...] = jnp.where(allowed, 0.0, MASKED)
    blocks = [(lo, lo + QUERIES) for lo in range(0, win, QUERIES)]

    def operands(h):
        base = 3 * dim * h
        query = qkv_ref[0, :, base : base + dim] * factor
        keys = qkv_ref[0, :, base + dim : base + 2 * dim]
        values = qkv_ref[0, :, base + 2 * dim : base + 3 * dim]
        return query, keys, values, gmixed_ref[0, :, h * dim : (h + 1) * dim]

    def score(h):
        query, keys, values, gout = operands(h)
        return [
            (nt(keys[:hi], query[lo:hi]) + bias[:hi, lo:hi], nt(values[:hi], gout[lo:hi])) for lo, hi in blocks
        ]

    def pull(h, scores):
        query, keys, _, gout = operands(h)
        keys_t = jnp.concatenate([keys, keys], axis=1).T[:dim]
        probs, gscores, gqueries = [], [], []
        for (lo, hi), (some, gprobs) in zip(blocks, scores):
            weights = jnp.exp(some - lse_ref[0, h : h + 1, lo:hi])
            inner = jnp.sum(weights * gprobs, axis=0, keepdims=True)
            gscore = (weights * (gprobs - inner)).astype(BF)
            probs.append(weights.astype(BF))
            gscores.append(gscore)
            gqueries.append(nn(keys_t[:, :hi], gscore))
        gkeys, gvalues = [], []
        for lo, hi in blocks:
            later = [i for i, (_, end) in enumerate(blocks) if end >= hi]
            gkeys.append(nn(jnp.concatenate([gscores[i][lo:hi] for i in later], axis=1), query[lo:]))
            gvalues.append(nn(jnp.concatenate([probs[i][lo:hi] for i in later], axis=1), gout[lo:]))
        gquery = jnp.concatenate(gqueries, axis=1) * factor
        return gquery.astype(BF), [jnp.concatenate(part, axis=0).astype(BF) for part in (gkeys, gvalues)]

    done = []
    scores = score(0)
    for h in range(H):
        later = score(h + 1) if h + 1 < H else None
        done.append(pull(h, scores))
        scores = later
        if h % 2:
            packed = jnp.concatenate([done[-2][0], done[-1][0]], axis=0).T
            parts = [packed[:, :dim], *done[-2][1], packed[:, dim:], *done[-1][1]]
            gproj[:, 3 * dim * (h - 1) : 3 * dim * (h + 1)] = jnp.concatenate(parts, axis=1)
    hidden = x_ref[...].reshape(win, width).astype(F32) + pos_ref[...]
    low_t = hidden.astype(BF).T
    total = mid_ref[0]
    for t in range(tiles):
        part = gproj[:, t * tile : (t + 1) * tile]
        acc[t] += nn(low_t, part)
        total += nt(part, w_ref[t])
    ginput_ref[...] = total.astype(BF).reshape(ginput_ref.shape)
    for j in range(width // tile):
        acc[tiles + j] += total[:, j * tile : (j + 1) * tile]

    @pl.when(step == last)
    def _():
        if out_plans is not None:
            small = jnp.concatenate(
                [dnorm_ref[:, j * tile : (j + 1) * tile] for j in range(width // tile)], axis=0
            )
            small = jnp.concatenate([small, jnp.zeros((rows - small.shape[0], tile), F32)], axis=0)
            for b in range(win // rows):
                acc[acc.shape[0] - 1, b * rows : (b + 1) * rows] = small
        take_blocks(me_ref, acc, grads, out_plans, reps, rows)


def attend_backward(
    me, x, positions, ids, qkv, lse, gmixed, mid, dnorm, behind, w, plans, out_plans, grad_shapes, tiles, tile, reps, rows
):
    group, wins, span, width = x.shape
    win = group * span
    seq_spec = pl.BlockSpec((group, 1, span, width), lambda i: (0, i, 0, 0))
    row_spec = pl.BlockSpec((1, win, width), lambda i: (i, 0, 0))
    return pl.pallas_call(
        functools.partial(attend_back_kernel, plans, out_plans, reps, rows, len(behind)),
        grid=(wins,),
        in_specs=[
            SCALARS,
            seq_spec,
            same((win, width)),
            pl.BlockSpec((1, 1, win), lambda i: (i, 0, 0)),
            pl.BlockSpec((1, win, 1), lambda i: (i, 0, 0)),
            pl.BlockSpec((1, win, 3 * width), lambda i: (i, 0, 0)),
            pl.BlockSpec((1, H, win), lambda i: (i, 0, 0)),
            row_spec,
            row_spec,
            same(dnorm.shape),
        ]
        + [same(piece.shape) for piece in w]
        + [pl.BlockSpec(memory_space=pl.ANY) for _ in behind],
        out_specs=[seq_spec] + [whole(shape) for shape in grad_shapes],
        out_shape=[jax.ShapeDtypeStruct(x.shape, BF)]
        + [jax.ShapeDtypeStruct(shape, BF) for shape in grad_shapes],
        scratch_shapes=[
            pltpu.VMEM((win, win), F32),
            pltpu.VMEM((win, 3 * width), BF),
            pltpu.VMEM((tiles, width, tile), BF),
            pltpu.VMEM((tiles + width // tile + 1, width, tile), F32),
        ],
        compiler_params=memory(30),
        cost_estimate=takes(22),
        name="attend_backward",
    )(me, x, positions, ids[:, None, :], ids[:, :, None], qkv, lse, gmixed, mid, dnorm, *w, *behind)


def right_kernel(rows_ref, right_ref, out_ref):
    seqs, _, _ = out_ref.shape
    slots, _, tile = rows_ref.shape
    cols = tile // seqs
    for s in range(slots):
        turned = nn(rows_ref[s], right_ref[s]).astype(BF)
        for j in range(seqs):
            out_ref[j, :, s * cols : (s + 1) * cols] = turned[:, j * cols : (j + 1) * cols]


def right_turn(rows, right, seqs):
    slots, rows_dev, tile = rows.shape
    return pl.pallas_call(
        right_kernel,
        out_shape=jax.ShapeDtypeStruct((seqs, rows_dev, slots * tile // seqs), BF),
        compiler_params=memory(16),
        cost_estimate=takes(3),
        name="right_turn",
    )(rows, right)


def left_kernel(x_ref, moments_ref, left_ref, out_ref):
    seqs, rows_dev, wide = x_ref.shape
    slots, width, _ = left_ref.shape
    cols = wide // slots
    x = x_ref[...].reshape(width, wide)
    at = moments_ref.shape[2] - 2 * wide
    moments = moments_ref[:, :, at:].reshape(width, 2 * wide).astype(F32)
    spare = -wide % 128
    x_t = jnp.concatenate([x, jnp.zeros((width, spare), BF)], axis=1).T
    turned = [nn(x_t[s * cols : (s + 1) * cols], left_ref[s]) for s in range(slots)]
    turned = jnp.concatenate(turned + [jnp.zeros((spare, width), F32)], axis=0).T[:, :wide]
    direction = adam_step(turned, moments[:, :wide], moments[:, wide:])[2].astype(BF)
    change = [nn(left_ref[s], direction[:, s * cols : (s + 1) * cols]) for s in range(slots)]
    out = jnp.concatenate(change + [turned], axis=1).astype(BF)
    out_ref[...] = out.reshape(out_ref.shape)


def left_turns(x, moments, left):
    seqs, rows_dev, wide = x.shape
    return pl.pallas_call(
        left_kernel,
        out_shape=jax.ShapeDtypeStruct((seqs, rows_dev, 2 * wide), BF),
        compiler_params=PARAMS,
        cost_estimate=takes(3),
        name="left_turns",
    )(x, moments, left)


def last_kernel(back_ref, right_ref, w_ref, one_ref, two_ref, new_one, new_two, new_w):
    seqs, rows_dev, _ = back_ref.shape
    slots, _, tile = w_ref.shape
    cols = tile // seqs
    for s in range(slots):

        def columns(first):
            return jnp.concatenate(
                [back_ref[j, :, first + s * cols : first + (s + 1) * cols] for j in range(seqs)], axis=1
            )

        change = nt(columns(0), right_ref[s])
        turned = columns(slots * cols).astype(F32)
        new_one[s], new_two[s], _ = adam_step(turned, one_ref[s], two_ref[s])
        old = w_ref[s]
        new_w[s] = old - LEARN * (change + DECAY * old)


def last_turn(back, right, weights, one, two):
    shape = jax.ShapeDtypeStruct(weights.shape, F32)
    return pl.pallas_call(
        last_kernel,
        out_shape=[shape, shape, shape],
        compiler_params=memory(16),
        cost_estimate=takes(3),
        name="last_turn",
    )(back, right, weights, one, two)


def columns_kernel(one_ref, two_ref, out_ref):
    seqs = out_ref.shape[0]
    slots, _, tile = one_ref.shape
    cols = tile // seqs
    for first, ref in ((0, one_ref), (slots, two_ref)):
        for s in range(slots):
            values = ref[s].astype(BF)
            for j in range(seqs):
                at = (first + s) * cols
                out_ref[j, :, at : at + cols] = values[:, j * cols : (j + 1) * cols]


def moment_columns(one, two, seqs):
    slots, rows_dev, tile = one.shape
    return pl.pallas_call(
        columns_kernel,
        out_shape=jax.ShapeDtypeStruct((seqs, rows_dev, 2 * slots * tile // seqs), BF),
        compiler_params=PARAMS,
        cost_estimate=takes(3000),
        name="moment_columns",
    )(one, two)


def bases_kernel(left_ref, right_ref, low_left, low_right):
    low_left[...] = left_ref[...].astype(BF)
    low_right[...] = right_ref[...].astype(BF)


def low_bases(left, right):
    slots, width, _ = left.shape
    tile = right.shape[1]
    some = 3 if slots % 3 == 0 else 1
    big = pl.BlockSpec((some, width, width), lambda i: (i, 0, 0))
    little = pl.BlockSpec((some, tile, tile), lambda i: (i, 0, 0))
    return pl.pallas_call(
        bases_kernel,
        grid=(slots // some,),
        in_specs=[big, little],
        out_specs=[big, little],
        out_shape=[
            jax.ShapeDtypeStruct(left.shape, BF),
            jax.ShapeDtypeStruct(right.shape, BF),
        ],
        compiler_params=PARAMS,
        cost_estimate=takes(3),
        name="low_bases",
    )(left, right)


def swap(x, axis, bit):
    size = lax.axis_size(axis)
    return lax.ppermute(x, axis, [(i, i ^ bit) for i in range(size)])


def exchange(x, axis, group):
    size = lax.axis_size(axis)
    groups = None
    if group != size:
        groups = [[base + i for i in range(group)] for base in range(0, size, group)]
    return lax.all_to_all(x, axis, 0, 0, axis_index_groups=groups, tiled=True)


def after(x, *others):
    return lax.optimization_barrier((x,) + others)[0]


def powers(first, size):
    bits = []
    while first < size:
        bits.append(first)
        first *= 2
    return bits


def gather(block, order):
    own = block[None]
    for axis, bit in order[:-1]:
        own = jnp.concatenate([own, swap(own, axis, bit)], axis=0)
    return own, swap(own, *order[-1])


def add(a, b, *others):
    if others:
        b = after(b, *others)
    return (a.astype(F32) + b.astype(F32)).astype(BF)


def double(buf, axis, bit, *others):
    got = swap(buf, axis, bit)
    if others:
        got = after(got, *others)
    return jnp.concatenate([buf, got], axis=0)


def halve(buf, axis, bit, *others):
    cut = buf.shape[0] // 2
    return add(buf[:cut], swap(buf[cut:], axis, bit), *others)


def body(
    inputs,
    cotangent,
    segments,
    owners,
    weights,
    left_bases,
    right_bases,
    moment_one,
    moment_two,
    norm_params,
    norm_one,
    norm_two,
    positions,
    pos_one,
    pos_two,
):
    seqs = lax.axis_size("seq")
    reps = lax.axis_size("rep")
    me_s = lax.axis_index("seq")
    me_r = lax.axis_index("rep")
    me = jnp.stack([me_s, me_r]).astype(jnp.int32)
    seq_local, span, width = inputs.shape
    rows_dev, slots, tile = weights.shape
    tiles = owners.shape[0]
    rows = rows_dev // reps
    group = WIN // span
    place = me_s % group
    wins = seq_local // group
    aligned = rows % 16 == 0
    blocks = seqs * reps
    seq_bits = [("seq", b) for b in powers(1, seqs)[::-1]]
    far_bits = [("rep", b) for b in powers(2, reps)]
    core_bit = [("rep", 1)]

    low_w = weights.astype(BF).transpose(1, 0, 2).reshape(slots, reps, rows, tile).transpose(1, 0, 2, 3)
    near = [lax.dynamic_index_in_dim(low_w, me_r, 0, keepdims=False)]
    for k in range(1, reps):
        near.append(swap(lax.dynamic_index_in_dim(low_w, me_r ^ k, 0, keepdims=False), "rep", k))
    near = jnp.concatenate(near, axis=0)
    near = jnp.take(near, ((owners // slots) ^ me_r) * slots + owners % slots, axis=0)
    ids = segments.reshape(-1)
    id_tiles = -(-2 * ids.shape[0] // (rows * tile))
    ids = jnp.concatenate([ids // 64, ids % 64]).astype(BF)
    ids = jnp.pad(ids, (0, id_tiles * rows * tile - ids.shape[0])).reshape(id_tiles, rows, tile)

    qkv_tiles = 3 * width // tile
    rest_tiles = tiles - qkv_tiles
    qkv_at, rest_at = qkv_tiles // 2, rest_tiles // 2
    split = qkv_at + id_tiles
    by_slot = [values.transpose(1, 0, 2) for values in (weights, moment_one, moment_two)]
    rest = near[qkv_tiles:][None]
    near = jnp.concatenate([near[:qkv_at], ids, near[qkv_at:qkv_tiles]], axis=0)[None]
    moments = moment_columns(after(by_slot[1], near), by_slot[2], seqs)
    for i, step in enumerate(seq_bits[:-1]):
        near = double(near, *step, *([moments] if i == 0 else []))
        rest = double(after(rest, moments) if i == 0 else rest, *step, near)
        if i == 0:
            x = after(inputs, near)
    x = exchange(x, "seq", group)
    cot = exchange(after(cotangent, x), "seq", group).reshape(group, wins, span, width)
    x = x.reshape(group, wins, span, width)

    def table_of(masks):
        table = np.zeros(blocks, np.int32)
        for k, (s, t) in enumerate(masks):
            table[s * reps + t] = k
        return jnp.asarray(table)

    orders = [seq_bits[-1:] + far_bits, far_bits + seq_bits[-1:]]

    def pieces_of(bufs, ranges):
        pieces, plans = [], []
        for buf, order, (first, last) in zip(bufs, orders, ranges):
            masks = gather_masks(seq_bits[:-1] + order)
            pieces += [buf, swap(buf, *core_bit[0])]
            plans += [(first, last, masks), (first, last, beyond(masks))]
        return settle(pieces, plans)

    def settle(pieces, plans):
        if aligned:
            return pieces, plans
        at = jnp.arange(blocks)
        full = []
        for i in range(0, len(pieces), 2):
            count = plans[i][1] - plans[i][0]
            table = table_of(plans[i][2] + plans[i + 1][2])
            both = jnp.concatenate([pieces[i][:, :count], pieces[i + 1][:, :count]], axis=0)
            both = jnp.take(both, table[((at // reps) ^ me_s) * reps + ((at % reps) ^ me_r)], axis=0)
            full.append(both.transpose(1, 0, 2, 3).reshape(count, blocks * rows, tile))
        return [jnp.concatenate(full, axis=0)], None

    bufs = [near[:, :split], near[:, split:]]
    bufs = [double(buf, *order[0]) for buf, order in zip(bufs, orders)]
    ids = bufs[0][:, qkv_at:]
    rest = after(rest, *bufs)
    for i in range(1, len(orders[0])):
        bufs = [double(buf, *order[i]) for buf, order in zip(bufs, orders)]
    w_qkv, qkv_plans = pieces_of(bufs, [(0, qkv_at), (qkv_at, qkv_tiles)])
    rest = [rest[:, :rest_at], rest[:, rest_at:]]
    rest = [double(buf, *order[0], *bufs) for buf, order in zip(rest, orders)]

    ids = ids.reshape(seqs, -1)[:, : 2 * seq_local * span].astype(jnp.int32)
    ids = (ids[:, : seq_local * span] * 64 + ids[:, seq_local * span :]).reshape(seqs, seq_local, span)
    spots = [0] * seqs
    for k, (s, _) in enumerate(gather_masks(seq_bits[:-1] + seq_bits[-1:])):
        spots[s] = k
    ids = jnp.take(ids, jnp.asarray(spots[:group])[jnp.arange(group) ^ place], axis=0)
    ids = lax.dynamic_slice_in_dim(ids, place * wins, wins, 1)
    ids = ids.transpose(1, 0, 2).reshape(wins, WIN)

    def scatter_plans(parts):
        count = parts[-1][1]
        if not aligned:
            return None, [(count, blocks * rows, tile)]
        own = [(first, last, gather_masks(order[:0:-1])) for first, last, order in parts]
        other = [(first, last, beyond(masks)) for first, last, masks in own]
        shape = (count * blocks // 2, rows, tile)
        return [own, other], [shape, shape]

    def scatter_tiles(grads, parts, *others):
        if not aligned:
            plain = grads[0].reshape(-1, blocks, rows, tile).transpose(1, 0, 2, 3)
            own, other = [], []
            for first, last, order in parts:
                masks = gather_masks(order[:0:-1])
                for target, some in ((own, masks), (other, beyond(masks))):
                    spots = np.array([s * reps + t for s, t in some])
                    at = ((spots // reps) ^ me_s) * reps + ((spots % reps) ^ me_r)
                    target.append(jnp.take(plain[:, first:last], at, axis=0).reshape(-1, rows, tile))
            grads = [jnp.concatenate(own, axis=0), jnp.concatenate(other, axis=0)]
        return add(grads[0], swap(grads[1], *core_bit[0]), *others)

    def cut_parts(buf, parts):
        out, at = [], 0
        for first, last, _ in parts:
            size = (last - first) * blocks // 2
            out.append(buf[at : at + size])
            at += size
        return out

    def join(bufs, parts):
        entries = 2 ** len(seq_bits[:-1])
        return jnp.concatenate([buf.reshape(entries, -1, rows, tile) for buf in bufs], axis=1)

    zyxc = seq_bits + far_bits + core_bit
    zxyc = seq_bits[:-1] + far_bits + seq_bits[-1:] + core_bit
    ahead = attend_forward(me, x, positions, ids, w_qkv, qkv_plans, qkv_tiles, tile, reps)
    for i in range(1, len(orders[0])):
        got = [swap(buf, *order[i]) for buf, order in zip(rest, orders)]
        qkv, mixed, lse, *got = lax.optimization_barrier((*ahead, *got))
        rest = [jnp.concatenate([buf, part], axis=0) for buf, part in zip(rest, got)]
    w_rest, rest_plans = pieces_of(rest, [(0, rest_at), (rest_at, rest_tiles)])
    rest_parts = [(0, rest_at, zyxc[::-1]), (rest_at, rest_tiles, zxyc[::-1])]
    out_plans, shapes = scatter_plans(rest_parts)
    result, mid, gmixed, d_norm, *d_rest = middle(
        me, x, positions, mixed, cot, norm_params, moments, group == seqs, w_rest, rest_plans, out_plans, shapes, rest_tiles, tile, reps, rows
    )
    result = exchange(result, "seq", group)
    rest = cut_parts(scatter_tiles(d_rest, rest_parts), rest_parts)
    steps = [[order[1 + i] for _, _, order in rest_parts] for i in range(len(orders[0]))]
    cuts = [buf.shape[0] // 2 for buf in rest]
    got = [swap(buf[cut:], *step) for buf, cut, step in zip(rest, cuts, steps[0])]

    qkv_total = qkv_tiles + width // tile + 1
    qkv_parts = [(0, 6, zyxc[::-1]), (6, qkv_total, zxyc[::-1])]
    out_plans, shapes = scatter_plans(qkv_parts)
    g_input, *d_qkv = attend_backward(
        me, x, positions, ids, qkv, lse, gmixed, mid, d_norm, rest,
        w_qkv, qkv_plans, out_plans, shapes, qkv_tiles, tile, reps, rows,
    )
    count = len(d_qkv)
    g_input, *some = lax.optimization_barrier((g_input, *d_qkv, *got))
    d_qkv, got = some[:count], some[count:]
    g_input = after(g_input, result)
    if group == seqs:
        moments = result
    else:
        moments = lax.all_to_all(after(moments, result), "seq", 0, 0, tiled=True)
    result = result[:, :, : wins * width].reshape(group, span, wins, width)
    result = result.transpose(0, 2, 1, 3).reshape(seq_local, span, width)
    rest = [add(buf[:cut], part) for buf, cut, part in zip(rest, cuts, got)]

    qkv_buf = scatter_tiles(d_qkv, qkv_parts)
    mine = cut_parts(qkv_buf, qkv_parts)
    low_left, low_right = low_bases(after(left_bases, qkv_buf), right_bases)
    mine = [halve(buf, *step, low_left) for buf, step in zip(mine, steps[0])]
    for some in steps[1:]:
        rest = [halve(buf, *step, *mine) for buf, step in zip(rest, some)]
        mine = [halve(buf, *step, *rest) for buf, step in zip(mine, some)]
    rest, mine = join(rest, rest_parts), join(mine, qkv_parts)
    for step in seq_bits[-2::-1]:
        rest = halve(rest, *step, mine)
        mine = halve(mine, *step, rest)
    rest, mine = rest[0], mine[0]
    g_input = exchange(g_input.reshape(seq_local, span, width), "seq", group)

    small = mine[qkv_tiles:]
    grad_norms = small[-1, : 4 * width // tile].astype(F32)
    sums = jnp.concatenate([mine[:qkv_tiles], rest], axis=0)
    tile_of = jnp.sum(
        jnp.where(owners[None, :] == jnp.arange(tiles)[:, None], jnp.arange(tiles)[None, :], 0), axis=1
    )
    sums = jnp.take(sums, tile_of, axis=0).reshape(reps, slots, rows, tile)
    g_input = after(g_input, sums).astype(F32)
    small = small[: width // tile]
    near = []
    for k in range(reps):
        part = lax.dynamic_index_in_dim(sums, me_r ^ k, 0, keepdims=False)
        part = jnp.concatenate([part, small], axis=0)
        near.append(swap(part, "rep", k) if k else part)
    sums = jnp.take(jnp.stack(near), jnp.arange(reps) ^ me_r, axis=0)
    sums = sums.transpose(1, 0, 2, 3).reshape(-1, rows_dev, tile)
    small = sums[slots:]
    sums = sums[:slots]

    turned = right_turn(sums, low_right, seqs)
    small = after(small, turned)
    turned = lax.all_to_all(after(turned, g_input), "seq", 0, 0, tiled=True)
    back = left_turns(turned, moments, low_left)
    news = last_turn(lax.all_to_all(back, "seq", 0, 0, tiled=True), low_right, *by_slot)
    first_new, second_new, new_weights = [values.transpose(1, 0, 2) for values in news]

    own = small[None]
    for i, step in enumerate(seq_bits):
        own = double(own, *step, *([turned] if i == 0 else [back]))
    masks = gather_masks(seq_bits)
    table = np.zeros(seqs, np.int32)
    for k, (i, _) in enumerate(masks):
        table[i] = k
    grad_pos = jnp.take(own, jnp.asarray(table)[jnp.arange(seqs) ^ me_s], axis=0)
    grad_pos = grad_pos.transpose(0, 2, 1, 3).reshape(WIN, width).astype(F32)
    if aligned:
        grad_norms = grad_norms.reshape(width // tile, 4, tile).transpose(1, 0, 2).reshape(4, width)
    else:
        grad_norms = lax.psum(d_norm, ("seq", "rep"))
    norm_first, norm_second, norm_dir = adam_step(grad_norms, norm_one, norm_two)
    pos_first, pos_second, pos_dir = adam_step(grad_pos, pos_one, pos_two)
    return (
        result,
        g_input,
        first_new,
        second_new,
        new_weights,
        norm_first,
        norm_second,
        norm_params - LEARN_SMALL * norm_dir,
        pos_first,
        pos_second,
        positions - LEARN_SMALL * pos_dir,
    )


def solution(mesh):
    tokens = P("rep", "seq", None)
    slots = P("seq", "rep", None)
    bases = P("rep", None, None)
    return jax.shard_map(
        body,
        mesh=mesh,
        in_specs=(
            tokens,
            tokens,
            P("rep", "seq"),
            P(),
            slots,
            bases,
            bases,
            slots,
            slots,
            P(),
            P(),
            P(),
            P(),
            P(),
            P(),
        ),
        out_specs=(tokens, tokens, slots, slots, slots, P(), P(), P(), P(), P(), P()),
        check_vma=False,
    )
```

```python
import functools

import jax
import jax.numpy as jnp
import numpy as np
from jax import lax
from jax.experimental import pallas as pl
from jax.experimental.pallas import tpu as pltpu
from jax.sharding import PartitionSpec as P

H = 8
WIN = 512
STEP = 10

EPS_NORM = 1e-05
EPS_ADAM = 1e-08
BETA = 0.5
LEARN = 0.02
LEARN_SMALL = 0.2
DECAY = 0.01
MASKED = -1e30
QUERIES = 128

BF = jnp.bfloat16
F32 = jnp.float32
PARAMS = pltpu.CompilerParams(vmem_limit_bytes=58 * 1024 * 1024)
GELU_A = 0.7978845608028654
GELU_B = 0.044715


def nn(a, b):
    return lax.dot_general(a, b, (((1,), (0,)), ((), ())), preferred_element_type=F32)


def nt(a, b):
    return lax.dot_general(a, b, (((1,), (1,)), ((), ())), preferred_element_type=F32)


def tn(a, b):
    return lax.dot_general(a, b, (((0,), (0,)), ((), ())), preferred_element_type=F32)


def adam_step(gradient, first, second):
    first_new = BETA * first + (1.0 - BETA) * gradient
    second_new = BETA * second + (1.0 - BETA) * gradient * gradient
    fix = 1.0 - BETA**STEP
    direction = first_new / fix / (jnp.sqrt(second_new / fix) + EPS_ADAM)
    return (first_new, second_new, direction)


def row_norm(values):
    center = values - jnp.mean(values, axis=-1, keepdims=True)
    inverse = lax.rsqrt(jnp.mean(center * center, axis=-1, keepdims=True) + EPS_NORM)
    return center * inverse, inverse


def norm_pull(grad_rows, scaled, inverse, gain):
    scaled_grad = grad_rows * gain
    grad_input = inverse * (
        scaled_grad
        - jnp.mean(scaled_grad, axis=-1, keepdims=True)
        - scaled * jnp.mean(scaled_grad * scaled, axis=-1, keepdims=True)
    )
    grad_gain = jnp.sum(grad_rows * scaled, axis=0, keepdims=True)
    grad_shift = jnp.sum(grad_rows, axis=0, keepdims=True)
    return grad_input, grad_gain, grad_shift


def memory(mebibytes):
    return pltpu.CompilerParams(vmem_limit_bytes=mebibytes * 1024 * 1024)


def same(shape):
    return pl.BlockSpec(shape, lambda *_: (0,) * len(shape), pipeline_mode=pl.Buffered(1))


def whole(shape):
    return pl.BlockSpec(shape, lambda *_: (0,) * len(shape))


SCALARS = pl.BlockSpec(memory_space=pltpu.SMEM)


def takes(microseconds):
    return pl.CostEstimate(flops=int(microseconds * 1e6), bytes_accessed=0, transcendentals=0)


def gather_masks(order):
    masks = [(0, 0)]
    for axis, bit in order:
        step = (bit, 0) if axis == "seq" else (0, bit)
        masks = masks + [(s ^ step[0], t ^ step[1]) for s, t in masks]
    return tuple(masks)


def beyond(masks):
    return tuple((s, t ^ 1) for s, t in masks)


def block_at(me_ref, mask, reps, rows):
    block = (me_ref[0] ^ mask[0]) * reps + (me_ref[1] ^ mask[1])
    return pl.ds(pl.multiple_of(block * rows, rows), rows)


def place_blocks(me_ref, refs, target, plans, reps):
    if plans is None:
        target[...] = refs[0][...]
        return
    for ref, (first, last, masks) in zip(refs, plans):
        for k, mask in enumerate(masks):
            where = block_at(me_ref, mask, reps, ref.shape[2])
            target[first:last, where, :] = ref[k, : last - first]


def take_blocks(me_ref, source, outs, plans, reps, rows):
    if plans is None:
        outs[0][...] = source[...].astype(BF)
        return
    for out, parts in zip(outs, plans):
        at = 0
        for first, last, masks in parts:
            for mask in masks:
                where = block_at(me_ref, mask, reps, rows)
                out[at : at + last - first] = source[first:last, where, :].astype(BF)
                at += last - first


def attend_kernel(plans, reps, me_ref, x_ref, pos_ref, ids_row, ids_col, *refs):
    count = 1 if plans is None else len(plans)
    pieces = refs[:count]
    qkv_ref, mixed_ref, lse_ref, bias, w_ref = refs[count:]
    win, width = pos_ref.shape
    dim = width // H
    tile = w_ref.shape[2]


    @pl.when(pl.program_id(0) == 0)
    def _():
        place_blocks(me_ref, pieces, w_ref, plans, reps)

    hidden = x_ref[...].reshape(win, width).astype(F32) + pos_ref[...]
    low = hidden.astype(BF)
    for t in range(w_ref.shape[0]):
        qkv_ref[0, :, t * tile : (t + 1) * tile] = nn(low, w_ref[t]).astype(BF)
    row = lax.broadcasted_iota(jnp.int32, (win, win), 0)
    col = lax.broadcasted_iota(jnp.int32, (win, win), 1)
    allowed = (ids_col[0] == ids_row[0]) & (col >= row)
    bias[...] = jnp.where(allowed, 0.0, MASKED)
    ones = jnp.ones((win, dim), BF)
    blocks = [(lo, lo + QUERIES) for lo in range(0, win, QUERIES)]

    def score(h):
        base = 3 * dim * h
        query = qkv_ref[0, :, base : base + dim] * (dim**-0.5)
        keys = qkv_ref[0, :, base + dim : base + 2 * dim]
        return [nt(keys[:hi], query[lo:hi]) + bias[:hi, lo:hi] for lo, hi in blocks]

    def mix(h, scores):
        base = 3 * dim * h
        values = jnp.concatenate([qkv_ref[0, :, base + 2 * dim : base + 3 * dim], ones], axis=1)
        values = values.T[: dim + 16]
        parts, logs = [], []
        for some in scores:
            highest = jnp.max(some, axis=0, keepdims=True)
            both = nn(values[:, : some.shape[0]], jnp.exp(some - highest).astype(BF))
            total = both[dim : dim + 1]
            parts.append(both[:dim] / total)
            logs.append(highest + jnp.log(total))
        lse_ref[0, h : h + 1] = jnp.concatenate(logs, axis=1)
        return jnp.concatenate(parts, axis=1).astype(BF)

    outs = []
    scores = score(0)
    for h in range(H):
        later = score(h + 1) if h + 1 < H else None
        outs.append(mix(h, scores))
        scores = later
    mixed_ref[0] = jnp.concatenate(outs, axis=0).T


def attend_forward(me, x, positions, ids, w, plans, tiles, tile, reps):
    group, wins, span, width = x.shape
    win = group * span
    return pl.pallas_call(
        functools.partial(attend_kernel, plans, reps),
        grid=(wins,),
        in_specs=[
            SCALARS,
            pl.BlockSpec((group, 1, span, width), lambda i: (0, i, 0, 0)),
            same((win, width)),
            pl.BlockSpec((1, 1, win), lambda i: (i, 0, 0)),
            pl.BlockSpec((1, win, 1), lambda i: (i, 0, 0)),
        ]
        + [same(piece.shape) for piece in w],
        out_specs=[
            pl.BlockSpec((1, win, 3 * width), lambda i: (i, 0, 0)),
            pl.BlockSpec((1, win, width), lambda i: (i, 0, 0)),
            pl.BlockSpec((1, H, win), lambda i: (i, 0, 0)),
        ],
        out_shape=[
            jax.ShapeDtypeStruct((wins, win, 3 * width), BF),
            jax.ShapeDtypeStruct((wins, win, width), BF),
            jax.ShapeDtypeStruct((wins, H, win), F32),
        ],
        scratch_shapes=[pltpu.VMEM((win, win), F32), pltpu.VMEM((tiles, width, tile), BF)],
        compiler_params=memory(28),
        cost_estimate=takes(18),
        name="attend_forward",
    )(me, x, positions, ids[:, None, :], ids[:, :, None], *w)


def middle_kernel(
    plans, out_plans, reps, rows, outs, wins, me_ref, x_ref, pos_ref, mixed_ref, cot_ref, norm_ref, moments_ref, *refs
):
    count = 1 if plans is None else len(plans)
    pieces = refs[:count]
    refs = refs[count:]
    result_ref, mid_ref, gmixed_ref, dnorm_ref = refs[:4]
    count = 1 if out_plans is None else 2
    grads = refs[4 : 4 + count]
    act, slope, gpre, w_ref, acc = refs[4 + count :]
    step = pl.program_id(0)
    last = wins - 1
    win, width = pos_ref.shape
    tile = w_ref.shape[2]
    ups = (w_ref.shape[0] - outs) // 2
    blocks = ups // 2
    up, down = outs, outs + ups

    @pl.when(step == 0)
    def _():
        place_blocks(me_ref, pieces, w_ref, plans, reps)
        acc[...] = jnp.zeros_like(acc)
        dnorm_ref[...] = jnp.zeros_like(dnorm_ref)
        if result_ref.shape[2] > (last + 1) * width:
            result_ref[:, :, (last + 1) * width :] = moments_ref[...]

    mixed = mixed_ref[0]
    hidden = x_ref[...].reshape(win, width).astype(F32) + pos_ref[...]
    attn = jnp.concatenate([nn(mixed, w_ref[t]) for t in range(outs)], axis=1)
    scaled_one, inverse_one = row_norm(hidden + attn)
    normed = scaled_one * norm_ref[0:1] + norm_ref[1:2]
    low = normed.astype(BF)
    for t in range(ups):
        pre = nn(low, w_ref[up + t])
        square = pre * pre
        lifted = 1.0 + jnp.tanh(pre * (GELU_A + GELU_A * GELU_B * square))
        halved = 0.5 * pre
        steep = halved * (GELU_A + 3.0 * GELU_A * GELU_B * square)
        act[:, t * tile : (t + 1) * tile] = (halved * lifted).astype(BF)
        slope[:, t * tile : (t + 1) * tile] = (lifted * (0.5 + steep * (2.0 - lifted))).astype(BF)
    branch = jnp.concatenate(
        [
            sum(nn(act[:, b * width : (b + 1) * width], w_ref[down + 2 * b + j]) for b in range(blocks))
            for j in range(2)
        ],
        axis=1,
    )
    scaled_two, inverse_two = row_norm(normed + branch)
    result = scaled_two * norm_ref[2:3] + norm_ref[3:4]
    result = result.astype(BF).reshape(*result_ref.shape[:2], width)
    for window in range(wins):

        @pl.when(step == window)
        def _():
            result_ref[:, :, window * width : (window + 1) * width] = result

    grad_resid, gain_two, shift_two = norm_pull(
        cot_ref[...].reshape(win, width).astype(F32), scaled_two, inverse_two, norm_ref[2:3]
    )
    gb = grad_resid.astype(BF)
    for b in range(blocks):
        cols = slice(b * width, (b + 1) * width)
        gact = nt(gb[:, :tile], w_ref[down + 2 * b]) + nt(gb[:, tile:], w_ref[down + 2 * b + 1])
        gpre[:, cols] = (gact * slope[:, cols].astype(F32)).astype(BF)
    grad_normed = grad_resid + sum(
        nt(gpre[:, t * tile : (t + 1) * tile], w_ref[up + t]) for t in range(ups)
    )
    grad_mid, gain_one, shift_one = norm_pull(grad_normed, scaled_one, inverse_one, norm_ref[0:1])
    ga = grad_mid.astype(BF)
    mid_ref[0] = ga
    gmixed_ref[0] = sum(nt(ga[:, t * tile : (t + 1) * tile], w_ref[t]) for t in range(outs)).astype(BF)
    dnorm_ref[...] += jnp.concatenate([gain_one, shift_one, gain_two, shift_two], axis=0)
    for b in range(blocks):
        act_t = act[:, b * width : (b + 1) * width].T
        for j in range(2):
            acc[down + 2 * b + j] += nn(act_t, gb[:, j * tile : (j + 1) * tile])
    low_t = low.T
    for t in range(ups):
        acc[up + t] += nn(low_t, gpre[:, t * tile : (t + 1) * tile])
    mixed_t = mixed.T
    for t in range(outs):
        acc[t] += nn(mixed_t, ga[:, t * tile : (t + 1) * tile])

    @pl.when(step == last)
    def _():
        take_blocks(me_ref, acc, grads, out_plans, reps, rows)


def middle(me, x, positions, mixed, cot, norms, moments, together, w, plans, out_plans, grad_shapes, tiles, tile, reps, rows):
    group, wins, span, width = x.shape
    win = group * span
    outs = width // tile
    hidden = (tiles - outs) // 2 * tile
    sent = (group, span, wins * width + (moments.shape[2] if together else 0))
    seq_spec = pl.BlockSpec((group, 1, span, width), lambda i: (0, i, 0, 0))
    row_spec = pl.BlockSpec((1, win, width), lambda i: (i, 0, 0))
    return pl.pallas_call(
        functools.partial(middle_kernel, plans, out_plans, reps, rows, outs, wins),
        grid=(wins,),
        in_specs=[
            SCALARS,
            seq_spec,
            same((win, width)),
            row_spec,
            seq_spec,
            same(norms.shape),
            same(moments.shape),
        ]
        + [same(piece.shape) for piece in w],
        out_specs=[whole(sent), row_spec, row_spec, whole(norms.shape)]
        + [whole(shape) for shape in grad_shapes],
        out_shape=[
            jax.ShapeDtypeStruct(sent, BF),
            jax.ShapeDtypeStruct((wins, win, width), BF),
            jax.ShapeDtypeStruct((wins, win, width), BF),
            jax.ShapeDtypeStruct(norms.shape, F32),
        ]
        + [jax.ShapeDtypeStruct(shape, BF) for shape in grad_shapes],
        scratch_shapes=[
            pltpu.VMEM((win, hidden), BF),
            pltpu.VMEM((win, hidden), BF),
            pltpu.VMEM((win, hidden), BF),
            pltpu.VMEM((tiles, width, tile), BF),
            pltpu.VMEM((tiles, width, tile), F32),
        ],
        compiler_params=PARAMS,
        cost_estimate=takes(27),
        name="middle",
    )(me, x, positions, mixed, cot, norms, moments, *w)


def attend_back_kernel(
    plans,
    out_plans,
    reps,
    rows,
    behind,
    me_ref,
    x_ref,
    pos_ref,
    ids_row,
    ids_col,
    qkv_ref,
    lse_ref,
    gmixed_ref,
    mid_ref,
    dnorm_ref,
    *refs,
):
    count = 1 if plans is None else len(plans)
    pieces = refs[:count]
    ginput_ref = refs[count + behind]
    refs = refs[count + behind + 1 :]
    count = 1 if out_plans is None else 2
    grads = refs[:count]
    bias, gproj, w_ref, acc = refs[count:]
    step = pl.program_id(0)
    last = pl.num_programs(0) - 1
    win, width = pos_ref.shape
    dim = width // H
    tiles, _, tile = w_ref.shape
    factor = dim**-0.5
    half = win // 2

    @pl.when(step == 0)
    def _():
        place_blocks(me_ref, pieces, w_ref, plans, reps)
        acc[...] = jnp.zeros_like(acc)

    key = lax.broadcasted_iota(jnp.int32, (win, win), 0)
    query_at = lax.broadcasted_iota(jnp.int32, (win, win), 1)
    allowed = (ids_col[0] == ids_row[0]) & (query_at >= key)
    bias[...] = jnp.where(allowed, 0.0, MASKED)
    blocks = [(lo, lo + QUERIES) for lo in range(0, win, QUERIES)]

    def operands(h):
        base = 3 * dim * h
        query = qkv_ref[0, :, base : base + dim] * factor
        keys = qkv_ref[0, :, base + dim : base + 2 * dim]
        values = qkv_ref[0, :, base + 2 * dim : base + 3 * dim]
        return query, keys, values, gmixed_ref[0, :, h * dim : (h + 1) * dim]

    def score(h):
        query, keys, values, gout = operands(h)
        return [
            (nt(keys[:hi], query[lo:hi]) + bias[:hi, lo:hi], nt(values[:hi], gout[lo:hi])) for lo, hi in blocks
        ]

    def pull(h, scores):
        query, keys, _, gout = operands(h)
        keys_t = jnp.concatenate([keys, keys], axis=1).T[:dim]
        probs, gscores, gqueries = [], [], []
        for (lo, hi), (some, gprobs) in zip(blocks, scores):
            weights = jnp.exp(some - lse_ref[0, h : h + 1, lo:hi])
            inner = jnp.sum(weights * gprobs, axis=0, keepdims=True)
            gscore = (weights * (gprobs - inner)).astype(BF)
            probs.append(weights.astype(BF))
            gscores.append(gscore)
            gqueries.append(nn(keys_t[:, :hi], gscore))
        gkeys, gvalues = [], []
        for lo, hi in blocks:
            later = [i for i, (_, end) in enumerate(blocks) if end >= hi]
            gkeys.append(nn(jnp.concatenate([gscores[i][lo:hi] for i in later], axis=1), query[lo:]))
            gvalues.append(nn(jnp.concatenate([probs[i][lo:hi] for i in later], axis=1), gout[lo:]))
        gquery = jnp.concatenate(gqueries, axis=1) * factor
        return gquery.astype(BF), [jnp.concatenate(part, axis=0).astype(BF) for part in (gkeys, gvalues)]

    done = []
    scores = score(0)
    for h in range(H):
        later = score(h + 1) if h + 1 < H else None
        done.append(pull(h, scores))
        scores = later
        if h % 2:
            packed = jnp.concatenate([done[-2][0], done[-1][0]], axis=0).T
            parts = [packed[:, :dim], *done[-2][1], packed[:, dim:], *done[-1][1]]
            gproj[:, 3 * dim * (h - 1) : 3 * dim * (h + 1)] = jnp.concatenate(parts, axis=1)
    hidden = x_ref[...].reshape(win, width).astype(F32) + pos_ref[...]
    low_t = hidden.astype(BF).T
    total = mid_ref[0].astype(F32)
    for t in range(tiles):
        part = gproj[:, t * tile : (t + 1) * tile]
        acc[t] += nn(low_t, part)
        total += nt(part, w_ref[t])
    ginput_ref[...] = total.astype(BF).reshape(ginput_ref.shape)
    for j in range(width // tile):
        acc[tiles + j] += total[:, j * tile : (j + 1) * tile]

    @pl.when(step == last)
    def _():
        if out_plans is not None:
            small = jnp.concatenate(
                [dnorm_ref[:, j * tile : (j + 1) * tile] for j in range(width // tile)], axis=0
            )
            small = jnp.concatenate([small, jnp.zeros((rows - small.shape[0], tile), F32)], axis=0)
            for b in range(win // rows):
                acc[acc.shape[0] - 1, b * rows : (b + 1) * rows] = small
        take_blocks(me_ref, acc, grads, out_plans, reps, rows)


def attend_backward(
    me, x, positions, ids, qkv, lse, gmixed, mid, dnorm, behind, w, plans, out_plans, grad_shapes, tiles, tile, reps, rows
):
    group, wins, span, width = x.shape
    win = group * span
    seq_spec = pl.BlockSpec((group, 1, span, width), lambda i: (0, i, 0, 0))
    row_spec = pl.BlockSpec((1, win, width), lambda i: (i, 0, 0))
    return pl.pallas_call(
        functools.partial(attend_back_kernel, plans, out_plans, reps, rows, len(behind)),
        grid=(wins,),
        in_specs=[
            SCALARS,
            seq_spec,
            same((win, width)),
            pl.BlockSpec((1, 1, win), lambda i: (i, 0, 0)),
            pl.BlockSpec((1, win, 1), lambda i: (i, 0, 0)),
            pl.BlockSpec((1, win, 3 * width), lambda i: (i, 0, 0)),
            pl.BlockSpec((1, H, win), lambda i: (i, 0, 0)),
            row_spec,
            row_spec,
            same(dnorm.shape),
        ]
        + [same(piece.shape) for piece in w]
        + [pl.BlockSpec(memory_space=pl.ANY) for _ in behind],
        out_specs=[seq_spec] + [whole(shape) for shape in grad_shapes],
        out_shape=[jax.ShapeDtypeStruct(x.shape, BF)]
        + [jax.ShapeDtypeStruct(shape, BF) for shape in grad_shapes],
        scratch_shapes=[
            pltpu.VMEM((win, win), F32),
            pltpu.VMEM((win, 3 * width), BF),
            pltpu.VMEM((tiles, width, tile), BF),
            pltpu.VMEM((tiles + width // tile + 1, width, tile), F32),
        ],
        compiler_params=memory(30),
        cost_estimate=takes(22),
        name="attend_backward",
    )(me, x, positions, ids[:, None, :], ids[:, :, None], qkv, lse, gmixed, mid, dnorm, *w, *behind)


def right_kernel(rows_ref, right_ref, out_ref):
    seqs, _, _ = out_ref.shape
    slots, _, tile = rows_ref.shape
    cols = tile // seqs
    for s in range(slots):
        turned = nn(rows_ref[s], right_ref[s]).astype(BF)
        for j in range(seqs):
            out_ref[j, :, s * cols : (s + 1) * cols] = turned[:, j * cols : (j + 1) * cols]


def right_turn(rows, right, seqs):
    slots, rows_dev, tile = rows.shape
    return pl.pallas_call(
        right_kernel,
        out_shape=jax.ShapeDtypeStruct((seqs, rows_dev, slots * tile // seqs), BF),
        compiler_params=memory(16),
        cost_estimate=takes(3),
        name="right_turn",
    )(rows, right)


def left_kernel(x_ref, moments_ref, left_ref, out_ref):
    seqs, rows_dev, wide = x_ref.shape
    slots, width, _ = left_ref.shape
    cols = wide // slots
    x = x_ref[...].reshape(width, wide)
    at = moments_ref.shape[2] - 2 * wide
    moments = moments_ref[:, :, at:].reshape(width, 2 * wide).astype(F32)
    spare = -wide % 128
    x_t = jnp.concatenate([x, jnp.zeros((width, spare), BF)], axis=1).T
    turned = [nn(x_t[s * cols : (s + 1) * cols], left_ref[s]) for s in range(slots)]
    turned = jnp.concatenate(turned + [jnp.zeros((spare, width), F32)], axis=0).T[:, :wide]
    direction = adam_step(turned, moments[:, :wide], moments[:, wide:])[2].astype(BF)
    change = [nn(left_ref[s], direction[:, s * cols : (s + 1) * cols]) for s in range(slots)]
    out = jnp.concatenate(change + [turned], axis=1).astype(BF)
    out_ref[...] = out.reshape(out_ref.shape)


def left_turns(x, moments, left):
    seqs, rows_dev, wide = x.shape
    return pl.pallas_call(
        left_kernel,
        out_shape=jax.ShapeDtypeStruct((seqs, rows_dev, 2 * wide), BF),
        compiler_params=PARAMS,
        cost_estimate=takes(3),
        name="left_turns",
    )(x, moments, left)


def last_kernel(back_ref, right_ref, w_ref, one_ref, two_ref, new_one, new_two, new_w):
    seqs, rows_dev, _ = back_ref.shape
    slots, _, tile = w_ref.shape
    cols = tile // seqs
    for s in range(slots):

        def columns(first):
            return jnp.concatenate(
                [back_ref[j, :, first + s * cols : first + (s + 1) * cols] for j in range(seqs)], axis=1
            )

        change = nt(columns(0), right_ref[s])
        turned = columns(slots * cols).astype(F32)
        new_one[s], new_two[s], _ = adam_step(turned, one_ref[s], two_ref[s])
        old = w_ref[s]
        new_w[s] = old - LEARN * (change + DECAY * old)


def last_turn(back, right, weights, one, two):
    shape = jax.ShapeDtypeStruct(weights.shape, F32)
    return pl.pallas_call(
        last_kernel,
        out_shape=[shape, shape, shape],
        compiler_params=memory(16),
        cost_estimate=takes(3),
        name="last_turn",
    )(back, right, weights, one, two)


def columns_kernel(one_ref, two_ref, out_ref):
    seqs = out_ref.shape[0]
    slots, _, tile = one_ref.shape
    cols = tile // seqs
    for first, ref in ((0, one_ref), (slots, two_ref)):
        for s in range(slots):
            values = ref[s].astype(BF)
            for j in range(seqs):
                at = (first + s) * cols
                out_ref[j, :, at : at + cols] = values[:, j * cols : (j + 1) * cols]


def moment_columns(one, two, seqs):
    slots, rows_dev, tile = one.shape
    return pl.pallas_call(
        columns_kernel,
        out_shape=jax.ShapeDtypeStruct((seqs, rows_dev, 2 * slots * tile // seqs), BF),
        compiler_params=PARAMS,
        cost_estimate=takes(3000),
        name="moment_columns",
    )(one, two)


def bases_kernel(left_ref, right_ref, low_left, low_right):
    low_left[...] = left_ref[...].astype(BF)
    low_right[...] = right_ref[...].astype(BF)


def low_bases(left, right):
    slots, width, _ = left.shape
    tile = right.shape[1]
    some = 3 if slots % 3 == 0 else 1
    big = pl.BlockSpec((some, width, width), lambda i: (i, 0, 0))
    little = pl.BlockSpec((some, tile, tile), lambda i: (i, 0, 0))
    return pl.pallas_call(
        bases_kernel,
        grid=(slots // some,),
        in_specs=[big, little],
        out_specs=[big, little],
        out_shape=[
            jax.ShapeDtypeStruct(left.shape, BF),
            jax.ShapeDtypeStruct(right.shape, BF),
        ],
        compiler_params=PARAMS,
        cost_estimate=takes(3),
        name="low_bases",
    )(left, right)


def swap(x, axis, bit):
    size = lax.axis_size(axis)
    return lax.ppermute(x, axis, [(i, i ^ bit) for i in range(size)])


def exchange(x, axis, group):
    size = lax.axis_size(axis)
    groups = None
    if group != size:
        groups = [[base + i for i in range(group)] for base in range(0, size, group)]
    return lax.all_to_all(x, axis, 0, 0, axis_index_groups=groups, tiled=True)


def after(x, *others):
    return lax.optimization_barrier((x,) + others)[0]


def powers(first, size):
    bits = []
    while first < size:
        bits.append(first)
        first *= 2
    return bits


def gather(block, order):
    own = block[None]
    for axis, bit in order[:-1]:
        own = jnp.concatenate([own, swap(own, axis, bit)], axis=0)
    return own, swap(own, *order[-1])


def add(a, b, *others):
    if others:
        b = after(b, *others)
    return (a.astype(F32) + b.astype(F32)).astype(BF)


def double(buf, axis, bit, *others):
    got = swap(buf, axis, bit)
    if others:
        got = after(got, *others)
    return jnp.concatenate([buf, got], axis=0)


def halve(buf, axis, bit, *others):
    cut = buf.shape[0] // 2
    return add(buf[:cut], swap(buf[cut:], axis, bit), *others)


def body(
    inputs,
    cotangent,
    segments,
    owners,
    weights,
    left_bases,
    right_bases,
    moment_one,
    moment_two,
    norm_params,
    norm_one,
    norm_two,
    positions,
    pos_one,
    pos_two,
):
    seqs = lax.axis_size("seq")
    reps = lax.axis_size("rep")
    me_s = lax.axis_index("seq")
    me_r = lax.axis_index("rep")
    me = jnp.stack([me_s, me_r]).astype(jnp.int32)
    seq_local, span, width = inputs.shape
    rows_dev, slots, tile = weights.shape
    tiles = owners.shape[0]
    rows = rows_dev // reps
    group = WIN // span
    place = me_s % group
    wins = seq_local // group
    aligned = rows % 16 == 0
    blocks = seqs * reps
    seq_bits = [("seq", b) for b in powers(1, seqs)[::-1]]
    far_bits = [("rep", b) for b in powers(2, reps)]
    core_bit = [("rep", 1)]

    low_w = weights.astype(BF).transpose(1, 0, 2).reshape(slots, reps, rows, tile).transpose(1, 0, 2, 3)
    near = [lax.dynamic_index_in_dim(low_w, me_r, 0, keepdims=False)]
    for k in range(1, reps):
        near.append(swap(lax.dynamic_index_in_dim(low_w, me_r ^ k, 0, keepdims=False), "rep", k))
    near = jnp.concatenate(near, axis=0)
    near = jnp.take(near, ((owners // slots) ^ me_r) * slots + owners % slots, axis=0)
    ids = segments.reshape(-1)
    id_tiles = -(-2 * ids.shape[0] // (rows * tile))
    ids = jnp.concatenate([ids // 64, ids % 64]).astype(BF)
    ids = jnp.pad(ids, (0, id_tiles * rows * tile - ids.shape[0])).reshape(id_tiles, rows, tile)

    qkv_tiles = 3 * width // tile
    rest_tiles = tiles - qkv_tiles
    qkv_at, rest_at = qkv_tiles // 2, rest_tiles // 2
    split = qkv_at + id_tiles
    by_slot = [values.transpose(1, 0, 2) for values in (weights, moment_one, moment_two)]
    rest = near[qkv_tiles:][None]
    near = jnp.concatenate([near[:qkv_at], ids, near[qkv_at:qkv_tiles]], axis=0)[None]
    moments = moment_columns(after(by_slot[1], near), by_slot[2], seqs)
    for i, step in enumerate(seq_bits[:-1]):
        near = double(near, *step, *([moments] if i == 0 else []))
        rest = double(after(rest, moments) if i == 0 else rest, *step, near)
        if i == 0:
            x = after(inputs, near)
    x = exchange(x, "seq", group)
    cot = exchange(after(cotangent, x), "seq", group).reshape(group, wins, span, width)
    x = x.reshape(group, wins, span, width)

    def table_of(masks):
        table = np.zeros(blocks, np.int32)
        for k, (s, t) in enumerate(masks):
            table[s * reps + t] = k
        return jnp.asarray(table)

    orders = [seq_bits[-1:] + far_bits, far_bits + seq_bits[-1:]]

    def pieces_of(bufs, ranges):
        pieces, plans = [], []
        for buf, order, (first, last) in zip(bufs, orders, ranges):
            masks = gather_masks(seq_bits[:-1] + order)
            pieces += [buf, swap(buf, *core_bit[0])]
            plans += [(first, last, masks), (first, last, beyond(masks))]
        return settle(pieces, plans)

    def settle(pieces, plans):
        if aligned:
            return pieces, plans
        at = jnp.arange(blocks)
        full = []
        for i in range(0, len(pieces), 2):
            count = plans[i][1] - plans[i][0]
            table = table_of(plans[i][2] + plans[i + 1][2])
            both = jnp.concatenate([pieces[i][:, :count], pieces[i + 1][:, :count]], axis=0)
            both = jnp.take(both, table[((at // reps) ^ me_s) * reps + ((at % reps) ^ me_r)], axis=0)
            full.append(both.transpose(1, 0, 2, 3).reshape(count, blocks * rows, tile))
        return [jnp.concatenate(full, axis=0)], None

    bufs = [near[:, :split], near[:, split:]]
    bufs = [double(buf, *order[0]) for buf, order in zip(bufs, orders)]
    ids = bufs[0][:, qkv_at:]
    rest = after(rest, *bufs)
    for i in range(1, len(orders[0])):
        bufs = [double(buf, *order[i]) for buf, order in zip(bufs, orders)]
    w_qkv, qkv_plans = pieces_of(bufs, [(0, qkv_at), (qkv_at, qkv_tiles)])
    rest = [rest[:, :rest_at], rest[:, rest_at:]]
    rest = [double(buf, *order[0], *bufs) for buf, order in zip(rest, orders)]

    ids = ids.reshape(seqs, -1)[:, : 2 * seq_local * span].astype(jnp.int32)
    ids = (ids[:, : seq_local * span] * 64 + ids[:, seq_local * span :]).reshape(seqs, seq_local, span)
    spots = [0] * seqs
    for k, (s, _) in enumerate(gather_masks(seq_bits[:-1] + seq_bits[-1:])):
        spots[s] = k
    ids = jnp.take(ids, jnp.asarray(spots[:group])[jnp.arange(group) ^ place], axis=0)
    ids = lax.dynamic_slice_in_dim(ids, place * wins, wins, 1)
    ids = ids.transpose(1, 0, 2).reshape(wins, WIN)

    def scatter_plans(parts):
        count = parts[-1][1]
        if not aligned:
            return None, [(count, blocks * rows, tile)]
        own = [(first, last, gather_masks(order[:0:-1])) for first, last, order in parts]
        other = [(first, last, beyond(masks)) for first, last, masks in own]
        shape = (count * blocks // 2, rows, tile)
        return [own, other], [shape, shape]

    def scatter_tiles(grads, parts, *others):
        if not aligned:
            plain = grads[0].reshape(-1, blocks, rows, tile).transpose(1, 0, 2, 3)
            own, other = [], []
            for first, last, order in parts:
                masks = gather_masks(order[:0:-1])
                for target, some in ((own, masks), (other, beyond(masks))):
                    spots = np.array([s * reps + t for s, t in some])
                    at = ((spots // reps) ^ me_s) * reps + ((spots % reps) ^ me_r)
                    target.append(jnp.take(plain[:, first:last], at, axis=0).reshape(-1, rows, tile))
            grads = [jnp.concatenate(own, axis=0), jnp.concatenate(other, axis=0)]
        return add(grads[0], swap(grads[1], *core_bit[0]), *others)

    def cut_parts(buf, parts):
        out, at = [], 0
        for first, last, _ in parts:
            size = (last - first) * blocks // 2
            out.append(buf[at : at + size])
            at += size
        return out

    def join(bufs, parts):
        entries = 2 ** len(seq_bits[:-1])
        return jnp.concatenate([buf.reshape(entries, -1, rows, tile) for buf in bufs], axis=1)

    zyxc = seq_bits + far_bits + core_bit
    zxyc = seq_bits[:-1] + far_bits + seq_bits[-1:] + core_bit
    ahead = attend_forward(me, x, positions, ids, w_qkv, qkv_plans, qkv_tiles, tile, reps)
    for i in range(1, len(orders[0])):
        got = [swap(buf, *order[i]) for buf, order in zip(rest, orders)]
        qkv, mixed, lse, *got = lax.optimization_barrier((*ahead, *got))
        rest = [jnp.concatenate([buf, part], axis=0) for buf, part in zip(rest, got)]
    w_rest, rest_plans = pieces_of(rest, [(0, rest_at), (rest_at, rest_tiles)])
    rest_parts = [(0, rest_at, zyxc[::-1]), (rest_at, rest_tiles, zxyc[::-1])]
    out_plans, shapes = scatter_plans(rest_parts)
    result, mid, gmixed, d_norm, *d_rest = middle(
        me, x, positions, mixed, cot, norm_params, moments, group == seqs, w_rest, rest_plans, out_plans, shapes, rest_tiles, tile, reps, rows
    )
    result = exchange(result, "seq", group)
    rest = cut_parts(scatter_tiles(d_rest, rest_parts), rest_parts)
    steps = [[order[1 + i] for _, _, order in rest_parts] for i in range(len(orders[0]))]
    cuts = [buf.shape[0] // 2 for buf in rest]
    got = [swap(buf[cut:], *step) for buf, cut, step in zip(rest, cuts, steps[0])]

    qkv_total = qkv_tiles + width // tile + 1
    qkv_parts = [(0, 6, zyxc[::-1]), (6, qkv_total, zxyc[::-1])]
    out_plans, shapes = scatter_plans(qkv_parts)
    g_input, *d_qkv = attend_backward(
        me, x, positions, ids, qkv, lse, gmixed, mid, d_norm, rest,
        w_qkv, qkv_plans, out_plans, shapes, qkv_tiles, tile, reps, rows,
    )
    count = len(d_qkv)
    g_input, *some = lax.optimization_barrier((g_input, *d_qkv, *got))
    d_qkv, got = some[:count], some[count:]
    g_input = after(g_input, result)
    if group == seqs:
        moments = result
    else:
        moments = lax.all_to_all(after(moments, result), "seq", 0, 0, tiled=True)
    result = result[:, :, : wins * width].reshape(group, span, wins, width)
    result = result.transpose(0, 2, 1, 3).reshape(seq_local, span, width)
    rest = [add(buf[:cut], part) for buf, cut, part in zip(rest, cuts, got)]

    qkv_buf = scatter_tiles(d_qkv, qkv_parts)
    mine = cut_parts(qkv_buf, qkv_parts)
    low_left, low_right = low_bases(after(left_bases, qkv_buf), right_bases)
    mine = [halve(buf, *step, low_left) for buf, step in zip(mine, steps[0])]
    for some in steps[1:]:
        rest = [halve(buf, *step, *mine) for buf, step in zip(rest, some)]
        mine = [halve(buf, *step, *rest) for buf, step in zip(mine, some)]
    rest, mine = join(rest, rest_parts), join(mine, qkv_parts)
    for step in seq_bits[-2::-1]:
        rest = halve(rest, *step, mine)
        mine = halve(mine, *step, rest)
    rest, mine = rest[0], mine[0]
    g_input = exchange(g_input.reshape(seq_local, span, width), "seq", group)

    small = mine[qkv_tiles:]
    grad_norms = small[-1, : 4 * width // tile].astype(F32)
    sums = jnp.concatenate([mine[:qkv_tiles], rest], axis=0)
    tile_of = jnp.sum(
        jnp.where(owners[None, :] == jnp.arange(tiles)[:, None], jnp.arange(tiles)[None, :], 0), axis=1
    )
    sums = jnp.take(sums, tile_of, axis=0).reshape(reps, slots, rows, tile)
    g_input = after(g_input, sums).astype(F32)
    small = small[: width // tile]
    near = []
    for k in range(reps):
        part = lax.dynamic_index_in_dim(sums, me_r ^ k, 0, keepdims=False)
        part = jnp.concatenate([part, small], axis=0)
        near.append(swap(part, "rep", k) if k else part)
    sums = jnp.take(jnp.stack(near), jnp.arange(reps) ^ me_r, axis=0)
    sums = sums.transpose(1, 0, 2, 3).reshape(-1, rows_dev, tile)
    small = sums[slots:]
    sums = sums[:slots]

    turned = right_turn(sums, low_right, seqs)
    small = after(small, turned)
    turned = lax.all_to_all(after(turned, g_input), "seq", 0, 0, tiled=True)
    back = left_turns(turned, moments, low_left)
    news = last_turn(lax.all_to_all(back, "seq", 0, 0, tiled=True), low_right, *by_slot)
    first_new, second_new, new_weights = [values.transpose(1, 0, 2) for values in news]

    own = small[None]
    for i, step in enumerate(seq_bits):
        own = double(own, *step, *([turned] if i == 0 else [back]))
    masks = gather_masks(seq_bits)
    table = np.zeros(seqs, np.int32)
    for k, (i, _) in enumerate(masks):
        table[i] = k
    grad_pos = jnp.take(own, jnp.asarray(table)[jnp.arange(seqs) ^ me_s], axis=0)
    grad_pos = grad_pos.transpose(0, 2, 1, 3).reshape(WIN, width).astype(F32)
    if aligned:
        grad_norms = grad_norms.reshape(width // tile, 4, tile).transpose(1, 0, 2).reshape(4, width)
    else:
        grad_norms = lax.psum(d_norm, ("seq", "rep"))
    norm_first, norm_second, norm_dir = adam_step(grad_norms, norm_one, norm_two)
    pos_first, pos_second, pos_dir = adam_step(grad_pos, pos_one, pos_two)
    return (
        result,
        g_input,
        first_new,
        second_new,
        new_weights,
        norm_first,
        norm_second,
        norm_params - LEARN_SMALL * norm_dir,
        pos_first,
        pos_second,
        positions - LEARN_SMALL * pos_dir,
    )


def solution(mesh):
    tokens = P("rep", "seq", None)
    slots = P("seq", "rep", None)
    bases = P("rep", None, None)
    return jax.shard_map(
        body,
        mesh=mesh,
        in_specs=(
            tokens,
            tokens,
            P("rep", "seq"),
            P(),
            slots,
            bases,
            bases,
            slots,
            slots,
            P(),
            P(),
            P(),
            P(),
            P(),
            P(),
        ),
        out_specs=(tokens, tokens, slots, slots, slots, P(), P(), P(), P(), P(), P()),
        check_vma=False,
    )
```
